128 devices in a mesh: row: 8 (over y_hi, x), col: 16 (over z, y_lo, core).
Axes of the slice: x: 4, y: 4 (y_hi: 2, y_lo: 2; y = y_hi * 2 + y_lo), z: 4, core: 2. Of those that a mesh axis runs over, the one named last changes fastest.
Arguments:
- psi_val: bfloat16 [16, 48, 2304], P(None, 'row'), may hold values from -6 to 6
- psi_cond: bfloat16 [256, 48, 2304], P('col', 'row'), may hold values from -6 to 6
- energy_val: float32 [16], replicated, may hold values from -12 to -1
- energy_cond: float32 [256], P('col'), may hold values from 0.5 to 12
- stick_map: int32 [1536], replicated, may hold values from 0 to 2303, as said below
- gvec_map: int32 [40960], P('row'), may hold values from 0 to 9215, as said below
- slab_index: int32 [1024], replicated, may hold values from 0 to 40959, as said below
Outputs:
- chi_slab: float32 [40960, 1024], P(('row', 'col'))
The draws below stay inside these ranges and needn't reach their ends.
Inputs may be any that keep to these rules, and one draw needn't show every extreme that they name: `stick_map`: distinct values. `gvec_map`: within each aligned block of 5120 entries the values are distinct. `slab_index`: distinct values.
All inputs are finite; a program needn't handle non-finite values.
Results may differ from the reference program's by a relative error of at most 0.022.
Values may be sent and summed in bfloat16 or wider, within the bound.
A program may use at most 128 MiB of HBM per device.

```python
import math
import jax
import jax.numpy as jnp
from jax import lax

NX = 48
NY = 48
NZ = 48
NC = 256
NV = 16
STK_DEV = 192
GV_DEV = 320
NS = 1024
NSTK = 1536
NG = 40960
N_ROW = 8


def distinct_with_ends(key, count, span):
    inner = jax.random.permutation(key, span - 2)[:count - 2] + 1
    first = jnp.zeros((1,), jnp.int32)
    last = jnp.full((1,), span - 1, jnp.int32)
    return jnp.concatenate([first, inner.astype(jnp.int32), last])


def draw_stick_map(key, part):
    key = jax.random.fold_in(key, 11)
    values = distinct_with_ends(key, NSTK, NY * NZ)
    order = jax.random.permutation(jax.random.fold_in(key, 1), NSTK)
    return values[order].astype(jnp.int32)


def draw_gvec_map(key, part):
    key = jax.random.fold_in(key, 23)
    g_row = GV_DEV * (NG // (GV_DEV * (NSTK // STK_DEV)))
    blocks = NG // g_row
    keys = jax.random.split(key, blocks)
    table = jax.vmap(lambda k: distinct_with_ends(k, g_row, NX * STK_DEV))(keys)
    return table.reshape(NG).astype(jnp.int32)


def draw_slab_index(key, part):
    key = jax.random.fold_in(key, 37)
    values = distinct_with_ends(key, NS, NG)
    order = jax.random.permutation(jax.random.fold_in(key, 1), NS)
    return values[order].astype(jnp.int32)


def level_of(key, dims, cuts, least, top_value):
    gain, own = 1.0, jax.random.fold_in(key, 6)
    for position, shards_of in cuts:
        draws = jnp.exp(jax.random.uniform(jax.random.fold_in(own, position), (shards_of,), jnp.float32, least / len(cuts), top_value / len(cuts)))
        gain = gain * jnp.repeat(draws, dims[position] // shards_of).reshape([-1 if axis == position else 1 for axis in range(len(dims))])
    return gain


def normal_values(rng, extent, scale, bound, pieces=(), kind=jnp.bfloat16):
    entries = jax.random.normal(rng, extent, jnp.float32) * scale
    if len(pieces) > 0:
        entries = level_of(rng, extent, pieces, -0.22, 0.18) * entries
    return jnp.clip(entries, min=-bound, max=bound).astype(kind)


def setup_inputs(seed: int = 0) -> dict:
    seeds = jax.random.split(jax.random.key(seed), 8)
    return {
        "psi_val": normal_values(seeds[0], (NV, NX, NY * NZ), 1.0, 6.0, ((1, 8),)),
        "psi_cond": normal_values(seeds[1], (NC, NX, NY * NZ), 1.0, 6.0, ((0, 16), (1, 8))),
        "energy_val": jnp.clip(jax.random.uniform(seeds[2], (NV,), jnp.float32, -12.0, -1.0), -12.0, -1.0),
        "energy_cond": jnp.clip(0.5 + 11.5 * jax.random.uniform(seeds[3], (NC,), jnp.float32) ** level_of(seeds[3], (NC,), ((0, 16),), -0.2, 0.2), 0.5, 12.0),
        "stick_map": draw_stick_map(jax.random.fold_in(seeds[7], 71), 0),
        "gvec_map": draw_gvec_map(jax.random.fold_in(seeds[7], 71), 0),
        "slab_index": draw_slab_index(jax.random.fold_in(seeds[7], 71), 0),
    }


def stick_tables(stick_map):
    flat = jnp.arange(NY * NZ, dtype=jnp.int32)
    plane_y = flat // NZ
    plane_z = flat % NZ
    freq_y = stick_map // NZ
    freq_z = stick_map % NZ
    turns = (plane_y[:, None] * freq_y[None, :] * NZ + plane_z[:, None] * freq_z[None, :] * NY) % (NY * NZ)
    angle = turns.astype(jnp.float32) * (2.0 * math.pi / (NY * NZ))
    factor = 1.0 / math.sqrt(NY * NZ)
    return ((jnp.cos(angle) * factor).astype(jnp.bfloat16), (-jnp.sin(angle) * factor).astype(jnp.bfloat16))

def plane_tables():
    freq = jnp.arange(NX, dtype=jnp.int32)
    turns = freq[:, None] * freq[None, :] % NX
    angle = turns.astype(jnp.float32) * (2.0 * math.pi / NX)
    factor = 1.0 / math.sqrt(NX)
    return ((jnp.cos(angle) * factor).astype(jnp.bfloat16), (jnp.sin(angle) * factor).astype(jnp.bfloat16))

def reference(psi_val, psi_cond, energy_val, energy_cond, stick_map, gvec_map, slab_index):
    high = lax.Precision.HIGHEST
    cos_yz, sin_yz = stick_tables(stick_map)
    table = jnp.concatenate([cos_yz, sin_yz], axis=1).astype(jnp.float32)
    cos_x, sin_x = plane_tables()
    cos_x = cos_x.astype(jnp.float32)
    sin_x = sin_x.astype(jnp.float32)
    g_row = NG // N_ROW
    gidx = jnp.arange(NG, dtype=jnp.int32)
    freq_x = gvec_map // STK_DEV
    stick = gidx // g_row * STK_DEV + gvec_map % STK_DEV
    flat = freq_x * NSTK + stick
    cond = psi_cond.astype(jnp.float32)

    def per_band(carry, inputs):
        psi_one, level = inputs
        weight = jnp.sqrt(2.0 / (energy_cond - level))
        density = (weight[:, None, None] * psi_one[None].astype(jnp.float32) * cond).astype(jnp.bfloat16)
        density = lax.optimization_barrier(density).astype(jnp.float32)
        planes = jnp.dot(density.reshape(NC * NX, NY * NZ), table, precision=high)
        planes = lax.optimization_barrier(planes.astype(jnp.bfloat16)).astype(jnp.float32)
        planes = planes.reshape(NC, NX, 2 * NSTK)
        y_real = planes[:, :, :NSTK]
        y_imag = planes[:, :, NSTK:]
        x_real = jnp.einsum('kx,cxs->cks', cos_x, y_real, precision=high) + jnp.einsum('kx,cxs->cks', sin_x, y_imag, precision=high)
        x_imag = jnp.einsum('kx,cxs->cks', cos_x, y_imag, precision=high) - jnp.einsum('kx,cxs->cks', sin_x, y_real, precision=high)
        m_real = x_real.reshape(NC, NX * NSTK)[:, flat]
        m_imag = x_imag.reshape(NC, NX * NSTK)[:, flat]
        moments = jnp.concatenate([m_real, m_imag], axis=0).astype(jnp.bfloat16)
        moments = lax.optimization_barrier(moments).astype(jnp.float32)
        columns = moments[:, slab_index]
        return (carry + jnp.dot(moments.T, columns, precision=high), None)
    start = jnp.zeros((NG, NS), jnp.float32)
    total, _ = lax.scan(per_band, start, (psi_val, energy_val))
    return total * (-1.0 / math.sqrt(NV * NC))
```

```python
import functools
import math

import jax
import jax.numpy as jnp
from jax import lax
from jax.experimental import pallas as pl
from jax.experimental.pallas import tpu as pltpu
from jax.sharding import PartitionSpec as P

NX = 48
NY = 48
NZ = 48
CELLS = NY * NZ
HALF = CELLS // 2
NC = 256
NV = 16
CL = 16
PAIRS = NV * CL
STK = 192
G_ROW = 5120
NS = 1024
JS = 128
XB = 4
LANES = 256
VMEM_LIMIT = 60 * 1024 * 1024


def half_phase(ky, kz):
    unit = math.pi / 48.0
    y = 2 * jnp.arange(NY // 2, dtype=jnp.int32) + 1
    z = 2 * jnp.arange(NZ, dtype=jnp.int32) + 1
    ay = ((y[:, None] * ky[None, :]) % 96).astype(jnp.float32) * unit
    az = ((z[:, None] * kz[None, :]) % 96).astype(jnp.float32) * unit
    cy, sy = jnp.cos(ay)[:, None, :], jnp.sin(ay)[:, None, :]
    cz, sz = jnp.cos(az)[None, :, :], jnp.sin(az)[None, :, :]
    cos = (cy * cz - sy * sz).reshape(HALF, -1)
    sin = -(sy * cz + cy * sz).reshape(HALF, -1)
    return cos.astype(jnp.bfloat16), sin.astype(jnp.bfloat16)


def planes_kernel(psi_ref, tc_ref, ts_ref, rot_ref, ph_ref, w_ref, y_ref, s_ref, pvf, ev, od, sacc):
    step = pl.program_id(0)

    @pl.when(step == 0)
    def _():
        sacc[...] = jnp.zeros_like(sacc)

    for xi in range(XB):
        pvf[xi] = psi_ref[xi, :NV, :].astype(jnp.float32)

    for xi in range(XB):

        def one(v, carry, xi=xi):
            row = pvf[xi, pl.ds(v, 1), :]
            d = jnp.broadcast_to(row, (CL, CELLS)).astype(jnp.bfloat16) * psi_ref[xi, NV:, :]
            lo, hi = d[:, :HALF], d[:, HALF:]
            at = pl.ds(pl.multiple_of(xi * PAIRS + v * CL, CL), CL)
            ev[at, :] = lo + hi
            od[at, :] = lo - hi
            return carry

        lax.fori_loop(0, NV, one, 0, unroll=2)

    cosr = rot_ref[0:1, :]
    sinr = rot_ref[1:2, :]
    for xi in range(XB):
        rows = pl.ds(xi * PAIRS, PAIRS)
        a = jnp.dot(ev[rows, :], tc_ref[...], preferred_element_type=jnp.float32)
        b = jnp.dot(od[rows, :], ts_ref[...], preferred_element_type=jnp.float32)
        am, bm = a[:, :LANES], b[:, :LANES]
        y_ref[xi, 0] = (cosr * am - sinr * bm).astype(jnp.bfloat16)
        y_ref[xi, 1] = (cosr * bm + sinr * am).astype(jnp.bfloat16)
        asl, bsl = a[:, LANES:], b[:, LANES:]
        cp = ph_ref[xi, 0:1, :]
        sp = ph_ref[xi, 1:2, :]
        sacc[0] += cp * asl - sp * bsl
        sacc[1] += cp * bsl + sp * asl

    @pl.when(step == pl.num_programs(0) - 1)
    def _():
        s_ref[0] = (sacc[0] * w_ref[...]).astype(jnp.bfloat16)
        s_ref[1] = (sacc[1] * w_ref[...]).astype(jnp.bfloat16)


def planes(psi, tc, ts, rot, ph, wide):
    full = lambda *shape: pl.BlockSpec(shape, lambda i: (0,) * len(shape))
    return pl.pallas_call(
        planes_kernel,
        grid=(NX // XB,),
        in_specs=[
            pl.BlockSpec((XB, NV + CL, CELLS), lambda i: (i, 0, 0)),
            full(HALF, LANES + JS),
            full(HALF, LANES + JS),
            full(2, LANES),
            pl.BlockSpec((XB, 2, JS), lambda i: (i, 0, 0)),
            full(PAIRS, JS),
        ],
        out_specs=[
            pl.BlockSpec((XB, 2, PAIRS, LANES), lambda i: (i, 0, 0, 0)),
            full(2, PAIRS, JS),
        ],
        out_shape=[
            jax.ShapeDtypeStruct((NX, 2, PAIRS, LANES), jnp.bfloat16),
            jax.ShapeDtypeStruct((2, PAIRS, JS), jnp.bfloat16),
        ],
        scratch_shapes=[
            pltpu.VMEM((XB, NV, CELLS), jnp.float32),
            pltpu.VMEM((XB * PAIRS, HALF), jnp.bfloat16),
            pltpu.VMEM((XB * PAIRS, HALF), jnp.bfloat16),
            pltpu.VMEM((2, PAIRS, JS), jnp.float32),
        ],
        compiler_params=pltpu.CompilerParams(vmem_limit_bytes=VMEM_LIMIT),
        name="planes",
    )(psi, tc, ts, rot, ph, wide)


PB = 16


def lines_kernel(w_ref, y_ref, t_ref, m_ref, yr, yi, mo):
    base = pl.program_id(0) * PB
    for h in range(LANES // 128):
        lanes = slice(h * 128, h * 128 + 128)
        yr[h] = y_ref[:, 0, :, lanes].astype(jnp.float32).reshape(NX * PB, 128)
        yi[h] = y_ref[:, 1, :, lanes].astype(jnp.float32).reshape(NX * PB, 128)
    for p in range(PB):
        at = pl.ds(p, NX, stride=PB)
        real = jnp.concatenate([yr[0, at, :], yr[1, at, :]], axis=1)
        imag = jnp.concatenate([yi[0, at, :], yi[1, at, :]], axis=1)
        rhs = jnp.concatenate([real, imag], axis=0).astype(jnp.bfloat16)
        out = jnp.dot(t_ref[...], rhs, preferred_element_type=jnp.float32) * w_ref[base + p]
        for h in range(LANES // 128):
            mo[h, pl.ds(p, 2 * NX, stride=PB), :] = out[:, h * 128 : h * 128 + 128]
    for h in range(LANES // 128):
        lanes = slice(h * 128, h * 128 + 128)
        m_ref[:, :, lanes] = mo[h].reshape(2 * NX, PB, 128).astype(jnp.bfloat16)


def lines(weights, y, table):
    return pl.pallas_call(
        lines_kernel,
        grid_spec=pltpu.PrefetchScalarGridSpec(
            num_scalar_prefetch=1,
            grid=(PAIRS // PB,),
            in_specs=[
                pl.BlockSpec((NX, 2, PB, LANES), lambda i, w: (0, 0, i, 0)),
                pl.BlockSpec((2 * NX, 2 * NX), lambda i, w: (0, 0)),
            ],
            out_specs=pl.BlockSpec((2 * NX, PB, LANES), lambda i, w: (0, i, 0)),
            scratch_shapes=[
                pltpu.VMEM((2, NX * PB, 128), jnp.float32),
                pltpu.VMEM((2, NX * PB, 128), jnp.float32),
                pltpu.VMEM((2, 2 * NX * PB, 128), jnp.float32),
            ],
        ),
        out_shape=jax.ShapeDtypeStruct((2 * NX, PAIRS, LANES), jnp.bfloat16),
        compiler_params=pltpu.CompilerParams(vmem_limit_bytes=VMEM_LIMIT),
        name="lines",
    )(weights, y, table)


GB = 320
QS = 2 * PAIRS // 128


def chi_kernel(g_ref, m_ref, s_ref, o_ref, mt, sel):
    step = pl.program_id(0)

    @pl.when(step < NX)
    def _():
        for h in range(2):
            for q in range(2):
                a = m_ref[h, 0, q * 128 : q * 128 + 128, :].astype(jnp.float32)
                t = a.T
                at = pl.ds(step * (STK * QS) + h * 2 + q, STK, stride=QS)
                mt[at, :] = t[:STK, :]

    @pl.when(step >= NX)
    def _():
        base = (step - NX) * GB

        def pick(i, carry):
            for u in range(8):
                g = g_ref[base + i * 8 + u]
                sel[pl.ds(pl.multiple_of(i * 32 + u * QS, QS), QS), :] = mt[
                    pl.ds(pl.multiple_of(g * QS, QS), QS), :
                ]
            return carry

        lax.fori_loop(0, GB // 8, pick, 0)
        lhs = jnp.concatenate(
            [sel[pl.ds(q, GB, stride=QS), :].astype(jnp.bfloat16) for q in range(QS)], axis=1
        )
        scale = -1.0 / math.sqrt(NV * NC)
        for r in range(NS // JS):
            out = jnp.dot(lhs, s_ref[r], preferred_element_type=jnp.float32)
            o_ref[:, r * JS : r * JS + JS] = (out * scale).astype(jnp.bfloat16)


def chi(gvec, m, s):
    return pl.pallas_call(
        chi_kernel,
        grid_spec=pltpu.PrefetchScalarGridSpec(
            num_scalar_prefetch=1,
            grid=(NX + G_ROW // GB,),
            in_specs=[
                pl.BlockSpec((2, 1, PAIRS, LANES), lambda i, g: (0, jnp.minimum(i, NX - 1), 0, 0)),
                pl.BlockSpec((NS // JS, 2 * PAIRS, JS), lambda i, g: (0, 0, 0)),
            ],
            out_specs=pl.BlockSpec((GB, NS), lambda i, g: (jnp.maximum(i - NX, 0), 0)),
            scratch_shapes=[
                pltpu.VMEM((NX * STK * QS, 128), jnp.float32),
                pltpu.VMEM((GB * QS, 128), jnp.float32),
            ],
        ),
        out_shape=jax.ShapeDtypeStruct((G_ROW, NS), jnp.bfloat16),
        compiler_params=pltpu.CompilerParams(vmem_limit_bytes=VMEM_LIMIT),
        name="chi",
    )(gvec, m, s)


def body(psi_val, psi_cond, energy_val, energy_cond, stick_map, gvec_map, slab_index):
    row = lax.axis_index("row")
    both = jnp.concatenate([psi_val, psi_cond], axis=0).transpose(1, 0, 2)
    both = jnp.concatenate([both[:, :, :HALF], jnp.flip(both[:, :, HALF:], axis=2)], axis=2)
    psi = lax.all_gather(both, "row", axis=0, tiled=True)
    maps = lax.all_gather(gvec_map, "row", axis=0, tiled=True)

    mine = lax.dynamic_slice(stick_map, (row * STK,), (STK,))
    cols = lax.dynamic_slice(slab_index, (row * JS,), (JS,))
    place = jnp.take(maps, cols)
    col_kx = place // STK
    col_stick = jnp.take(stick_map, cols // G_ROW * STK + place % STK)
    pad = jnp.zeros((LANES - STK,), jnp.int32)
    flat = jnp.concatenate([mine, pad, col_stick])
    ky, kz = flat // NZ, flat % NZ
    tc, ts = half_phase(ky, kz)
    turn = ((ky + kz) % 96).astype(jnp.float32) * (math.pi / 48.0)
    rot = jnp.stack([jnp.cos(turn[:LANES]), jnp.sin(turn[:LANES])])
    xs = jnp.arange(NX, dtype=jnp.int32)
    theta = (
        ((ky + kz)[None, LANES:] - 2 * (xs[:, None] * col_kx[None, :]) + 96 * NX) % 96
    ).astype(jnp.float32) * (math.pi / 48.0)
    ph = jnp.stack([jnp.cos(theta), jnp.sin(theta)], axis=1)

    weight = jnp.sqrt(2.0 / (energy_cond[None, :] - energy_val[:, None])) * (
        1.0 / (math.sqrt(NY * NZ) * math.sqrt(NX))
    )
    weight = weight.reshape(PAIRS)
    wide = jnp.broadcast_to(weight[:, None], (PAIRS, JS))
    ax = (xs[:, None] * xs[None, :] % NX).astype(jnp.float32) * (2.0 * math.pi / NX)
    cx, sx = jnp.cos(ax), jnp.sin(ax)
    table = jnp.concatenate(
        [jnp.concatenate([cx, sx], axis=1), jnp.concatenate([-sx, cx], axis=1)], axis=0
    ).astype(jnp.bfloat16)

    y, s_part = planes(psi, tc, ts, rot, ph, wide)
    slab = lax.all_gather(s_part.reshape(2 * PAIRS, JS), "row", axis=0, tiled=False)
    m = lines(weight, y, table)
    part = chi(gvec_map, m.reshape(2, NX, PAIRS, LANES), slab)
    return lax.psum_scatter(part, "col", scatter_dimension=0, tiled=True).astype(jnp.float32)


def solution(mesh):
    in_specs = (P(None, "row", None), P("col", "row", None), P(), P("col"), P(), P("row"), P())
    out_specs = P(("row", "col"), None)
    return jax.shard_map(body, mesh=mesh, in_specs=in_specs, out_specs=out_specs, check_vma=False)
```

```python
import functools
import math

import jax
import jax.numpy as jnp
from jax import lax
from jax.experimental import pallas as pl
from jax.experimental.pallas import tpu as pltpu
from jax.sharding import PartitionSpec as P

NX = 48
NY = 48
NZ = 48
CELLS = NY * NZ
HALF = CELLS // 2
NC = 256
NV = 16
CL = 16
PAIRS = NV * CL
STK = 192
G_ROW = 5120
NS = 1024
JS = 128
XB = 4
LANES = 256
VMEM_LIMIT = 60 * 1024 * 1024


def half_phase(ky, kz):
    unit = math.pi / 48.0
    y = 2 * jnp.arange(NY // 2, dtype=jnp.int32) + 1
    z = 2 * jnp.arange(NZ, dtype=jnp.int32) + 1
    ay = ((y[:, None] * ky[None, :]) % 96).astype(jnp.float32) * unit
    az = ((z[:, None] * kz[None, :]) % 96).astype(jnp.float32) * unit
    cy, sy = jnp.cos(ay)[:, None, :], jnp.sin(ay)[:, None, :]
    cz, sz = jnp.cos(az)[None, :, :], jnp.sin(az)[None, :, :]
    cos = (cy * cz - sy * sz).reshape(HALF, -1)
    sin = -(sy * cz + cy * sz).reshape(HALF, -1)
    return cos.astype(jnp.bfloat16), sin.astype(jnp.bfloat16)


def planes_kernel(psi_ref, tc_ref, ts_ref, rot_ref, ph_ref, w_ref, y_ref, s_ref, pvf, ev, od, sacc):
    step = pl.program_id(0)

    @pl.when(step == 0)
    def _():
        sacc[...] = jnp.zeros_like(sacc)

    for xi in range(XB):
        pvf[xi] = psi_ref[xi, :NV, :].astype(jnp.float32)

    for xi in range(XB):

        def one(v, carry, xi=xi):
            row = pvf[xi, pl.ds(v, 1), :]
            d = jnp.broadcast_to(row, (CL, CELLS)).astype(jnp.bfloat16) * psi_ref[xi, NV:, :]
            lo, hi = d[:, :HALF], d[:, HALF:]
            at = pl.ds(pl.multiple_of(xi * PAIRS + v * CL, CL), CL)
            ev[at, :] = lo + hi
            od[at, :] = lo - hi
            return carry

        lax.fori_loop(0, NV, one, 0, unroll=2)

    cosr = rot_ref[0:1, :]
    sinr = rot_ref[1:2, :]
    for xi in range(XB):
        rows = pl.ds(xi * PAIRS, PAIRS)
        a = jnp.dot(ev[rows, :], tc_ref[...], preferred_element_type=jnp.float32)
        b = jnp.dot(od[rows, :], ts_ref[...], preferred_element_type=jnp.float32)
        am, bm = a[:, :LANES], b[:, :LANES]
        y_ref[xi, 0] = (cosr * am - sinr * bm).astype(jnp.bfloat16)
        y_ref[xi, 1] = (cosr * bm + sinr * am).astype(jnp.bfloat16)
        asl, bsl = a[:, LANES:], b[:, LANES:]
        cp = ph_ref[xi, 0:1, :]
        sp = ph_ref[xi, 1:2, :]
        sacc[0] += cp * asl - sp * bsl
        sacc[1] += cp * bsl + sp * asl

    @pl.when(step == pl.num_programs(0) - 1)
    def _():
        s_ref[0] = (sacc[0] * w_ref[...]).astype(jnp.bfloat16)
        s_ref[1] = (sacc[1] * w_ref[...]).astype(jnp.bfloat16)


def planes(psi, tc, ts, rot, ph, wide):
    full = lambda *shape: pl.BlockSpec(shape, lambda i: (0,) * len(shape))
    return pl.pallas_call(
        planes_kernel,
        grid=(NX // XB,),
        in_specs=[
            pl.BlockSpec((XB, NV + CL, CELLS), lambda i: (i, 0, 0)),
            full(HALF, LANES + JS),
            full(HALF, LANES + JS),
            full(2, LANES),
            pl.BlockSpec((XB, 2, JS), lambda i: (i, 0, 0)),
            full(PAIRS, JS),
        ],
        out_specs=[
            pl.BlockSpec((XB, 2, PAIRS, LANES), lambda i: (i, 0, 0, 0)),
            full(2, PAIRS, JS),
        ],
        out_shape=[
            jax.ShapeDtypeStruct((NX, 2, PAIRS, LANES), jnp.bfloat16),
            jax.ShapeDtypeStruct((2, PAIRS, JS), jnp.bfloat16),
        ],
        scratch_shapes=[
            pltpu.VMEM((XB, NV, CELLS), jnp.float32),
            pltpu.VMEM((XB * PAIRS, HALF), jnp.bfloat16),
            pltpu.VMEM((XB * PAIRS, HALF), jnp.bfloat16),
            pltpu.VMEM((2, PAIRS, JS), jnp.float32),
        ],
        compiler_params=pltpu.CompilerParams(vmem_limit_bytes=VMEM_LIMIT),
        name="planes",
    )(psi, tc, ts, rot, ph, wide)


PB = 16


def lines_kernel(w_ref, y_ref, t_ref, m_ref, yr, yi, mo):
    base = pl.program_id(0) * PB
    for h in range(LANES // 128):
        lanes = slice(h * 128, h * 128 + 128)
        yr[h] = y_ref[:, 0, :, lanes].astype(jnp.float32).reshape(NX * PB, 128)
        yi[h] = y_ref[:, 1, :, lanes].astype(jnp.float32).reshape(NX * PB, 128)
    for p in range(PB):
        at = pl.ds(p, NX, stride=PB)
        real = jnp.concatenate([yr[0, at, :], yr[1, at, :]], axis=1)
        imag = jnp.concatenate([yi[0, at, :], yi[1, at, :]], axis=1)
        rhs = jnp.concatenate([real, imag], axis=0).astype(jnp.bfloat16)
        out = jnp.dot(t_ref[...], rhs, preferred_element_type=jnp.float32) * w_ref[base + p]
        for h in range(LANES // 128):
            mo[h, pl.ds(p, 2 * NX, stride=PB), :] = out[:, h * 128 : h * 128 + 128]
    for h in range(LANES // 128):
        lanes = slice(h * 128, h * 128 + 128)
        m_ref[:, :, lanes] = mo[h].reshape(2 * NX, PB, 128).astype(jnp.bfloat16)


def lines(weights, y, table):
    return pl.pallas_call(
        lines_kernel,
        grid_spec=pltpu.PrefetchScalarGridSpec(
            num_scalar_prefetch=1,
            grid=(PAIRS // PB,),
            in_specs=[
                pl.BlockSpec((NX, 2, PB, LANES), lambda i, w: (0, 0, i, 0)),
                pl.BlockSpec((2 * NX, 2 * NX), lambda i, w: (0, 0)),
            ],
            out_specs=pl.BlockSpec((2 * NX, PB, LANES), lambda i, w: (0, i, 0)),
            scratch_shapes=[
                pltpu.VMEM((2, NX * PB, 128), jnp.float32),
                pltpu.VMEM((2, NX * PB, 128), jnp.float32),
                pltpu.VMEM((2, 2 * NX * PB, 128), jnp.float32),
            ],
        ),
        out_shape=jax.ShapeDtypeStruct((2 * NX, PAIRS, LANES), jnp.bfloat16),
        compiler_params=pltpu.CompilerParams(vmem_limit_bytes=VMEM_LIMIT),
        name="lines",
    )(weights, y, table)


GB = 320
QS = 2 * PAIRS // 128


def chi_kernel(g_ref, m_ref, s_ref, o_ref, mt, sel):
    step = pl.program_id(0)

    @pl.when(step < NX)
    def _():
        for h in range(2):
            for q in range(2):
                a = m_ref[h, 0, q * 128 : q * 128 + 128, :].astype(jnp.float32)
                t = a.T
                at = pl.ds(step * (STK * QS) + h * 2 + q, STK, stride=QS)
                mt[at, :] = t[:STK, :]

    @pl.when(step >= NX)
    def _():
        base = (step - NX) * GB

        def pick(i, carry):
            for u in range(8):
                g = g_ref[base + i * 8 + u]
                sel[pl.ds(pl.multiple_of(i * 32 + u * QS, QS), QS), :] = mt[
                    pl.ds(pl.multiple_of(g * QS, QS), QS), :
                ]
            return carry

        lax.fori_loop(0, GB // 8, pick, 0)
        lhs = jnp.concatenate(
            [sel[pl.ds(q, GB, stride=QS), :].astype(jnp.bfloat16) for q in range(QS)], axis=1
        )
        scale = -1.0 / math.sqrt(NV * NC)
        for r in range(NS // JS):
            out = jnp.dot(lhs, s_ref[r], preferred_element_type=jnp.float32)
            o_ref[:, r * JS : r * JS + JS] = (out * scale).astype(jnp.bfloat16)


def chi(gvec, m, s):
    return pl.pallas_call(
        chi_kernel,
        grid_spec=pltpu.PrefetchScalarGridSpec(
            num_scalar_prefetch=1,
            grid=(NX + G_ROW // GB,),
            in_specs=[
                pl.BlockSpec((2, 1, PAIRS, LANES), lambda i, g: (0, jnp.minimum(i, NX - 1), 0, 0)),
                pl.BlockSpec((NS // JS, 2 * PAIRS, JS), lambda i, g: (0, 0, 0)),
            ],
            out_specs=pl.BlockSpec((GB, NS), lambda i, g: (jnp.maximum(i - NX, 0), 0)),
            scratch_shapes=[
                pltpu.VMEM((NX * STK * QS, 128), jnp.float32),
                pltpu.VMEM((GB * QS, 128), jnp.float32),
            ],
        ),
        out_shape=jax.ShapeDtypeStruct((G_ROW, NS), jnp.bfloat16),
        compiler_params=pltpu.CompilerParams(vmem_limit_bytes=VMEM_LIMIT),
        name="chi",
    )(gvec, m, s)


MESH = pl.DeviceIdType.MESH
G_DEV = 320
HR = G_DEV // 2


def add_rows(dst, dst_at, a, b, rows, step=32):
    def one(i, carry):
        at = pl.ds(pl.multiple_of(dst_at + i * step, 16), step)
        src = pl.ds(pl.multiple_of(b[1] + i * step, 16), step)
        dst[at, :] = (a[at, :].astype(jnp.float32) + b[0][src, :].astype(jnp.float32)).astype(dst.dtype)
        return carry

    lax.fori_loop(0, rows // step, one, 0)


def share_kernel(part, out, acc, r1, zr2, yr1, zr1, yr2, lsem, s1, d1, sz2, dz2, sy1, dy1, sz1, dz1, sy2, dy2):
    row, col = lax.axis_index("row"), lax.axis_index("col")
    z, yl, core = col // 4, (col // 2) % 2, col % 2
    core_peer = {"row": row, "col": z * 4 + yl * 2 + (1 - core)}
    y_peer = {"row": row, "col": z * 4 + (1 - yl) * 2 + core}
    z_peer = lambda k: {"row": row, "col": ((z + k) % 4) * 4 + yl * 2 + core}
    barrier = pltpu.get_barrier_semaphore()
    for peer in (core_peer, y_peer, z_peer(1), z_peer(2), z_peer(3)):
        pl.semaphore_signal(barrier, inc=1, device_id=peer, device_id_type=MESH)
    pl.semaphore_wait(barrier, 5)

    order = [(k, s) for k in (2, 1, 3, 0) for s in (0, 1)]
    first, local = {}, {}
    for k, s in order:
        slot = k * 2 + s
        q = ((z + k) % 4) * 4 + (yl if s else 1 - yl) * 2
        first[slot] = pltpu.make_async_remote_copy(
            part.at[q + 1 - core], r1.at[slot], s1.at[slot], d1.at[slot], device_id=core_peer, device_id_type=MESH
        )
        first[slot].start()
        local[slot] = pltpu.make_async_copy(part.at[q + core], acc.at[slot], lsem.at[slot])
        local[slot].start()
    sends = []

    def send(src, dst, ss, ds, peer):
        copy = pltpu.make_async_remote_copy(src, dst, ss, ds, device_id=peer, device_id_type=MESH)
        copy.start()
        sends.append(copy)
        return copy

    lo, hi = pl.ds(0, HR), pl.ds(HR, HR)
    along_y, along_z = {}, {}
    for k, s in order:
        slot = k * 2 + s
        local[slot].wait()
        first[slot].wait_recv()
        add_rows(acc.at[slot], 0, acc.at[slot], (r1.at[slot], 0), G_DEV)
        if k:
            i = (k - 1) * 2 + s
            along_z[k, s] = send(acc.at[slot, hi], zr2.at[i], sz2.at[i], dz2.at[i], z_peer(k))
        if s == 0:
            along_y[k] = send(acc.at[slot, lo], yr1.at[k], sy1.at[k], dy1.at[k], y_peer)
    last_z = {}
    for k in (2, 1, 3, 0):
        along_y[k].wait_recv()
        if k:
            slot = k * 2 + 1
            add_rows(acc.at[slot], 0, acc.at[slot], (yr1.at[k], 0), HR)
            last_z[k] = send(acc.at[slot, lo], zr1.at[k - 1], sz1.at[k - 1], dz1.at[k - 1], z_peer(k))
    for k in (1, 3, 2):
        along_z[k, 0].wait_recv()

    def total(i, base, terms):
        at = pl.ds(pl.multiple_of(i * 16, 16), 16)
        value = base[pl.ds(pl.multiple_of(i * 16, 16), 16), :].astype(jnp.float32)
        for ref in terms:
            value = value + ref[at, :].astype(jnp.float32)
        return at, value

    def turn(i, carry):
        at, value = total(i, acc.at[0, hi], [zr2.at[0], zr2.at[2], zr2.at[4]])
        yr2[0, at, :] = value.astype(jnp.bfloat16)
        return carry

    lax.fori_loop(0, HR // 16, turn, 0)
    last_y = send(yr2.at[0], yr2.at[1], sy2.at[0], dy2.at[0], y_peer)
    for k in (1, 3, 2):
        last_z[k].wait_recv()

    def low(i, carry):
        at, value = total(i, acc.at[1, lo], [yr1.at[0], zr1.at[0], zr1.at[1], zr1.at[2]])
        out[at, :] = value
        return carry

    lax.fori_loop(0, HR // 16, low, 0)
    for k in (1, 3, 2):
        along_z[k, 1].wait_recv()
    last_y.wait_recv()

    def high(i, carry):
        at, value = total(i, acc.at[1, hi], [zr2.at[1], zr2.at[3], zr2.at[5], yr2.at[1]])
        out[pl.ds(pl.multiple_of(HR + i * 16, 16), 16), :] = value
        return carry

    lax.fori_loop(0, HR // 16, high, 0)
    for copy in list(first.values()) + sends:
        copy.wait_send()


def share(part):
    dma = pltpu.SemaphoreType.DMA
    half = lambda n: pltpu.VMEM((n, HR, NS), jnp.bfloat16)
    return pl.pallas_call(
        share_kernel,
        in_specs=[pl.BlockSpec(memory_space=pl.ANY)],
        out_specs=pl.BlockSpec(memory_space=pltpu.VMEM),
        out_shape=jax.ShapeDtypeStruct((G_DEV, NS), jnp.float32),
        scratch_shapes=[
            pltpu.VMEM((8, G_DEV, NS), jnp.bfloat16),
            pltpu.VMEM((8, G_DEV, NS), jnp.bfloat16),
            half(6), half(4), half(3), half(2),
            dma((8,)), dma((8,)), dma((8,)), dma((6,)), dma((6,)), dma((4,)), dma((4,)),
            dma((3,)), dma((3,)), dma((1,)), dma((1,)),
        ],
        compiler_params=pltpu.CompilerParams(
            collective_id=3, has_side_effects=True, vmem_limit_bytes=VMEM_LIMIT
        ),
        name="share",
    )(part)


def places_kernel(mine, out, got, send_sem, recv_sem):
    row, col = lax.axis_index("row"), lax.axis_index("col")
    barrier = pltpu.get_barrier_semaphore()
    for k in range(1, 8):
        pl.semaphore_signal(barrier, inc=1, device_id={"row": (row + k) % 8, "col": col}, device_id_type=MESH)
    pl.semaphore_wait(barrier, 7)
    copies = []
    for k in range(1, 8):
        to = (row + k) % 8
        copies.append(
            pltpu.make_async_remote_copy(
                mine.at[to], got.at[k - 1], send_sem.at[k - 1], recv_sem.at[k - 1],
                device_id={"row": to, "col": col}, device_id_type=MESH,
            )
        )
        copies[-1].start()
    total = mine[row]
    for k in range(1, 8):
        copies[k - 1].wait_recv()
        total = total + got[k - 1]
    out[...] = total
    for copy in copies:
        copy.wait_send()


def places(mine):
    return pl.pallas_call(
        places_kernel,
        in_specs=[pl.BlockSpec(memory_space=pltpu.VMEM)],
        out_specs=pl.BlockSpec(memory_space=pltpu.VMEM),
        out_shape=jax.ShapeDtypeStruct((8, JS), jnp.int32),
        scratch_shapes=[
            pltpu.VMEM((7, 8, JS), jnp.int32),
            pltpu.SemaphoreType.DMA((7,)),
            pltpu.SemaphoreType.DMA((7,)),
        ],
        compiler_params=pltpu.CompilerParams(collective_id=1, has_side_effects=True),
        name="places",
    )(mine)


def body(psi_val, psi_cond, energy_val, energy_cond, stick_map, gvec_map, slab_index):
    row = lax.axis_index("row")
    both = jnp.concatenate([psi_val, psi_cond], axis=0).transpose(1, 0, 2)
    both = jnp.concatenate([both[:, :, :HALF], jnp.flip(both[:, :, HALF:], axis=2)], axis=2)
    psi = lax.all_gather(both, "row", axis=0, tiled=True)

    mine = lax.dynamic_slice(stick_map, (row * STK,), (STK,))
    cols = lax.dynamic_slice(slab_index, (row * JS,), (JS,))
    held = jnp.where(slab_index // G_ROW == row, jnp.take(gvec_map, slab_index % G_ROW), 0)
    held = jnp.broadcast_to(held.reshape(NS // JS, 1, JS), (NS // JS, 8, JS))
    place = places(held)[0]
    col_kx = place // STK
    col_stick = jnp.take(stick_map, cols // G_ROW * STK + place % STK)
    pad = jnp.zeros((LANES - STK,), jnp.int32)
    flat = jnp.concatenate([mine, pad, col_stick])
    ky, kz = flat // NZ, flat % NZ
    tc, ts = half_phase(ky, kz)
    turn = ((ky + kz) % 96).astype(jnp.float32) * (math.pi / 48.0)
    rot = jnp.stack([jnp.cos(turn[:LANES]), jnp.sin(turn[:LANES])])
    xs = jnp.arange(NX, dtype=jnp.int32)
    theta = (
        ((ky + kz)[None, LANES:] - 2 * (xs[:, None] * col_kx[None, :]) + 96 * NX) % 96
    ).astype(jnp.float32) * (math.pi / 48.0)
    ph = jnp.stack([jnp.cos(theta), jnp.sin(theta)], axis=1)

    weight = jnp.sqrt(2.0 / (energy_cond[None, :] - energy_val[:, None])) * (
        1.0 / (math.sqrt(NY * NZ) * math.sqrt(NX))
    )
    weight = weight.reshape(PAIRS)
    wide = jnp.broadcast_to(weight[:, None], (PAIRS, JS))
    ax = (xs[:, None] * xs[None, :] % NX).astype(jnp.float32) * (2.0 * math.pi / NX)
    cx, sx = jnp.cos(ax), jnp.sin(ax)
    table = jnp.concatenate(
        [jnp.concatenate([cx, sx], axis=1), jnp.concatenate([-sx, cx], axis=1)], axis=0
    ).astype(jnp.bfloat16)

    y, s_part = planes(psi, tc, ts, rot, ph, wide)
    slab = lax.all_gather(s_part.reshape(2 * PAIRS, JS), "row", axis=0, tiled=False)
    m = lines(weight, y, table)
    part = chi(gvec_map, m.reshape(2, NX, PAIRS, LANES), slab)
    return share(part.reshape(G_ROW // G_DEV, G_DEV, NS))


def solution(mesh):
    in_specs = (P(None, "row", None), P("col", "row", None), P(), P("col"), P(), P("row"), P())
    out_specs = P(("row", "col"), None)
    return jax.shard_map(body, mesh=mesh, in_specs=in_specs, out_specs=out_specs, check_vma=False)
```

```python
import functools
import math

import jax
import jax.numpy as jnp
from jax import lax
from jax.experimental import pallas as pl
from jax.experimental.pallas import tpu as pltpu
from jax.sharding import PartitionSpec as P

NX = 48
NY = 48
NZ = 48
CELLS = NY * NZ
HALF = CELLS // 2
NC = 256
NV = 16
CL = 16
PAIRS = NV * CL
STK = 192
G_ROW = 5120
NS = 1024
JS = 128
XB = 4
LANES = 256
VMEM_LIMIT = 60 * 1024 * 1024
MESH = pl.DeviceIdType.MESH


def half_phase(ky, kz):
    unit = math.pi / 48.0
    y = 2 * jnp.arange(NY // 2, dtype=jnp.int32) + 1
    z = 2 * jnp.arange(NZ, dtype=jnp.int32) + 1
    ay = ((y[:, None] * ky[None, :]) % 96).astype(jnp.float32) * unit
    az = ((z[:, None] * kz[None, :]) % 96).astype(jnp.float32) * unit
    cy, sy = jnp.cos(ay)[:, None, :], jnp.sin(ay)[:, None, :]
    cz, sz = jnp.cos(az)[None, :, :], jnp.sin(az)[None, :, :]
    cos = (cy * cz - sy * sz).reshape(HALF, -1)
    sin = -(sy * cz + cy * sz).reshape(HALF, -1)
    return cos.astype(jnp.bfloat16), sin.astype(jnp.bfloat16)


BLOCKS = 8
PX = NX // BLOCKS
PT = 3
PB = 16


def density(vf, cbuf, b, plane, at, even, odd):
    def one(v, carry):
        out = pl.ds(pl.multiple_of(at * PAIRS + v * CL, CL), CL)
        cond = cbuf.at[b, plane]
        spread = lambda h: jnp.broadcast_to(vf[h, plane, pl.ds(v, 1), :], (CL, HALF)).astype(jnp.bfloat16)
        lo = spread(0) * cond[:, :HALF]
        hi = spread(1) * cond[:, HALF:]
        even[out, :] = lo + hi
        odd[out, :] = lo - hi
        return carry

    lax.fori_loop(0, NV, one, 0, unroll=4)


def transform(b, first, even, odd, tc, ts, rot, ph, y, sacc):
    a = jnp.dot(even[...], tc[...], preferred_element_type=jnp.float32)
    c = jnp.dot(odd[...], ts[...], preferred_element_type=jnp.float32)
    cosr, sinr = rot[0:1, :], rot[1:2, :]
    real, imag = sacc[0], sacc[1]
    for i in range(PT):
        x = b * PX + first + i
        rows = slice(i * PAIRS, i * PAIRS + PAIRS)
        am, cm = a[rows, :LANES], c[rows, :LANES]
        y[x, 0] = (cosr * am - sinr * cm).astype(jnp.bfloat16)
        y[x, 1] = (cosr * cm + sinr * am).astype(jnp.bfloat16)
        av, cv = a[rows, LANES:], c[rows, LANES:]
        cp, sp = ph[x, 0:1, :], ph[x, 1:2, :]
        real = real + (cp * av - sp * cv)
        imag = imag + (cp * cv + sp * av)
    sacc[0] = real
    sacc[1] = imag


def front_kernel(
    weights, cond, val, tc, ts, rot, ph, wide, table, m_out, slab_out,
    cbuf, vbuf, vf, even, odd, y, sacc, sl, yr, yi, mo, mb,
    lsem, cs, cr, vs, vr, gs, gr, ss, sr, ms,
):
    row, col = lax.axis_index("row"), lax.axis_index("col")
    yh, x = row // 4, row % 4
    z, yl, core = col // 4, (col // 2) % 2, col % 2
    zo = z + 1 - 2 * (z % 2)
    xp = {"row": yh * 4 + (x + 1) % 4, "col": col}
    xm = {"row": yh * 4 + (x + 3) % 4, "col": col}
    yc = {"row": (1 - yh) * 4 + x, "col": col}
    yv = {"row": (1 - yh) * 4 + x, "col": z * 4 + (1 - yl) * 2 + core}
    group = [
        {"row": row, "col": zo * 4 + yl * 2 + core},
        {"row": row, "col": z * 4 + yl * 2 + 1 - core},
        {"row": row, "col": zo * 4 + yl * 2 + 1 - core},
    ]
    across = [{"row": (row + k) % 8, "col": col} for k in range(1, 8)]
    part = core * 2 + z % 2

    own = [
        pltpu.make_async_copy(cond, cbuf.at[0], lsem.at[0]),
        pltpu.make_async_copy(val, vbuf.at[0], lsem.at[1]),
    ]
    for copy in own:
        copy.start()
    barrier = pltpu.get_barrier_semaphore()
    for peer in across + group + [yv]:
        pl.semaphore_signal(barrier, inc=1, device_id=peer, device_id_type=MESH)
    pl.semaphore_wait(barrier, 11)

    hops = [(0, 3, None), (0, 2, xp), (0, 1, xm), (3, 5, xp), (3, 4, xm), (2, 6, xp), (4, 7, xm)]

    def relay(n):
        src, dst, peer = hops[n]
        c = pltpu.make_async_remote_copy(
            cond if src == 0 else cbuf.at[src], cbuf.at[dst], cs.at[n], cr.at[dst],
            device_id=peer or yc, device_id_type=MESH,
        )
        v = pltpu.make_async_remote_copy(
            val.at[part] if src == 0 else vbuf.at[src, part], vbuf.at[dst, part], vs.at[n], vr.at[dst],
            device_id=peer or yv, device_id_type=MESH,
        )
        return c, v

    def go(n):
        for copy in relay(n):
            copy.start()

    def incoming(dst):
        return relay([hop[1] for hop in hops].index(dst))

    def spread(b, j):
        return pltpu.make_async_remote_copy(
            vbuf.at[b, part], vbuf.at[b, part], gs.at[b * 3 + j], gr.at[b * 3 + j],
            device_id=group[j], device_id_type=MESH,
        )

    def land(b, *forward):
        c, v = incoming(b)
        v.wait_recv()
        for j in range(3):
            spread(b, j).start()
        c.wait_recv()
        for n in forward:
            go(n)

    def ready(b):
        for j in range(3):
            spread(b, j).wait_recv()

    for n in range(3):
        go(n)
    sacc[...] = jnp.zeros_like(sacc)
    for copy in own:
        copy.wait()

    def block(b, carry):
        @pl.when(b == 1)
        def _():
            land(2, 5)
            land(1)
            land(3, 3, 4)
            ready(1)

        @pl.when(b == 2)
        def _():
            ready(2)

        @pl.when(b == 3)
        def _():
            land(4, 6)
            ready(3)

        @pl.when(b == 4)
        def _():
            land(5)
            land(6)
            ready(4)

        @pl.when(b == 5)
        def _():
            ready(5)

        @pl.when(b == 6)
        def _():
            land(7)
            ready(6)

        @pl.when(b == 7)
        def _():
            ready(7)

        def widen(j, carry):
            for q in range(4):
                vf[q % 2, (q // 2) * 3 + j] = vbuf[b, q, j].astype(jnp.float32)
            return carry

        lax.fori_loop(0, 3, widen, 0)

        def some(i, carry):
            for u in range(PT):
                density(vf, cbuf, b, i * PT + u, u, even, odd)
            transform(b, i * PT, even, odd, tc, ts, rot, ph, y, sacc)
            return carry

        lax.fori_loop(0, PX // PT, some, 0)
        return carry

    lax.fori_loop(0, BLOCKS, block, 0)

    for h in range(2):
        sl[h * PAIRS : h * PAIRS + PAIRS, :] = (sacc[h] * wide[...]).astype(jnp.bfloat16)
    keep = pltpu.make_async_copy(sl, slab_out.at[row], lsem.at[2])
    keep.start()
    pushes = []
    for k in range(7):
        pushes.append(
            pltpu.make_async_remote_copy(
                sl, slab_out.at[row], ss.at[k], sr.at[k], device_id=across[k], device_id_type=MESH
            )
        )
        pushes[-1].start()

    def chunk(i, carry):
        slot = i % 2
        ps = pl.ds(pl.multiple_of(i * PB, PB), PB)
        out = pltpu.make_async_copy(mb.at[slot], m_out.at[:, ps, :], ms.at[slot])
        for h in range(LANES // 128):
            lanes = slice(h * 128, h * 128 + 128)
            yr[h] = y[:, 0, ps, lanes].astype(jnp.float32).reshape(NX * PB, 128)
            yi[h] = y[:, 1, ps, lanes].astype(jnp.float32).reshape(NX * PB, 128)
        for p in range(PB):
            at = pl.ds(p, NX, stride=PB)
            real = jnp.concatenate([yr[0, at, :], yr[1, at, :]], axis=1)
            imag = jnp.concatenate([yi[0, at, :], yi[1, at, :]], axis=1)
            rhs = jnp.concatenate([real, imag], axis=0).astype(jnp.bfloat16)
            res = jnp.dot(table[...], rhs, preferred_element_type=jnp.float32) * weights[i * PB + p]
            for h in range(LANES // 128):
                mo[h, pl.ds(p, 2 * NX, stride=PB), :] = res[:, h * 128 : h * 128 + 128]

        @pl.when(i >= 2)
        def _():
            out.wait()

        for h in range(LANES // 128):
            lanes = slice(h * 128, h * 128 + 128)
            mb[slot, :, :, lanes] = mo[h].reshape(2 * NX, PB, 128).astype(jnp.bfloat16)
        out.start()
        return carry

    lax.fori_loop(0, PAIRS // PB, chunk, 0)
    for slot in range(2):
        pltpu.make_async_copy(mb.at[slot], m_out.at[:, pl.ds(slot * PB, PB), :], ms.at[slot]).wait()
    keep.wait()
    for push in pushes:
        push.wait_recv()
        push.wait_send()
    for n in range(7):
        for copy in relay(n):
            copy.wait_send()
    for b in range(1, BLOCKS):
        for j in range(3):
            spread(b, j).wait_send()


def front(weights, cond, val, tc, ts, rot, ph, wide, table):
    dma = pltpu.SemaphoreType.DMA
    vmem = pl.BlockSpec(memory_space=pltpu.VMEM)
    hbm = pl.BlockSpec(memory_space=pl.ANY)
    bf = lambda *shape: pltpu.VMEM(shape, jnp.bfloat16)
    fl = lambda *shape: pltpu.VMEM(shape, jnp.float32)
    return pl.pallas_call(
        front_kernel,
        in_specs=[pl.BlockSpec(memory_space=pltpu.SMEM)] + [vmem] * 8,
        out_specs=[hbm, hbm],
        out_shape=[
            jax.ShapeDtypeStruct((2 * NX, PAIRS, LANES), jnp.bfloat16),
            jax.ShapeDtypeStruct((BLOCKS, 2 * PAIRS, JS), jnp.bfloat16),
        ],
        scratch_shapes=[
            bf(BLOCKS, PX, CL, CELLS),
            bf(BLOCKS, 4, PX // 2, NV, HALF),
            fl(2, PX, NV, HALF),
            bf(PT * PAIRS, HALF),
            bf(PT * PAIRS, HALF),
            bf(NX, 2, PAIRS, LANES),
            fl(2, PAIRS, JS),
            bf(2 * PAIRS, JS),
            fl(2, NX * PB, 128),
            fl(2, NX * PB, 128),
            fl(2, 2 * NX * PB, 128),
            bf(2, 2 * NX, PB, LANES),
            dma((3,)), dma((7,)), dma((8,)), dma((7,)), dma((8,)),
            dma((24,)), dma((24,)), dma((7,)), dma((7,)), dma((2,)),
        ],
        compiler_params=pltpu.CompilerParams(
            collective_id=2, has_side_effects=True, vmem_limit_bytes=VMEM_LIMIT
        ),
        name="front",
    )(weights, cond, val, tc, ts, rot, ph, wide, table)


GB = 320
QS = 2 * PAIRS // 128


def chi_kernel(g_ref, m_ref, s_ref, o_ref, mt, sel):
    step = pl.program_id(0)

    @pl.when(step < NX)
    def _():
        for h in range(2):
            for q in range(2):
                a = m_ref[h, 0, q * 128 : q * 128 + 128, :].astype(jnp.float32)
                t = a.T
                at = pl.ds(step * (STK * QS) + h * 2 + q, STK, stride=QS)
                mt[at, :] = t[:STK, :]

    @pl.when(step >= NX)
    def _():
        base = (step - NX) * GB

        def pick(i, carry):
            for u in range(8):
                g = g_ref[base + i * 8 + u]
                sel[pl.ds(pl.multiple_of(i * 32 + u * QS, QS), QS), :] = mt[
                    pl.ds(pl.multiple_of(g * QS, QS), QS), :
                ]
            return carry

        lax.fori_loop(0, GB // 8, pick, 0)
        lhs = jnp.concatenate(
            [sel[pl.ds(q, GB, stride=QS), :].astype(jnp.bfloat16) for q in range(QS)], axis=1
        )
        scale = -1.0 / math.sqrt(NV * NC)
        for r in range(NS // JS):
            out = jnp.dot(lhs, s_ref[r], preferred_element_type=jnp.float32)
            o_ref[:, r * JS : r * JS + JS] = (out * scale).astype(jnp.bfloat16)


def chi(gvec, m, s):
    return pl.pallas_call(
        chi_kernel,
        grid_spec=pltpu.PrefetchScalarGridSpec(
            num_scalar_prefetch=1,
            grid=(NX + G_ROW // GB,),
            in_specs=[
                pl.BlockSpec((2, 1, PAIRS, LANES), lambda i, g: (0, jnp.minimum(i, NX - 1), 0, 0)),
                pl.BlockSpec((NS // JS, 2 * PAIRS, JS), lambda i, g: (0, 0, 0)),
            ],
            out_specs=pl.BlockSpec((GB, NS), lambda i, g: (jnp.maximum(i - NX, 0), 0)),
            scratch_shapes=[
                pltpu.VMEM((NX * STK * QS, 128), jnp.float32),
                pltpu.VMEM((GB * QS, 128), jnp.float32),
            ],
        ),
        out_shape=jax.ShapeDtypeStruct((G_ROW, NS), jnp.bfloat16),
        compiler_params=pltpu.CompilerParams(vmem_limit_bytes=VMEM_LIMIT),
        name="chi",
    )(gvec, m, s)


G_DEV = 320
HR = G_DEV // 2


def add_rows(dst, dst_at, a, b, rows, step=32):
    def one(i, carry):
        at = pl.ds(pl.multiple_of(dst_at + i * step, 16), step)
        src = pl.ds(pl.multiple_of(b[1] + i * step, 16), step)
        dst[at, :] = (a[at, :].astype(jnp.float32) + b[0][src, :].astype(jnp.float32)).astype(dst.dtype)
        return carry

    lax.fori_loop(0, rows // step, one, 0)


def share_kernel(part, out, acc, r1, zr2, yr1, zr1, yr2, lsem, s1, d1, sz2, dz2, sy1, dy1, sz1, dz1, sy2, dy2):
    row, col = lax.axis_index("row"), lax.axis_index("col")
    z, yl, core = col // 4, (col // 2) % 2, col % 2
    core_peer = {"row": row, "col": z * 4 + yl * 2 + (1 - core)}
    y_peer = {"row": row, "col": z * 4 + (1 - yl) * 2 + core}
    z_peer = lambda k: {"row": row, "col": ((z + k) % 4) * 4 + yl * 2 + core}
    barrier = pltpu.get_barrier_semaphore()
    for peer in (core_peer, y_peer, z_peer(1), z_peer(2), z_peer(3)):
        pl.semaphore_signal(barrier, inc=1, device_id=peer, device_id_type=MESH)
    pl.semaphore_wait(barrier, 5)

    order = [(k, s) for k in (2, 1, 3, 0) for s in (0, 1)]
    first, local = {}, {}
    for k, s in order:
        slot = k * 2 + s
        q = ((z + k) % 4) * 4 + (yl if s else 1 - yl) * 2
        first[slot] = pltpu.make_async_remote_copy(
            part.at[q + 1 - core], r1.at[slot], s1.at[slot], d1.at[slot], device_id=core_peer, device_id_type=MESH
        )
        first[slot].start()
        local[slot] = pltpu.make_async_copy(part.at[q + core], acc.at[slot], lsem.at[slot])
        local[slot].start()
    sends = []

    def send(src, dst, ss, ds, peer):
        copy = pltpu.make_async_remote_copy(src, dst, ss, ds, device_id=peer, device_id_type=MESH)
        copy.start()
        sends.append(copy)
        return copy

    lo, hi = pl.ds(0, HR), pl.ds(HR, HR)
    along_y, along_z = {}, {}
    for k, s in order:
        slot = k * 2 + s
        local[slot].wait()
        first[slot].wait_recv()
        add_rows(acc.at[slot], 0, acc.at[slot], (r1.at[slot], 0), G_DEV)
        if k:
            i = (k - 1) * 2 + s
            along_z[k, s] = send(acc.at[slot, hi], zr2.at[i], sz2.at[i], dz2.at[i], z_peer(k))
        if s == 0:
            along_y[k] = send(acc.at[slot, lo], yr1.at[k], sy1.at[k], dy1.at[k], y_peer)
    last_z = {}
    for k in (2, 1, 3, 0):
        along_y[k].wait_recv()
        if k:
            slot = k * 2 + 1
            add_rows(acc.at[slot], 0, acc.at[slot], (yr1.at[k], 0), HR)
            last_z[k] = send(acc.at[slot, lo], zr1.at[k - 1], sz1.at[k - 1], dz1.at[k - 1], z_peer(k))
    for k in (1, 3, 2):
        along_z[k, 0].wait_recv()

    def total(i, base, terms):
        at = pl.ds(pl.multiple_of(i * 16, 16), 16)
        value = base[pl.ds(pl.multiple_of(i * 16, 16), 16), :].astype(jnp.float32)
        for ref in terms:
            value = value + ref[at, :].astype(jnp.float32)
        return at, value

    def turn(i, carry):
        at, value = total(i, acc.at[0, hi], [zr2.at[0], zr2.at[2], zr2.at[4]])
        yr2[0, at, :] = value.astype(jnp.bfloat16)
        return carry

    lax.fori_loop(0, HR // 16, turn, 0)
    last_y = send(yr2.at[0], yr2.at[1], sy2.at[0], dy2.at[0], y_peer)
    for k in (1, 3, 2):
        last_z[k].wait_recv()

    def low(i, carry):
        at, value = total(i, acc.at[1, lo], [yr1.at[0], zr1.at[0], zr1.at[1], zr1.at[2]])
        out[at, :] = value
        return carry

    lax.fori_loop(0, HR // 16, low, 0)
    for k in (1, 3, 2):
        along_z[k, 1].wait_recv()
    last_y.wait_recv()

    def high(i, carry):
        at, value = total(i, acc.at[1, hi], [zr2.at[1], zr2.at[3], zr2.at[5], yr2.at[1]])
        out[pl.ds(pl.multiple_of(HR + i * 16, 16), 16), :] = value
        return carry

    lax.fori_loop(0, HR // 16, high, 0)
    for copy in list(first.values()) + sends:
        copy.wait_send()


def share(part):
    dma = pltpu.SemaphoreType.DMA
    half = lambda n: pltpu.VMEM((n, HR, NS), jnp.bfloat16)
    return pl.pallas_call(
        share_kernel,
        in_specs=[pl.BlockSpec(memory_space=pl.ANY)],
        out_specs=pl.BlockSpec(memory_space=pltpu.VMEM),
        out_shape=jax.ShapeDtypeStruct((G_DEV, NS), jnp.float32),
        scratch_shapes=[
            pltpu.VMEM((8, G_DEV, NS), jnp.bfloat16),
            pltpu.VMEM((8, G_DEV, NS), jnp.bfloat16),
            half(6), half(4), half(3), half(2),
            dma((8,)), dma((8,)), dma((8,)), dma((6,)), dma((6,)), dma((4,)), dma((4,)),
            dma((3,)), dma((3,)), dma((1,)), dma((1,)),
        ],
        compiler_params=pltpu.CompilerParams(
            collective_id=3, has_side_effects=True, vmem_limit_bytes=VMEM_LIMIT
        ),
        name="share",
    )(part)


def places_kernel(mine, out, got, send_sem, recv_sem):
    row, col = lax.axis_index("row"), lax.axis_index("col")
    barrier = pltpu.get_barrier_semaphore()
    for k in range(1, 8):
        pl.semaphore_signal(barrier, inc=1, device_id={"row": (row + k) % 8, "col": col}, device_id_type=MESH)
    pl.semaphore_wait(barrier, 7)
    copies = []
    for k in range(1, 8):
        to = (row + k) % 8
        copies.append(
            pltpu.make_async_remote_copy(
                mine.at[to], got.at[k - 1], send_sem.at[k - 1], recv_sem.at[k - 1],
                device_id={"row": to, "col": col}, device_id_type=MESH,
            )
        )
        copies[-1].start()
    total = mine[row]
    for k in range(1, 8):
        copies[k - 1].wait_recv()
        total = total + got[k - 1]
    out[...] = total
    for copy in copies:
        copy.wait_send()


def places(mine):
    return pl.pallas_call(
        places_kernel,
        in_specs=[pl.BlockSpec(memory_space=pltpu.VMEM)],
        out_specs=pl.BlockSpec(memory_space=pltpu.VMEM),
        out_shape=jax.ShapeDtypeStruct((8, JS), jnp.int32),
        scratch_shapes=[
            pltpu.VMEM((7, 8, JS), jnp.int32),
            pltpu.SemaphoreType.DMA((7,)),
            pltpu.SemaphoreType.DMA((7,)),
        ],
        compiler_params=pltpu.CompilerParams(collective_id=1, has_side_effects=True),
        name="places",
    )(mine)


def body(psi_val, psi_cond, energy_val, energy_cond, stick_map, gvec_map, slab_index):
    row = lax.axis_index("row")
    fold = lambda psi: (psi[:, :, :HALF], jnp.flip(psi[:, :, HALF:], axis=2))
    cond = jnp.concatenate(fold(psi_cond.transpose(1, 0, 2)), axis=2)
    val = jnp.stack([half.reshape(2, PX // 2, NV, HALF) for half in fold(psi_val.transpose(1, 0, 2))], axis=1)
    val = val.reshape(4, PX // 2, NV, HALF)

    mine = lax.dynamic_slice(stick_map, (row * STK,), (STK,))
    cols = lax.dynamic_slice(slab_index, (row * JS,), (JS,))
    held = jnp.where(slab_index // G_ROW == row, jnp.take(gvec_map, slab_index % G_ROW), 0)
    held = jnp.broadcast_to(held.reshape(NS // JS, 1, JS), (NS // JS, 8, JS))
    place = places(held)[0]
    col_kx = place // STK
    col_stick = jnp.take(stick_map, cols // G_ROW * STK + place % STK)
    pad = jnp.zeros((LANES - STK,), jnp.int32)
    flat = jnp.concatenate([mine, pad, col_stick])
    ky, kz = flat // NZ, flat % NZ
    tc, ts = half_phase(ky, kz)
    turn = ((ky + kz) % 96).astype(jnp.float32) * (math.pi / 48.0)
    rot = jnp.stack([jnp.cos(turn[:LANES]), jnp.sin(turn[:LANES])])
    dy = jnp.array([0, 0, 0, 1, 1, 1, 0, 1], jnp.int32)
    dx = jnp.array([0, 1, 3, 0, 1, 3, 2, 2], jnp.int32)
    source = (row // 4 + dy) % 2 * 4 + (row % 4 + dx) % 4
    xs = (source[:, None] * PX + jnp.arange(PX, dtype=jnp.int32)[None, :]).reshape(NX)
    theta = (
        ((ky + kz)[None, LANES:] - 2 * (xs[:, None] * col_kx[None, :]) + 96 * NX) % 96
    ).astype(jnp.float32) * (math.pi / 48.0)
    ph = jnp.stack([jnp.cos(theta), jnp.sin(theta)], axis=1)

    weight = jnp.sqrt(2.0 / (energy_cond[None, :] - energy_val[:, None])) * (
        1.0 / (math.sqrt(NY * NZ) * math.sqrt(NX))
    )
    weight = weight.reshape(PAIRS)
    wide = jnp.broadcast_to(weight[:, None], (PAIRS, JS))
    freq = jnp.arange(NX, dtype=jnp.int32)
    ax = (freq[:, None] * xs[None, :] % NX).astype(jnp.float32) * (2.0 * math.pi / NX)
    cx, sx = jnp.cos(ax), jnp.sin(ax)
    table = jnp.concatenate(
        [jnp.concatenate([cx, sx], axis=1), jnp.concatenate([-sx, cx], axis=1)], axis=0
    ).astype(jnp.bfloat16)

    m, slab = front(weight, cond, val, tc, ts, rot, ph, wide, table)
    part = chi(gvec_map, m.reshape(2, NX, PAIRS, LANES), slab)
    return share(part.reshape(G_ROW // G_DEV, G_DEV, NS))


def solution(mesh):
    in_specs = (P(None, "row", None), P("col", "row", None), P(), P("col"), P(), P("row"), P())
    out_specs = P(("row", "col"), None)
    return jax.shard_map(body, mesh=mesh, in_specs=in_specs, out_specs=out_specs, check_vma=False)
```

```python
import math

import jax
import jax.numpy as jnp
from jax import lax
from jax.experimental import pallas as pl
from jax.experimental.pallas import tpu as pltpu
from jax.sharding import PartitionSpec as P

NX = 48
NY = 48
NZ = 48
CELLS = NY * NZ
HALF = CELLS // 2
NC = 256
NV = 16
CL = 16
PAIRS = NV * CL
STK = 192
G_ROW = 5120
NS = 1024
JS = 128
XB = 4
LANES = 256
VMEM_LIMIT = 60 * 1024 * 1024
MESH = pl.DeviceIdType.MESH


def half_phase(ky, kz):
    unit = math.pi / 48.0
    y = 2 * jnp.arange(NY // 2, dtype=jnp.int32) + 1
    z = 2 * jnp.arange(NZ, dtype=jnp.int32) + 1
    ay = ((y[:, None] * ky[None, :]) % 96).astype(jnp.float32) * unit
    az = ((z[:, None] * kz[None, :]) % 96).astype(jnp.float32) * unit
    cy, sy = jnp.cos(ay)[:, None, :], jnp.sin(ay)[:, None, :]
    cz, sz = jnp.cos(az)[None, :, :], jnp.sin(az)[None, :, :]
    cos = (cy * cz - sy * sz).reshape(HALF, -1)
    sin = -(sy * cz + cy * sz).reshape(HALF, -1)
    return cos.astype(jnp.bfloat16), sin.astype(jnp.bfloat16)


BLOCKS = 8
PX = NX // BLOCKS
PT = 3
PB = 16


def density(vf, cbuf, b, plane, at, even, odd):
    def one(v, carry):
        out = pl.ds(pl.multiple_of(at * PAIRS + v * CL, CL), CL)
        cond = cbuf.at[b, plane]
        spread = lambda h: jnp.broadcast_to(vf[h, plane, pl.ds(v, 1), :], (CL, HALF)).astype(jnp.bfloat16)
        lo = spread(0) * cond[:, :HALF]
        hi = spread(1) * cond[:, HALF:]
        even[out, :] = lo + hi
        odd[out, :] = lo - hi
        return carry

    lax.fori_loop(0, NV, one, 0, unroll=4)


def transform(b, first, even, odd, tc, ts, rot, ph, y, sacc):
    a = jnp.dot(even[...], tc[...], preferred_element_type=jnp.float32)
    c = jnp.dot(odd[...], ts[...], preferred_element_type=jnp.float32)
    cosr, sinr = rot[0:1, :], rot[1:2, :]
    real, imag = sacc[0], sacc[1]
    for i in range(PT):
        x = b * PX + first + i
        rows = slice(i * PAIRS, i * PAIRS + PAIRS)
        am, cm = a[rows, :LANES], c[rows, :LANES]
        y[x, 0] = (cosr * am - sinr * cm).astype(jnp.bfloat16)
        y[x, 1] = (cosr * cm + sinr * am).astype(jnp.bfloat16)
        av, cv = a[rows, LANES:], c[rows, LANES:]
        cp, sp = ph[x, 0:1, :], ph[x, 1:2, :]
        real = real + (cp * av - sp * cv)
        imag = imag + (cp * cv + sp * av)
    sacc[0] = real
    sacc[1] = imag


def front_kernel(
    weights, cond, val, tc, ts, rot, ph, wide, table, m_out, slab_out,
    cbuf, vbuf, vf, even, odd, y, sacc, sl, yr, yi, mo, mb,
    lsem, cs, cr, vs, vr, gs, gr, ss, sr, ms,
):
    row, col = lax.axis_index("row"), lax.axis_index("col")
    yh, x = row // 4, row % 4
    z, yl, core = col // 4, (col // 2) % 2, col % 2
    zo = z + 1 - 2 * (z % 2)
    xp = {"row": yh * 4 + (x + 1) % 4, "col": col}
    xm = {"row": yh * 4 + (x + 3) % 4, "col": col}
    yc = {"row": (1 - yh) * 4 + x, "col": col}
    yv = {"row": (1 - yh) * 4 + x, "col": z * 4 + (1 - yl) * 2 + core}
    group = [
        {"row": row, "col": zo * 4 + yl * 2 + core},
        {"row": row, "col": z * 4 + yl * 2 + 1 - core},
        {"row": row, "col": zo * 4 + yl * 2 + 1 - core},
    ]
    across = [{"row": (row + k) % 8, "col": col} for k in range(1, 8)]
    part = core * 2 + z % 2

    own = [
        pltpu.make_async_copy(cond, cbuf.at[0], lsem.at[0]),
        pltpu.make_async_copy(val, vbuf.at[0], lsem.at[1]),
    ]
    for copy in own:
        copy.start()
    barrier = pltpu.get_barrier_semaphore()
    for peer in across + group + [yv]:
        pl.semaphore_signal(barrier, inc=1, device_id=peer, device_id_type=MESH)
    pl.semaphore_wait(barrier, 11)

    hops = [(0, 3, None), (0, 2, xp), (0, 1, xm), (3, 5, xp), (3, 4, xm), (2, 6, xp), (4, 7, xm)]

    def relay(n):
        src, dst, peer = hops[n]
        c = pltpu.make_async_remote_copy(
            cond if src == 0 else cbuf.at[src], cbuf.at[dst], cs.at[n], cr.at[dst],
            device_id=peer or yc, device_id_type=MESH,
        )
        v = pltpu.make_async_remote_copy(
            val.at[part] if src == 0 else vbuf.at[src, part], vbuf.at[dst, part], vs.at[n], vr.at[dst],
            device_id=peer or yv, device_id_type=MESH,
        )
        return c, v

    def go(n):
        for copy in relay(n):
            copy.start()

    def incoming(dst):
        return relay([hop[1] for hop in hops].index(dst))

    def spread(b, j):
        return pltpu.make_async_remote_copy(
            vbuf.at[b, part], vbuf.at[b, part], gs.at[b * 3 + j], gr.at[b * 3 + j],
            device_id=group[j], device_id_type=MESH,
        )

    def land(b, *forward):
        c, v = incoming(b)
        v.wait_recv()
        for j in range(3):
            spread(b, j).start()
        c.wait_recv()
        for n in forward:
            go(n)

    def ready(b):
        for j in range(3):
            spread(b, j).wait_recv()

    for n in range(3):
        go(n)
    sacc[...] = jnp.zeros_like(sacc)
    for copy in own:
        copy.wait()

    def block(b, carry):
        @pl.when(b == 1)
        def _():
            land(2, 5)
            land(1)
            land(3, 3, 4)
            ready(1)

        @pl.when(b == 2)
        def _():
            ready(2)

        @pl.when(b == 3)
        def _():
            land(4, 6)
            ready(3)

        @pl.when(b == 4)
        def _():
            land(5)
            land(6)
            ready(4)

        @pl.when(b == 5)
        def _():
            ready(5)

        @pl.when(b == 6)
        def _():
            land(7)
            ready(6)

        @pl.when(b == 7)
        def _():
            ready(7)

        def widen(j, carry):
            for q in range(4):
                vf[q % 2, (q // 2) * 3 + j] = vbuf[b, q, j].astype(jnp.float32)
            return carry

        lax.fori_loop(0, 3, widen, 0)

        def some(i, carry):
            for u in range(PT):
                density(vf, cbuf, b, i * PT + u, u, even, odd)
            transform(b, i * PT, even, odd, tc, ts, rot, ph, y, sacc)
            return carry

        lax.fori_loop(0, PX // PT, some, 0)
        return carry

    lax.fori_loop(0, BLOCKS, block, 0)

    for h in range(2):
        sl[h * PAIRS : h * PAIRS + PAIRS, :] = (sacc[h] * wide[...]).astype(jnp.bfloat16)
    keep = pltpu.make_async_copy(sl, slab_out.at[row], lsem.at[2])
    keep.start()
    pushes = []
    for k in range(7):
        pushes.append(
            pltpu.make_async_remote_copy(
                sl, slab_out.at[row], ss.at[k], sr.at[k], device_id=across[k], device_id_type=MESH
            )
        )
        pushes[-1].start()

    def chunk(i, carry):
        slot = i % 2
        ps = pl.ds(pl.multiple_of(i * PB, PB), PB)
        out = pltpu.make_async_copy(mb.at[slot], m_out.at[:, ps, :], ms.at[slot])
        for h in range(LANES // 128):
            lanes = slice(h * 128, h * 128 + 128)
            yr[h] = y[:, 0, ps, lanes].astype(jnp.float32).reshape(NX * PB, 128)
            yi[h] = y[:, 1, ps, lanes].astype(jnp.float32).reshape(NX * PB, 128)
        for p in range(PB):
            at = pl.ds(p, NX, stride=PB)
            real = jnp.concatenate([yr[0, at, :], yr[1, at, :]], axis=1)
            imag = jnp.concatenate([yi[0, at, :], yi[1, at, :]], axis=1)
            rhs = jnp.concatenate([real, imag], axis=0).astype(jnp.bfloat16)
            res = jnp.dot(table[...], rhs, preferred_element_type=jnp.float32) * weights[i * PB + p]
            for h in range(LANES // 128):
                mo[h, pl.ds(p, 2 * NX, stride=PB), :] = res[:, h * 128 : h * 128 + 128]

        @pl.when(i >= 2)
        def _():
            out.wait()

        for h in range(LANES // 128):
            lanes = slice(h * 128, h * 128 + 128)
            mb[slot, :, :, lanes] = mo[h].reshape(2 * NX, PB, 128).astype(jnp.bfloat16)
        out.start()
        return carry

    lax.fori_loop(0, PAIRS // PB, chunk, 0)
    for slot in range(2):
        pltpu.make_async_copy(mb.at[slot], m_out.at[:, pl.ds(slot * PB, PB), :], ms.at[slot]).wait()
    keep.wait()
    for push in pushes:
        push.wait_recv()
        push.wait_send()
    for n in range(7):
        for copy in relay(n):
            copy.wait_send()
    for b in range(1, BLOCKS):
        for j in range(3):
            spread(b, j).wait_send()


def front(weights, cond, val, tc, ts, rot, ph, wide, table):
    dma = pltpu.SemaphoreType.DMA
    vmem = pl.BlockSpec(memory_space=pltpu.VMEM)
    hbm = pl.BlockSpec(memory_space=pl.ANY)
    bf = lambda *shape: pltpu.VMEM(shape, jnp.bfloat16)
    fl = lambda *shape: pltpu.VMEM(shape, jnp.float32)
    return pl.pallas_call(
        front_kernel,
        in_specs=[pl.BlockSpec(memory_space=pltpu.SMEM)] + [vmem] * 8,
        out_specs=[hbm, hbm],
        out_shape=[
            jax.ShapeDtypeStruct((2 * NX, PAIRS, LANES), jnp.bfloat16),
            jax.ShapeDtypeStruct((BLOCKS, 2 * PAIRS, JS), jnp.bfloat16),
        ],
        scratch_shapes=[
            bf(BLOCKS, PX, CL, CELLS),
            bf(BLOCKS, 4, PX // 2, NV, HALF),
            fl(2, PX, NV, HALF),
            bf(PT * PAIRS, HALF),
            bf(PT * PAIRS, HALF),
            bf(NX, 2, PAIRS, LANES),
            fl(2, PAIRS, JS),
            bf(2 * PAIRS, JS),
            fl(2, NX * PB, 128),
            fl(2, NX * PB, 128),
            fl(2, 2 * NX * PB, 128),
            bf(2, 2 * NX, PB, LANES),
            dma((3,)), dma((7,)), dma((8,)), dma((7,)), dma((8,)),
            dma((24,)), dma((24,)), dma((7,)), dma((7,)), dma((2,)),
        ],
        compiler_params=pltpu.CompilerParams(
            collective_id=2, has_side_effects=True, vmem_limit_bytes=VMEM_LIMIT
        ),
        name="front",
    )(weights, cond, val, tc, ts, rot, ph, wide, table)


GB = 320
QS = 2 * PAIRS // 128
G_DEV = 320
HR = G_DEV // 2
DEPTH = 4
UNROLL = 16


def pick_kernel(g_ref, m, out, mt, mi, sel, lhs, ms, os):
    def fetch(step):
        slot = step % DEPTH
        return pltpu.make_async_copy(m.at[:, step], mi.at[slot], ms.at[slot])

    for step in range(DEPTH):
        fetch(step).start()

    def turn(step, carry):
        fetch(step).wait()
        for h in range(2):
            for q in range(2):
                t = mi[step % DEPTH, h, q * 128 : q * 128 + 128, :].T.astype(jnp.float32)
                mt[pl.ds(step * (STK * QS) + h * 2 + q, STK, stride=QS), :] = t[:STK, :]

        @pl.when(step < NX - DEPTH)
        def _():
            fetch(step + DEPTH).start()

        return carry

    lax.fori_loop(0, NX, turn, 0)
    store = lambda n: pltpu.make_async_copy(lhs.at[n % 2], out.at[n], os.at[n % 2])

    def block(n, carry):
        def rows(i, carry):
            for u in range(UNROLL):
                g = g_ref[n * GB + i * UNROLL + u]
                to = pl.ds(pl.multiple_of((i * UNROLL + u) * QS, QS), QS)
                sel[to, :] = mt[pl.ds(pl.multiple_of(g * QS, QS), QS), :]
            return carry

        lax.fori_loop(0, GB // UNROLL, rows, 0)

        @pl.when(n >= 2)
        def _():
            store(n - 2).wait()

        for k in range(QS):
            lhs[n % 2, :, k * 128 : k * 128 + 128] = sel[pl.ds(k, GB, stride=QS), :].astype(jnp.bfloat16)
        store(n).start()
        return carry

    lax.fori_loop(0, G_ROW // GB, block, 0)
    for n in range(2):
        store(G_ROW // GB - 2 + n).wait()


def pick(gvec, m):
    dma = pltpu.SemaphoreType.DMA
    return pl.pallas_call(
        pick_kernel,
        in_specs=[pl.BlockSpec(memory_space=pltpu.SMEM), pl.BlockSpec(memory_space=pl.ANY)],
        out_specs=pl.BlockSpec(memory_space=pl.ANY),
        out_shape=jax.ShapeDtypeStruct((G_ROW // GB, GB, 2 * PAIRS), jnp.bfloat16),
        scratch_shapes=[
            pltpu.VMEM((NX * STK * QS, 128), jnp.float32),
            pltpu.VMEM((DEPTH, 2, PAIRS, LANES), jnp.bfloat16),
            pltpu.VMEM((GB * QS, 128), jnp.float32),
            pltpu.VMEM((2, GB, 2 * PAIRS), jnp.bfloat16),
            dma((DEPTH,)), dma((2,)),
        ],
        compiler_params=pltpu.CompilerParams(vmem_limit_bytes=VMEM_LIMIT),
        name="pick",
    )(gvec, m)


def add_rows(dst, a, b, rows, step=32):
    def one(i, carry):
        at = pl.ds(pl.multiple_of(i * step, step), step)
        dst[at, :] = (a[at, :].astype(jnp.float32) + b[at, :].astype(jnp.float32)).astype(dst.dtype)
        return carry

    lax.fori_loop(0, rows // step, one, 0)


def back_kernel(
    rows, slab, out, sw, lhs, tx, acc, r1, zr2, yr1, zr1, yr2,
    ms, s1, d1, sz2, dz2, sy1, dy1, sz1, dz1, sy2, dy2,
):
    row, col = lax.axis_index("row"), lax.axis_index("col")
    z, yl, core = col // 4, (col // 2) % 2, col % 2
    core_peer = {"row": row, "col": z * 4 + yl * 2 + (1 - core)}
    y_peer = {"row": row, "col": z * 4 + (1 - yl) * 2 + core}
    z_peer = lambda k: {"row": row, "col": ((z + k) % 4) * 4 + yl * 2 + core}
    barrier = pltpu.get_barrier_semaphore()
    for peer in (core_peer, y_peer, z_peer(1), z_peer(2), z_peer(3)):
        pl.semaphore_signal(barrier, inc=1, device_id=peer, device_id_type=MESH)

    for r in range(NS // JS):
        sw[:, r * JS : r * JS + JS] = slab[r]

    pl.semaphore_wait(barrier, 5)

    scale = -1.0 / math.sqrt(NV * NC)
    load = lambda q, own: pltpu.make_async_copy(rows.at[q], lhs.at[own], ms.at[own])

    def product(own, dst):
        value = jnp.dot(lhs[own], sw[...], preferred_element_type=jnp.float32)
        dst[...] = (value * scale).astype(jnp.bfloat16)

    def remote(src, dst, ss, ds, peer):
        return pltpu.make_async_remote_copy(src, dst, ss, ds, device_id=peer, device_id_type=MESH)

    lo, hi = pl.ds(0, HR), pl.ds(HR, HR)
    first = lambda n: remote(tx.at[n], r1.at[n], s1.at[n], d1.at[n], core_peer)
    along_z = lambda k, s: remote(
        acc.at[(k + 3) % 4 * 2 + s, hi], zr2.at[(k - 1) * 2 + s], sz2.at[(k - 1) * 2 + s], dz2.at[(k - 1) * 2 + s], z_peer(k)
    )
    along_y = lambda k: remote(acc.at[(k + 3) % 4 * 2, lo], yr1.at[k], sy1.at[k], dy1.at[k], y_peer)
    last_z = lambda k: remote(acc.at[(k + 3) % 4 * 2 + 1, lo], zr1.at[k - 1], sz1.at[k - 1], dz1.at[k - 1], z_peer(k))

    def settle(n):
        k, s = (n // 2 + 1) % 4, n % 2
        first(n).wait_recv()
        add_rows(acc.at[n], acc.at[n], r1.at[n], G_DEV)

        @pl.when(n < 6)
        def _():
            along_z(k, s).start()

        @pl.when(s == 0)
        def _():
            along_y(k).start()

    def place(n):
        k, s = (n // 2 + 1) % 4, n % 2
        return ((z + k) % 4) * 4 + (yl * s + (1 - yl) * (1 - s)) * 2

    def slot(n, carry):
        load(place(n) + 1 - core, 0).wait()
        product(0, tx.at[n])
        first(n).start()

        @pl.when(n < 7)
        def _():
            load(place(n + 1) + 1 - core, 0).start()

        load(place(n) + core, 1).wait()
        product(1, acc.at[n])

        @pl.when(n < 7)
        def _():
            load(place(n + 1) + core, 1).start()

        @pl.when(n > 0)
        def _():
            settle(n - 1)

        return carry

    load(place(0) + 1 - core, 0).start()
    load(place(0) + core, 1).start()
    lax.fori_loop(0, 8, slot, 0)
    settle(7)
    for k in (1, 2, 3, 0):
        along_y(k).wait_recv()
        if k:
            at = acc.at[(k + 3) % 4 * 2 + 1]
            add_rows(at, at, yr1.at[k], HR)
            last_z(k).start()
    for k in (1, 2, 3):
        along_z(k, 0).wait_recv()

    def total(i, base, terms):
        at = pl.ds(pl.multiple_of(i * 16, 16), 16)
        value = base[at, :].astype(jnp.float32)
        for ref in terms:
            value = value + ref[at, :].astype(jnp.float32)
        return at, value

    def across(i, carry):
        at, value = total(i, acc.at[6, hi], [zr2.at[0], zr2.at[2], zr2.at[4]])
        yr2[0, at, :] = value.astype(jnp.bfloat16)
        return carry

    lax.fori_loop(0, HR // 16, across, 0)
    last_y = remote(yr2.at[0], yr2.at[1], sy2.at[0], dy2.at[0], y_peer)
    last_y.start()
    for k in (1, 2, 3):
        last_z(k).wait_recv()

    def low(i, carry):
        at, value = total(i, acc.at[7, lo], [yr1.at[0], zr1.at[0], zr1.at[1], zr1.at[2]])
        out[at, :] = value
        return carry

    lax.fori_loop(0, HR // 16, low, 0)
    for k in (1, 2, 3):
        along_z(k, 1).wait_recv()
    last_y.wait_recv()

    def high(i, carry):
        at, value = total(i, acc.at[7, hi], [zr2.at[1], zr2.at[3], zr2.at[5], yr2.at[1]])
        out[pl.ds(pl.multiple_of(HR + i * 16, 16), 16), :] = value
        return carry

    lax.fori_loop(0, HR // 16, high, 0)
    for n in range(8):
        first(n).wait_send()
    for k in range(4):
        along_y(k).wait_send()
        if k:
            last_z(k).wait_send()
            along_z(k, 0).wait_send()
            along_z(k, 1).wait_send()
    last_y.wait_send()


def back(rows, slab):
    dma = pltpu.SemaphoreType.DMA
    vmem = pl.BlockSpec(memory_space=pltpu.VMEM)
    half = lambda n: pltpu.VMEM((n, HR, NS), jnp.bfloat16)
    return pl.pallas_call(
        back_kernel,
        in_specs=[pl.BlockSpec(memory_space=pl.ANY), vmem],
        out_specs=vmem,
        out_shape=jax.ShapeDtypeStruct((G_DEV, NS), jnp.float32),
        scratch_shapes=[
            pltpu.VMEM((2 * PAIRS, NS), jnp.bfloat16),
            pltpu.VMEM((2, GB, 2 * PAIRS), jnp.bfloat16),
            pltpu.VMEM((8, G_DEV, NS), jnp.bfloat16),
            pltpu.VMEM((8, G_DEV, NS), jnp.bfloat16),
            pltpu.VMEM((8, G_DEV, NS), jnp.bfloat16),
            half(6), half(4), half(3), half(2),
            dma((2,)), dma((8,)), dma((8,)), dma((6,)), dma((6,)), dma((4,)), dma((4,)),
            dma((3,)), dma((3,)), dma((1,)), dma((1,)),
        ],
        compiler_params=pltpu.CompilerParams(
            collective_id=3, has_side_effects=True, vmem_limit_bytes=VMEM_LIMIT
        ),
        name="back",
    )(rows, slab)


def places_kernel(mine, out, send_sem, recv_sem):
    row, col = lax.axis_index("row"), lax.axis_index("col")
    barrier = pltpu.get_barrier_semaphore()
    peers = [{"row": (row + k) % 8, "col": col} for k in range(1, 8)]
    for peer in peers:
        pl.semaphore_signal(barrier, inc=1, device_id=peer, device_id_type=MESH)
    pl.semaphore_wait(barrier, 7)
    copies = []
    for k, peer in enumerate(peers):
        copies.append(
            pltpu.make_async_remote_copy(
                mine, out.at[row], send_sem.at[k], recv_sem.at[k], device_id=peer, device_id_type=MESH
            )
        )
        copies[-1].start()
    out[row] = mine[...]
    for copy in copies:
        copy.wait_recv()
    for copy in copies:
        copy.wait_send()


def places(mine):
    return pl.pallas_call(
        places_kernel,
        in_specs=[pl.BlockSpec(memory_space=pltpu.VMEM)],
        out_specs=pl.BlockSpec(memory_space=pltpu.VMEM),
        out_shape=jax.ShapeDtypeStruct((8, G_ROW // 128, 128), jnp.int32),
        scratch_shapes=[pltpu.SemaphoreType.DMA((7,)), pltpu.SemaphoreType.DMA((7,))],
        compiler_params=pltpu.CompilerParams(collective_id=1, has_side_effects=True),
        name="places",
    )(mine)


def body(psi_val, psi_cond, energy_val, energy_cond, stick_map, gvec_map, slab_index):
    row = lax.axis_index("row")
    fold = lambda psi: (psi[:, :, :HALF], jnp.flip(psi[:, :, HALF:], axis=2))
    cond = jnp.concatenate(fold(psi_cond.transpose(1, 0, 2)), axis=2)
    val = jnp.stack([half.reshape(2, PX // 2, NV, HALF) for half in fold(psi_val.transpose(1, 0, 2))], axis=1)
    val = val.reshape(4, PX // 2, NV, HALF)

    mine = lax.dynamic_slice(stick_map, (row * STK,), (STK,))
    cols = lax.dynamic_slice(slab_index, (row * JS,), (JS,))
    maps = places(gvec_map.reshape(G_ROW // 128, 128)).reshape(-1)
    place = jnp.take(maps, cols)
    col_kx = place // STK
    col_stick = jnp.take(stick_map, cols // G_ROW * STK + place % STK)
    pad = jnp.zeros((LANES - STK,), jnp.int32)
    flat = jnp.concatenate([mine, pad, col_stick])
    ky, kz = flat // NZ, flat % NZ
    tc, ts = half_phase(ky, kz)
    turn = ((ky + kz) % 96).astype(jnp.float32) * (math.pi / 48.0)
    rot = jnp.stack([jnp.cos(turn[:LANES]), jnp.sin(turn[:LANES])])
    dy = jnp.array([0, 0, 0, 1, 1, 1, 0, 1], jnp.int32)
    dx = jnp.array([0, 1, 3, 0, 1, 3, 2, 2], jnp.int32)
    source = (row // 4 + dy) % 2 * 4 + (row % 4 + dx) % 4
    xs = (source[:, None] * PX + jnp.arange(PX, dtype=jnp.int32)[None, :]).reshape(NX)
    theta = (
        ((ky + kz)[None, LANES:] - 2 * (xs[:, None] * col_kx[None, :]) + 96 * NX) % 96
    ).astype(jnp.float32) * (math.pi / 48.0)
    ph = jnp.stack([jnp.cos(theta), jnp.sin(theta)], axis=1)

    weight = jnp.sqrt(2.0 / (energy_cond[None, :] - energy_val[:, None])) * (
        1.0 / (math.sqrt(NY * NZ) * math.sqrt(NX))
    )
    weight = weight.reshape(PAIRS)
    wide = jnp.broadcast_to(weight[:, None], (PAIRS, JS))
    freq = jnp.arange(NX, dtype=jnp.int32)
    ax = (freq[:, None] * xs[None, :] % NX).astype(jnp.float32) * (2.0 * math.pi / NX)
    cx, sx = jnp.cos(ax), jnp.sin(ax)
    table = jnp.concatenate(
        [jnp.concatenate([cx, sx], axis=1), jnp.concatenate([-sx, cx], axis=1)], axis=0
    ).astype(jnp.bfloat16)

    m, slab = front(weight, cond, val, tc, ts, rot, ph, wide, table)
    return back(pick(gvec_map, m.reshape(2, NX, PAIRS, LANES)), slab)


def solution(mesh):
    in_specs = (P(None, "row", None), P("col", "row", None), P(), P("col"), P(), P("row"), P())
    out_specs = P(("row", "col"), None)
    return jax.shard_map(body, mesh=mesh, in_specs=in_specs, out_specs=out_specs, check_vma=False)
```

```python
import math

import jax
import jax.numpy as jnp
from jax import lax
from jax.experimental import pallas as pl
from jax.experimental.pallas import tpu as pltpu
from jax.sharding import PartitionSpec as P

NX = 48
NY = 48
NZ = 48
CELLS = NY * NZ
HALF = CELLS // 2
NC = 256
NV = 16
CL = 16
PAIRS = NV * CL
STK = 192
G_ROW = 5120
NS = 1024
JS = 128
XB = 4
LANES = 256
VMEM_LIMIT = 60 * 1024 * 1024
MESH = pl.DeviceIdType.MESH


def half_phase(ky, kz):
    unit = math.pi / 48.0
    y = 2 * jnp.arange(NY // 2, dtype=jnp.int32) + 1
    z = 2 * jnp.arange(NZ, dtype=jnp.int32) + 1
    ay = ((y[:, None] * ky[None, :]) % 96).astype(jnp.float32) * unit
    az = ((z[:, None] * kz[None, :]) % 96).astype(jnp.float32) * unit
    cy, sy = jnp.cos(ay)[:, None, :], jnp.sin(ay)[:, None, :]
    cz, sz = jnp.cos(az)[None, :, :], jnp.sin(az)[None, :, :]
    cos = (cy * cz - sy * sz).reshape(HALF, -1)
    sin = -(sy * cz + cy * sz).reshape(HALF, -1)
    return cos.astype(jnp.bfloat16), sin.astype(jnp.bfloat16)


BLOCKS = 8
PX = NX // BLOCKS
PT = 3
PB = 16


def density(vf, cbuf, b, plane, at, even, odd):
    def one(v, carry):
        out = pl.ds(pl.multiple_of(at * PAIRS + v * CL, CL), CL)
        cond = cbuf.at[b, plane]
        spread = lambda h: jnp.broadcast_to(vf[h, plane, pl.ds(v, 1), :], (CL, HALF)).astype(jnp.bfloat16)
        lo = spread(0) * cond[:, :HALF]
        hi = spread(1) * cond[:, HALF:]
        even[out, :] = lo + hi
        odd[out, :] = lo - hi
        return carry

    lax.fori_loop(0, NV, one, 0, unroll=4)


def transform(b, first, even, odd, tc, ts, rot, ph, y, sacc):
    a = jnp.dot(even[...], tc[...], preferred_element_type=jnp.float32)
    c = jnp.dot(odd[...], ts[...], preferred_element_type=jnp.float32)
    cosr, sinr = rot[0:1, :], rot[1:2, :]
    real, imag = sacc[0], sacc[1]
    for i in range(PT):
        x = b * PX + first + i
        rows = slice(i * PAIRS, i * PAIRS + PAIRS)
        am, cm = a[rows, :LANES], c[rows, :LANES]
        y[x, 0] = (cosr * am - sinr * cm).astype(jnp.bfloat16)
        y[x, 1] = (cosr * cm + sinr * am).astype(jnp.bfloat16)
        av, cv = a[rows, LANES:], c[rows, LANES:]
        cp, sp = ph[x, 0:1, :], ph[x, 1:2, :]
        real = real + (cp * av - sp * cv)
        imag = imag + (cp * cv + sp * av)
    sacc[0] = real
    sacc[1] = imag


def front_kernel(
    weights, cond, val, cond_y, val_y, tc, ts, rot, ph, wide, table, m_out, slab_out,
    cbuf, vbuf, vf, even, odd, y, sacc, sl, yr, yi, mo, mb,
    lsem, cs, cr, vs, vr, gs, gr, ss, sr, fs, fr, ms,
):
    row, col = lax.axis_index("row"), lax.axis_index("col")
    yh, x = row // 4, row % 4
    z, yl, core = col // 4, (col // 2) % 2, col % 2
    zo = z + 1 - 2 * (z % 2)
    xp = {"row": yh * 4 + (x + 1) % 4, "col": col}
    xm = {"row": yh * 4 + (x + 3) % 4, "col": col}
    group = [
        {"row": row, "col": zo * 4 + yl * 2 + core},
        {"row": row, "col": z * 4 + yl * 2 + 1 - core},
        {"row": row, "col": zo * 4 + yl * 2 + 1 - core},
    ]
    across = [{"row": (row + k) % 8, "col": col} for k in range(1, 8)]
    part = core * 2 + z % 2

    own = [
        pltpu.make_async_copy(cond, cbuf.at[0], lsem.at[0]),
        pltpu.make_async_copy(val, vbuf.at[0], lsem.at[1]),
        pltpu.make_async_copy(cond_y, cbuf.at[1], lsem.at[2]),
        pltpu.make_async_copy(val_y, vbuf.at[1, part], lsem.at[3]),
    ]
    for copy in own:
        copy.start()
    barrier = pltpu.get_barrier_semaphore()
    for peer in across + group:
        pl.semaphore_signal(barrier, inc=1, device_id=peer, device_id_type=MESH)
    pl.semaphore_wait(barrier, 10)

    hops = [(0, 3, xp), (0, 2, xm), (1, 5, xp), (1, 4, xm), (3, 6, xp), (4, 7, xm)]

    def relay(n):
        src, dst, peer = hops[n]
        c = pltpu.make_async_remote_copy(
            (cond, cond_y)[src] if src < 2 else cbuf.at[src], cbuf.at[dst], cs.at[n], cr.at[dst],
            device_id=peer, device_id_type=MESH,
        )
        v = pltpu.make_async_remote_copy(
            (val.at[part], val_y)[src] if src < 2 else vbuf.at[src, part], vbuf.at[dst, part], vs.at[n], vr.at[dst],
            device_id=peer, device_id_type=MESH,
        )
        return v, c

    def go(n):
        for copy in relay(n):
            copy.start()

    def incoming(dst):
        return relay([hop[1] for hop in hops].index(dst))

    def spread(b, j):
        return pltpu.make_async_remote_copy(
            vbuf.at[b, part], vbuf.at[b, part], gs.at[b * 3 + j], gr.at[b * 3 + j],
            device_id=group[j], device_id_type=MESH,
        )

    def land(b, *forward):
        v, c = incoming(b)
        v.wait_recv()
        for j in range(3):
            spread(b, j).start()
        c.wait_recv()
        for n in forward:
            go(n)

    def ready(b):
        for j in range(3):
            spread(b, j).wait_recv()

    for n in range(2):
        go(n)
    for copy in own:
        copy.wait()
    for j in range(3):
        spread(1, j).start()
    for n in range(2, 4):
        go(n)
    sacc[...] = jnp.zeros_like(sacc)

    def block(b, carry):
        @pl.when(b == 1)
        def _():
            ready(1)

        @pl.when(b == 2)
        def _():
            land(3, 4)
            land(2)
            ready(2)

        @pl.when(b == 3)
        def _():
            ready(3)

        @pl.when(b == 4)
        def _():
            land(4, 5)
            land(5)
            ready(4)

        @pl.when(b == 5)
        def _():
            ready(5)

        @pl.when(b == 6)
        def _():
            land(6)
            ready(6)

        @pl.when(b == 7)
        def _():
            land(7)
            ready(7)

        def widen(j, carry):
            for q in range(4):
                vf[q % 2, (q // 2) * 3 + j] = vbuf[b, q, j].astype(jnp.float32)
            return carry

        lax.fori_loop(0, 3, widen, 0)

        def some(i, carry):
            for u in range(PT):
                density(vf, cbuf, b, i * PT + u, u, even, odd)
            transform(b, i * PT, even, odd, tc, ts, rot, ph, y, sacc)
            return carry

        lax.fori_loop(0, PX // PT, some, 0)
        return carry

    lax.fori_loop(0, BLOCKS, block, 0)

    for h in range(2):
        sl[h * PAIRS : h * PAIRS + PAIRS, :] = (sacc[h] * wide[...]).astype(jnp.bfloat16)
    keep = pltpu.make_async_copy(sl, slab_out.at[0, row], lsem.at[4])
    keep.start()

    def push(k):
        return pltpu.make_async_remote_copy(
            sl, slab_out.at[0, row], ss.at[k], sr.at[k], device_id=across[k], device_id_type=MESH
        )

    def hand(k):
        at = (row + 7 - k) % 8
        return pltpu.make_async_remote_copy(
            sl if k == 7 else slab_out.at[0, at], slab_out.at[1, at], fs.at[k], fr.at[k],
            device_id=group[1], device_id_type=MESH,
        )

    for k in range(7):
        push(k).start()
    hand(7).start()

    def chunk(i, carry):
        for k in range(7):

            @pl.when(i == 5 + k)
            def _():
                push(k).wait_recv()
                hand(k).start()

        slot = i % 2
        ps = pl.ds(pl.multiple_of(i * PB, PB), PB)
        out = pltpu.make_async_copy(mb.at[slot], m_out.at[:, ps, :], ms.at[slot])
        for h in range(LANES // 128):
            lanes = slice(h * 128, h * 128 + 128)
            yr[h] = y[:, 0, ps, lanes].astype(jnp.float32).reshape(NX * PB, 128)
            yi[h] = y[:, 1, ps, lanes].astype(jnp.float32).reshape(NX * PB, 128)
        for p in range(PB):
            at = pl.ds(p, NX, stride=PB)
            real = jnp.concatenate([yr[0, at, :], yr[1, at, :]], axis=1)
            imag = jnp.concatenate([yi[0, at, :], yi[1, at, :]], axis=1)
            rhs = jnp.concatenate([real, imag], axis=0).astype(jnp.bfloat16)
            res = jnp.dot(table[...], rhs, preferred_element_type=jnp.float32) * weights[i * PB + p]
            for h in range(LANES // 128):
                mo[h, pl.ds(p, 2 * NX, stride=PB), :] = res[:, h * 128 : h * 128 + 128]

        @pl.when(i >= 2)
        def _():
            out.wait()

        for h in range(LANES // 128):
            lanes = slice(h * 128, h * 128 + 128)
            mb[slot, :, :, lanes] = mo[h].reshape(2 * NX, PB, 128).astype(jnp.bfloat16)
        out.start()
        return carry

    lax.fori_loop(0, PAIRS // PB, chunk, 0)
    for slot in range(2):
        pltpu.make_async_copy(mb.at[slot], m_out.at[:, pl.ds(slot * PB, PB), :], ms.at[slot]).wait()
    keep.wait()
    for k in range(8):
        hand(k).wait_recv()
        hand(k).wait_send()
    for k in range(7):
        push(k).wait_send()
    for n in range(len(hops)):
        for copy in relay(n):
            copy.wait_send()
    for b in range(1, BLOCKS):
        for j in range(3):
            spread(b, j).wait_send()


def front(weights, cond, val, cond_y, val_y, tc, ts, rot, ph, wide, table):
    dma = pltpu.SemaphoreType.DMA
    vmem = pl.BlockSpec(memory_space=pltpu.VMEM)
    hbm = pl.BlockSpec(memory_space=pl.ANY)
    bf = lambda *shape: pltpu.VMEM(shape, jnp.bfloat16)
    fl = lambda *shape: pltpu.VMEM(shape, jnp.float32)
    return pl.pallas_call(
        front_kernel,
        in_specs=[pl.BlockSpec(memory_space=pltpu.SMEM)] + [vmem] * 10,
        out_specs=[hbm, hbm],
        out_shape=[
            jax.ShapeDtypeStruct((2 * NX, PAIRS, LANES), jnp.bfloat16),
            jax.ShapeDtypeStruct((2, BLOCKS, 2 * PAIRS, JS), jnp.bfloat16),
        ],
        scratch_shapes=[
            bf(BLOCKS, PX, CL, CELLS),
            bf(BLOCKS, 4, PX // 2, NV, HALF),
            fl(2, PX, NV, HALF),
            bf(PT * PAIRS, HALF),
            bf(PT * PAIRS, HALF),
            bf(NX, 2, PAIRS, LANES),
            fl(2, PAIRS, JS),
            bf(2 * PAIRS, JS),
            fl(2, NX * PB, 128),
            fl(2, NX * PB, 128),
            fl(2, 2 * NX * PB, 128),
            bf(2, 2 * NX, PB, LANES),
            dma((5,)), dma((6,)), dma((8,)), dma((6,)), dma((8,)),
            dma((24,)), dma((24,)), dma((7,)), dma((7,)), dma((8,)), dma((8,)), dma((2,)),
        ],
        compiler_params=pltpu.CompilerParams(
            collective_id=2, has_side_effects=True, vmem_limit_bytes=VMEM_LIMIT
        ),
        name="front",
    )(weights, cond, val, cond_y, val_y, tc, ts, rot, ph, wide, table)


GB = 320
QS = 2 * PAIRS // 128
G_DEV = 320
HR = G_DEV // 2
DEPTH = 4
UNROLL = 16


def pick_kernel(g_ref, m, out, mt, mi, sel, lhs, ms, os):
    def fetch(step):
        slot = step % DEPTH
        return pltpu.make_async_copy(m.at[:, step], mi.at[slot], ms.at[slot])

    for step in range(DEPTH):
        fetch(step).start()

    def turn(step, carry):
        fetch(step).wait()
        for h in range(2):
            for q in range(2):
                t = mi[step % DEPTH, h, q * 128 : q * 128 + 128, :].T.astype(jnp.float32)
                mt[pl.ds(step * (STK * QS) + h * 2 + q, STK, stride=QS), :] = t[:STK, :]

        @pl.when(step < NX - DEPTH)
        def _():
            fetch(step + DEPTH).start()

        return carry

    lax.fori_loop(0, NX, turn, 0)
    store = lambda n: pltpu.make_async_copy(lhs.at[n % 2], out.at[n], os.at[n % 2])

    def block(n, carry):
        def rows(i, carry):
            for u in range(UNROLL):
                g = g_ref[n * GB + i * UNROLL + u]
                to = pl.ds(pl.multiple_of((i * UNROLL + u) * QS, QS), QS)
                sel[to, :] = mt[pl.ds(pl.multiple_of(g * QS, QS), QS), :]
            return carry

        lax.fori_loop(0, GB // UNROLL, rows, 0)

        @pl.when(n >= 2)
        def _():
            store(n - 2).wait()

        for k in range(QS):
            lhs[n % 2, :, k * 128 : k * 128 + 128] = sel[pl.ds(k, GB, stride=QS), :].astype(jnp.bfloat16)
        store(n).start()
        return carry

    lax.fori_loop(0, G_ROW // GB, block, 0)
    for n in range(2):
        store(G_ROW // GB - 2 + n).wait()


def pick(gvec, m):
    dma = pltpu.SemaphoreType.DMA
    return pl.pallas_call(
        pick_kernel,
        in_specs=[pl.BlockSpec(memory_space=pltpu.SMEM), pl.BlockSpec(memory_space=pl.ANY)],
        out_specs=pl.BlockSpec(memory_space=pl.ANY),
        out_shape=jax.ShapeDtypeStruct((G_ROW // GB, GB, 2 * PAIRS), jnp.bfloat16),
        scratch_shapes=[
            pltpu.VMEM((NX * STK * QS, 128), jnp.float32),
            pltpu.VMEM((DEPTH, 2, PAIRS, LANES), jnp.bfloat16),
            pltpu.VMEM((GB * QS, 128), jnp.float32),
            pltpu.VMEM((2, GB, 2 * PAIRS), jnp.bfloat16),
            dma((DEPTH,)), dma((2,)),
        ],
        compiler_params=pltpu.CompilerParams(vmem_limit_bytes=VMEM_LIMIT),
        name="pick",
    )(gvec, m)


def add_rows(dst, a, b, rows, step=32):
    def one(i, carry):
        at = pl.ds(pl.multiple_of(i * step, step), step)
        dst[at, :] = (a[at, :].astype(jnp.float32) + b[at, :].astype(jnp.float32)).astype(dst.dtype)
        return carry

    lax.fori_loop(0, rows // step, one, 0)


def back_kernel(
    rows, slab, out, sw, ours, theirs, acc, zr2, yr1, zr1, yr2,
    ms, s1, d1, sz2, dz2, sy1, dy1, sz1, dz1, sy2, dy2,
):
    row, col = lax.axis_index("row"), lax.axis_index("col")
    z, yl, core = col // 4, (col // 2) % 2, col % 2
    core_peer = {"row": row, "col": z * 4 + yl * 2 + (1 - core)}
    y_peer = {"row": row, "col": z * 4 + (1 - yl) * 2 + core}
    z_peer = lambda k: {"row": row, "col": ((z + k) % 4) * 4 + yl * 2 + core}
    barrier = pltpu.get_barrier_semaphore()
    for peer in (core_peer, y_peer, z_peer(1), z_peer(2), z_peer(3)):
        pl.semaphore_signal(barrier, inc=1, device_id=peer, device_id_type=MESH)

    def place(n):
        k, s = (n // 2 + 1) % 4, n % 2
        return ((z + k) % 4) * 4 + (yl * s + (1 - yl) * (1 - s)) * 2

    load = lambda n: pltpu.make_async_copy(rows.at[place(n) + core], ours.at[n], ms.at[n])
    for n in range(8):
        load(n).start()
    pl.semaphore_wait(barrier, 5)

    scale = -1.0 / math.sqrt(NV * NC)
    def remote(src, dst, ss, ds, peer):
        return pltpu.make_async_remote_copy(src, dst, ss, ds, device_id=peer, device_id_type=MESH)

    lo, hi = pl.ds(0, HR), pl.ds(HR, HR)
    first = lambda n: remote(rows.at[place(n) + 1 - core], theirs.at[n], s1.at[n], d1.at[n], core_peer)
    for n in range(8):
        first(n).start()
    for h in range(2):
        for r in range(NS // JS):
            sw[h * 2 * PAIRS : (h + 1) * 2 * PAIRS, r * JS : r * JS + JS] = slab[h, r]
    along_z = lambda k, s: remote(
        acc.at[(k + 3) % 4 * 2 + s, hi], zr2.at[(k - 1) * 2 + s], sz2.at[(k - 1) * 2 + s], dz2.at[(k - 1) * 2 + s], z_peer(k)
    )
    along_y = lambda k: remote(acc.at[(k + 3) % 4 * 2, lo], yr1.at[k], sy1.at[k], dy1.at[k], y_peer)
    last_z = lambda k: remote(acc.at[(k + 3) % 4 * 2 + 1, lo], zr1.at[k - 1], sz1.at[k - 1], dz1.at[k - 1], z_peer(k))

    def slot(n, carry):
        k, s = (n // 2 + 1) % 4, n % 2
        load(n).wait()
        first(n).wait_recv()
        lhs = jnp.concatenate([ours[n], theirs[n]], axis=1)
        acc[n] = (jnp.dot(lhs, sw[...], preferred_element_type=jnp.float32) * scale).astype(jnp.bfloat16)

        @pl.when(n < 6)
        def _():
            along_z(k, s).start()

        @pl.when(s == 0)
        def _():
            along_y(k).start()

        return carry

    lax.fori_loop(0, 8, slot, 0)
    for k in (1, 2, 3, 0):
        along_y(k).wait_recv()
        if k:
            at = acc.at[(k + 3) % 4 * 2 + 1]
            add_rows(at, at, yr1.at[k], HR)
            last_z(k).start()
    for k in (1, 2, 3):
        along_z(k, 0).wait_recv()

    def total(i, base, terms):
        at = pl.ds(pl.multiple_of(i * 16, 16), 16)
        value = base[at, :].astype(jnp.float32)
        for ref in terms:
            value = value + ref[at, :].astype(jnp.float32)
        return at, value

    def across(i, carry):
        at, value = total(i, acc.at[6, hi], [zr2.at[0], zr2.at[2], zr2.at[4]])
        yr2[0, at, :] = value.astype(jnp.bfloat16)
        return carry

    lax.fori_loop(0, HR // 16, across, 0)
    last_y = remote(yr2.at[0], yr2.at[1], sy2.at[0], dy2.at[0], y_peer)
    last_y.start()
    for k in (1, 2, 3):
        last_z(k).wait_recv()

    def low(i, carry):
        at, value = total(i, acc.at[7, lo], [yr1.at[0], zr1.at[0], zr1.at[1], zr1.at[2]])
        out[at, :] = value
        return carry

    lax.fori_loop(0, HR // 16, low, 0)
    for k in (1, 2, 3):
        along_z(k, 1).wait_recv()
    last_y.wait_recv()

    def high(i, carry):
        at, value = total(i, acc.at[7, hi], [zr2.at[1], zr2.at[3], zr2.at[5], yr2.at[1]])
        out[pl.ds(pl.multiple_of(HR + i * 16, 16), 16), :] = value
        return carry

    lax.fori_loop(0, HR // 16, high, 0)
    for n in range(8):
        first(n).wait_send()
    for k in range(4):
        along_y(k).wait_send()
        if k:
            last_z(k).wait_send()
            along_z(k, 0).wait_send()
            along_z(k, 1).wait_send()
    last_y.wait_send()


def back(rows, slab):
    dma = pltpu.SemaphoreType.DMA
    vmem = pl.BlockSpec(memory_space=pltpu.VMEM)
    half = lambda n: pltpu.VMEM((n, HR, NS), jnp.bfloat16)
    return pl.pallas_call(
        back_kernel,
        in_specs=[pl.BlockSpec(memory_space=pl.ANY), vmem],
        out_specs=vmem,
        out_shape=jax.ShapeDtypeStruct((G_DEV, NS), jnp.float32),
        scratch_shapes=[
            pltpu.VMEM((4 * PAIRS, NS), jnp.bfloat16),
            pltpu.VMEM((8, GB, 2 * PAIRS), jnp.bfloat16),
            pltpu.VMEM((8, GB, 2 * PAIRS), jnp.bfloat16),
            pltpu.VMEM((8, G_DEV, NS), jnp.bfloat16),
            half(6), half(4), half(3), half(2),
            dma((8,)), dma((8,)), dma((8,)), dma((6,)), dma((6,)), dma((4,)), dma((4,)),
            dma((3,)), dma((3,)), dma((1,)), dma((1,)),
        ],
        compiler_params=pltpu.CompilerParams(
            collective_id=3, has_side_effects=True, vmem_limit_bytes=VMEM_LIMIT
        ),
        name="back",
    )(rows, slab)


def places_kernel(mine, cond, val, out, cond_out, val_out, send_sem, recv_sem, ys, yr):
    row, col = lax.axis_index("row"), lax.axis_index("col")
    z, yl, core = col // 4, (col // 2) % 2, col % 2
    barrier = pltpu.get_barrier_semaphore()
    peers = [{"row": (row + k) % 8, "col": col} for k in range(1, 8)]
    yc = {"row": (row + 4) % 8, "col": col}
    yv = {"row": (row + 4) % 8, "col": z * 4 + (1 - yl) * 2 + core}
    for peer in peers + [yv]:
        pl.semaphore_signal(barrier, inc=1, device_id=peer, device_id_type=MESH)
    pl.semaphore_wait(barrier, 8)
    copies = [
        pltpu.make_async_remote_copy(
            cond, cond_out, ys.at[0], yr.at[0], device_id=yc, device_id_type=MESH
        ),
        pltpu.make_async_remote_copy(
            val.at[core * 2 + z % 2], val_out, ys.at[1], yr.at[1], device_id=yv, device_id_type=MESH
        ),
    ]
    for k, peer in enumerate(peers):
        copies.append(
            pltpu.make_async_remote_copy(
                mine, out.at[row], send_sem.at[k], recv_sem.at[k], device_id=peer, device_id_type=MESH
            )
        )
    for copy in copies:
        copy.start()
    out[row] = mine[...]
    for copy in copies:
        copy.wait_recv()
    for copy in copies:
        copy.wait_send()


def places(mine, cond, val):
    dma = pltpu.SemaphoreType.DMA
    vmem = pl.BlockSpec(memory_space=pltpu.VMEM)
    return pl.pallas_call(
        places_kernel,
        in_specs=[vmem] * 3,
        out_specs=[vmem] * 3,
        out_shape=[
            jax.ShapeDtypeStruct((8, G_ROW // 128, 128), jnp.int32),
            jax.ShapeDtypeStruct((PX, CL, CELLS), jnp.bfloat16),
            jax.ShapeDtypeStruct((PX // 2, NV, HALF), jnp.bfloat16),
        ],
        scratch_shapes=[dma((7,)), dma((7,)), dma((2,)), dma((2,))],
        compiler_params=pltpu.CompilerParams(collective_id=1, has_side_effects=True),
        name="places",
    )(mine, cond, val)


def body(psi_val, psi_cond, energy_val, energy_cond, stick_map, gvec_map, slab_index):
    row = lax.axis_index("row")
    fold = lambda psi: (psi[:, :, :HALF], jnp.flip(psi[:, :, HALF:], axis=2))
    cond = jnp.concatenate(fold(psi_cond.transpose(1, 0, 2)), axis=2)
    val = jnp.stack([half.reshape(2, PX // 2, NV, HALF) for half in fold(psi_val.transpose(1, 0, 2))], axis=1)
    val = val.reshape(4, PX // 2, NV, HALF)

    mine = lax.dynamic_slice(stick_map, (row * STK,), (STK,))
    cols = lax.dynamic_slice(slab_index, (row * JS,), (JS,))
    maps, cond_y, val_y = places(gvec_map.reshape(G_ROW // 128, 128), cond, val)
    maps = maps.reshape(-1)
    place = jnp.take(maps, cols)
    col_kx = place // STK
    col_stick = jnp.take(stick_map, cols // G_ROW * STK + place % STK)
    pad = jnp.zeros((LANES - STK,), jnp.int32)
    flat = jnp.concatenate([mine, pad, col_stick])
    ky, kz = flat // NZ, flat % NZ
    tc, ts = half_phase(ky, kz)
    turn = ((ky + kz) % 96).astype(jnp.float32) * (math.pi / 48.0)
    rot = jnp.stack([jnp.cos(turn[:LANES]), jnp.sin(turn[:LANES])])
    dy = jnp.array([0, 1, 0, 0, 1, 1, 0, 1], jnp.int32)
    dx = jnp.array([0, 0, 1, 3, 1, 3, 2, 2], jnp.int32)
    source = (row // 4 + dy) % 2 * 4 + (row % 4 + dx) % 4
    xs = (source[:, None] * PX + jnp.arange(PX, dtype=jnp.int32)[None, :]).reshape(NX)
    theta = (
        ((ky + kz)[None, LANES:] - 2 * (xs[:, None] * col_kx[None, :]) + 96 * NX) % 96
    ).astype(jnp.float32) * (math.pi / 48.0)
    ph = jnp.stack([jnp.cos(theta), jnp.sin(theta)], axis=1)

    weight = jnp.sqrt(2.0 / (energy_cond[None, :] - energy_val[:, None])) * (
        1.0 / (math.sqrt(NY * NZ) * math.sqrt(NX))
    )
    weight = weight.reshape(PAIRS)
    wide = jnp.broadcast_to(weight[:, None], (PAIRS, JS))
    freq = jnp.arange(NX, dtype=jnp.int32)
    ax = (freq[:, None] * xs[None, :] % NX).astype(jnp.float32) * (2.0 * math.pi / NX)
    cx, sx = jnp.cos(ax), jnp.sin(ax)
    table = jnp.concatenate(
        [jnp.concatenate([cx, sx], axis=1), jnp.concatenate([-sx, cx], axis=1)], axis=0
    ).astype(jnp.bfloat16)

    m, slab = front(weight, cond, val, cond_y, val_y, tc, ts, rot, ph, wide, table)
    return back(pick(gvec_map, m.reshape(2, NX, PAIRS, LANES)), slab)


def solution(mesh):
    in_specs = (P(None, "row", None), P("col", "row", None), P(), P("col"), P(), P("row"), P())
    out_specs = P(("row", "col"), None)
    return jax.shard_map(body, mesh=mesh, in_specs=in_specs, out_specs=out_specs, check_vma=False)
```

```python
import math

import jax
import jax.numpy as jnp
from jax import lax
from jax.experimental import pallas as pl
from jax.experimental.pallas import tpu as pltpu
from jax.sharding import PartitionSpec as P

NX = 48
NY = 48
NZ = 48
CELLS = NY * NZ
HALF = CELLS // 2
NC = 256
NV = 16
CL = 16
PAIRS = NV * CL
STK = 192
G_ROW = 5120
NS = 1024
JS = 128
XB = 4
LANES = 256
VMEM_LIMIT = 60 * 1024 * 1024
MESH = pl.DeviceIdType.MESH


def half_phase(ky, kz):
    unit = math.pi / 48.0
    y = 2 * jnp.arange(NY // 2, dtype=jnp.int32) + 1
    z = 2 * jnp.arange(NZ, dtype=jnp.int32) + 1
    ay = ((y[:, None] * ky[None, :]) % 96).astype(jnp.float32) * unit
    az = ((z[:, None] * kz[None, :]) % 96).astype(jnp.float32) * unit
    cy, sy = jnp.cos(ay)[:, None, :], jnp.sin(ay)[:, None, :]
    cz, sz = jnp.cos(az)[None, :, :], jnp.sin(az)[None, :, :]
    cos = (cy * cz - sy * sz).reshape(HALF, -1)
    sin = -(sy * cz + cy * sz).reshape(HALF, -1)
    return cos.astype(jnp.bfloat16), sin.astype(jnp.bfloat16)


BLOCKS = 8
PX = NX // BLOCKS
PT = 3
PB = 16


def density(vf, cbuf, b, plane, at, even, odd):
    cond = cbuf.at[b, plane]
    for v in range(NV):
        out = slice(at * PAIRS + v * CL, at * PAIRS + v * CL + CL)
        spread = lambda h: jnp.broadcast_to(vf[h, plane, v : v + 1, :], (CL, HALF)).astype(jnp.bfloat16)
        lo = spread(0) * cond[:, :HALF]
        hi = spread(1) * cond[:, HALF:]
        even[out, :] = lo + hi
        odd[out, :] = lo - hi


def transform(b, first, even, odd, tc, ts, rot, ph, y, sacc):
    a = jnp.dot(even[...], tc[...], preferred_element_type=jnp.float32)
    c = jnp.dot(odd[...], ts[...], preferred_element_type=jnp.float32)
    cosr, sinr = rot[0:1, :], rot[1:2, :]
    real, imag = sacc[0], sacc[1]
    for i in range(PT):
        x = b * PX + first + i
        rows = slice(i * PAIRS, i * PAIRS + PAIRS)
        am, cm = a[rows, :LANES], c[rows, :LANES]
        y[x, 0] = (cosr * am - sinr * cm).astype(jnp.bfloat16)
        y[x, 1] = (cosr * cm + sinr * am).astype(jnp.bfloat16)
        av, cv = a[rows, LANES:], c[rows, LANES:]
        cp, sp = ph[x, 0:1, :], ph[x, 1:2, :]
        real = real + (cp * av - sp * cv)
        imag = imag + (cp * cv + sp * av)
    sacc[0] = real
    sacc[1] = imag


def front_kernel(
    weights, cond, val, tc, ts, rot, ph, wide, table, m_out, slab_out,
    cbuf, vbuf, vf, even, odd, y, sacc, sl, yr, yi, mo, mb,
    lsem, cs, cr, vs, vr, gs, gr, ss, sr, fs, fr, ms,
):
    row, col = lax.axis_index("row"), lax.axis_index("col")
    yh, x = row // 4, row % 4
    z, yl, core = col // 4, (col // 2) % 2, col % 2
    zo = z + 1 - 2 * (z % 2)
    xp = {"row": yh * 4 + (x + 1) % 4, "col": col}
    xm = {"row": yh * 4 + (x + 3) % 4, "col": col}
    yc = {"row": (1 - yh) * 4 + x, "col": col}
    yv = {"row": (1 - yh) * 4 + x, "col": z * 4 + (1 - yl) * 2 + core}
    group = [
        {"row": row, "col": zo * 4 + yl * 2 + core},
        {"row": row, "col": z * 4 + yl * 2 + 1 - core},
        {"row": row, "col": zo * 4 + yl * 2 + 1 - core},
    ]
    across = [{"row": (row + k) % 8, "col": col} for k in range(1, 8)]
    part = core * 2 + z % 2

    own = [
        pltpu.make_async_copy(cond, cbuf.at[0], lsem.at[0]),
        pltpu.make_async_copy(val, vbuf.at[0], lsem.at[1]),
    ]
    for copy in own:
        copy.start()
    barrier = pltpu.get_barrier_semaphore()
    for peer in across + group + [yv]:
        pl.semaphore_signal(barrier, inc=1, device_id=peer, device_id_type=MESH)
    pl.semaphore_wait(barrier, 11)

    hops = [(0, 3, None), (0, 2, xp), (0, 1, xm), (3, 6, xp), (3, 5, xm), (2, 4, xp), (5, 7, xm)]
    hop_to = [hop[1] for hop in hops]

    def cond_hop(n):
        src, dst, peer = hops[n]
        return pltpu.make_async_remote_copy(
            cbuf.at[src] if src else cond, cbuf.at[dst], cs.at[n], cr.at[dst],
            device_id=peer or yc, device_id_type=MESH,
        )

    def val_hop(n):
        src, dst, peer = hops[n]
        return pltpu.make_async_remote_copy(
            vbuf.at[src, part] if src else val.at[part], vbuf.at[dst, part], vs.at[n], vr.at[dst],
            device_id=peer or yv, device_id_type=MESH,
        )

    def spread(b, j):
        return pltpu.make_async_remote_copy(
            vbuf.at[b, part], vbuf.at[b, part], gs.at[b * 3 + j], gr.at[b * 3 + j],
            device_id=group[j], device_id_type=MESH,
        )

    def land_val(b, *forward):
        val_hop(hop_to.index(b)).wait_recv()
        for n in forward:
            val_hop(n).start()
        for j in range(3):
            spread(b, j).start()

    def land(b, *forward):
        cond_hop(hop_to.index(b)).wait_recv()
        for n in forward:
            cond_hop(n).start()

    def ready(b):
        for j in range(3):
            spread(b, j).wait_recv()

    for n in range(3):
        val_hop(n).start()
    for n in range(3):
        cond_hop(n).start()
    sacc[...] = jnp.zeros_like(sacc)
    for copy in own:
        copy.wait()

    def block(b, carry):
        @pl.when(b == 1)
        def _():
            land_val(1)
            land_val(2, 5)
            land_val(3, 3, 4)
            land(2, 5)
            land(1)
            ready(1)

        @pl.when(b == 2)
        def _():
            land(3, 3, 4)
            land_val(4)
            land_val(5, 6)
            land_val(6)
            ready(2)

        @pl.when(b == 3)
        def _():
            land_val(7)
            ready(3)

        @pl.when(b == 4)
        def _():
            land(4)
            ready(4)

        @pl.when(b == 5)
        def _():
            land(5, 6)
            land(6)
            ready(5)

        @pl.when(b == 6)
        def _():
            ready(6)

        @pl.when(b == 7)
        def _():
            land(7)
            ready(7)

        def widen(j, carry):
            for q in range(4):
                vf[q % 2, (q // 2) * 3 + j] = vbuf[b, q, j].astype(jnp.float32)
            return carry

        lax.fori_loop(0, 3, widen, 0)

        def some(i, carry):
            for u in range(PT):
                density(vf, cbuf, b, i * PT + u, u, even, odd)
            transform(b, i * PT, even, odd, tc, ts, rot, ph, y, sacc)
            return carry

        lax.fori_loop(0, PX // PT, some, 0)
        return carry

    lax.fori_loop(0, BLOCKS, block, 0)

    for h in range(2):
        sl[h * PAIRS : h * PAIRS + PAIRS, :] = (sacc[h] * wide[...]).astype(jnp.bfloat16)
    keep = pltpu.make_async_copy(sl, slab_out.at[0, row], lsem.at[2])
    keep.start()

    def push(k):
        return pltpu.make_async_remote_copy(
            sl, slab_out.at[0, row], ss.at[k], sr.at[k], device_id=across[k], device_id_type=MESH
        )

    def hand(k):
        at = (row + 7 - k) % 8
        return pltpu.make_async_remote_copy(
            sl if k == 7 else slab_out.at[0, at], slab_out.at[1, at], fs.at[k], fr.at[k],
            device_id=group[1], device_id_type=MESH,
        )

    for k in range(7):
        push(k).start()
    hand(7).start()

    def chunk(i, carry):
        for k in range(7):

            @pl.when(i == 5 + k)
            def _():
                push(k).wait_recv()
                hand(k).start()

        slot = i % 2
        ps = pl.ds(pl.multiple_of(i * PB, PB), PB)
        out = pltpu.make_async_copy(mb.at[slot], m_out.at[:, ps, :], ms.at[slot])
        for h in range(LANES // 128):
            lanes = slice(h * 128, h * 128 + 128)
            yr[h] = y[:, 0, ps, lanes].astype(jnp.float32).reshape(NX * PB, 128)
            yi[h] = y[:, 1, ps, lanes].astype(jnp.float32).reshape(NX * PB, 128)
        for p in range(PB):
            at = pl.ds(p, NX, stride=PB)
            real = jnp.concatenate([yr[0, at, :], yr[1, at, :]], axis=1)
            imag = jnp.concatenate([yi[0, at, :], yi[1, at, :]], axis=1)
            rhs = jnp.concatenate([real, imag], axis=0).astype(jnp.bfloat16)
            res = jnp.dot(table[...], rhs, preferred_element_type=jnp.float32) * weights[i * PB + p]
            for h in range(LANES // 128):
                mo[h, pl.ds(p, 2 * NX, stride=PB), :] = res[:, h * 128 : h * 128 + 128]

        @pl.when(i >= 2)
        def _():
            out.wait()

        for h in range(LANES // 128):
            lanes = slice(h * 128, h * 128 + 128)
            mb[slot, :, :, lanes] = mo[h].reshape(2 * NX, PB, 128).astype(jnp.bfloat16)
        out.start()
        return carry

    lax.fori_loop(0, PAIRS // PB, chunk, 0)
    for slot in range(2):
        pltpu.make_async_copy(mb.at[slot], m_out.at[:, pl.ds(slot * PB, PB), :], ms.at[slot]).wait()
    keep.wait()
    for k in range(8):
        hand(k).wait_recv()
        hand(k).wait_send()
    for k in range(7):
        push(k).wait_send()
    for n in range(len(hops)):
        val_hop(n).wait_send()
        cond_hop(n).wait_send()
    for b in range(1, BLOCKS):
        for j in range(3):
            spread(b, j).wait_send()


def front(weights, cond, val, tc, ts, rot, ph, wide, table):
    dma = pltpu.SemaphoreType.DMA
    vmem = pl.BlockSpec(memory_space=pltpu.VMEM)
    hbm = pl.BlockSpec(memory_space=pl.ANY)
    bf = lambda *shape: pltpu.VMEM(shape, jnp.bfloat16)
    fl = lambda *shape: pltpu.VMEM(shape, jnp.float32)
    return pl.pallas_call(
        front_kernel,
        in_specs=[pl.BlockSpec(memory_space=pltpu.SMEM)] + [vmem] * 8,
        out_specs=[hbm, hbm],
        out_shape=[
            jax.ShapeDtypeStruct((2 * NX, PAIRS, LANES), jnp.bfloat16),
            jax.ShapeDtypeStruct((2, BLOCKS, 2 * PAIRS, JS), jnp.bfloat16),
        ],
        scratch_shapes=[
            bf(BLOCKS, PX, CL, CELLS),
            bf(BLOCKS, 4, PX // 2, NV, HALF),
            fl(2, PX, NV, HALF),
            bf(PT * PAIRS, HALF),
            bf(PT * PAIRS, HALF),
            bf(NX, 2, PAIRS, LANES),
            fl(2, PAIRS, JS),
            bf(2 * PAIRS, JS),
            fl(2, NX * PB, 128),
            fl(2, NX * PB, 128),
            fl(2, 2 * NX * PB, 128),
            bf(2, 2 * NX, PB, LANES),
            dma((3,)), dma((7,)), dma((8,)), dma((7,)), dma((8,)),
            dma((24,)), dma((24,)), dma((7,)), dma((7,)), dma((8,)), dma((8,)), dma((2,)),
        ],
        compiler_params=pltpu.CompilerParams(
            collective_id=2, has_side_effects=True, vmem_limit_bytes=VMEM_LIMIT
        ),
        name="front",
    )(weights, cond, val, tc, ts, rot, ph, wide, table)


GB = 320
QS = 2 * PAIRS // 128
G_DEV = 320
LO = 192
HI = G_DEV - LO
DEPTH = 4
UNROLL = 16


def pick_kernel(g_ref, m, out, mt, mi, sel, lhs, ms, os):
    def fetch(step):
        slot = step % DEPTH
        return pltpu.make_async_copy(m.at[:, step], mi.at[slot], ms.at[slot])

    for step in range(DEPTH):
        fetch(step).start()

    def turn(step, carry):
        fetch(step).wait()
        for h in range(2):
            for q in range(2):
                t = mi[step % DEPTH, h, q * 128 : q * 128 + 128, :].T.astype(jnp.float32)
                mt[pl.ds(step * (STK * QS) + h * 2 + q, STK, stride=QS), :] = t[:STK, :]

        @pl.when(step < NX - DEPTH)
        def _():
            fetch(step + DEPTH).start()

        return carry

    lax.fori_loop(0, NX, turn, 0)
    store = lambda n: pltpu.make_async_copy(lhs.at[n % 2], out.at[n], os.at[n % 2])

    def block(n, carry):
        def rows(i, carry):
            for u in range(UNROLL):
                g = g_ref[n * GB + i * UNROLL + u]
                to = pl.ds(pl.multiple_of((i * UNROLL + u) * QS, QS), QS)
                sel[to, :] = mt[pl.ds(pl.multiple_of(g * QS, QS), QS), :]
            return carry

        lax.fori_loop(0, GB // UNROLL, rows, 0)

        @pl.when(n >= 2)
        def _():
            store(n - 2).wait()

        for k in range(QS):
            lhs[n % 2, :, k * 128 : k * 128 + 128] = sel[pl.ds(k, GB, stride=QS), :].astype(jnp.bfloat16)
        store(n).start()
        return carry

    lax.fori_loop(0, G_ROW // GB, block, 0)
    for n in range(2):
        store(G_ROW // GB - 2 + n).wait()


def pick(gvec, m):
    dma = pltpu.SemaphoreType.DMA
    return pl.pallas_call(
        pick_kernel,
        in_specs=[pl.BlockSpec(memory_space=pltpu.SMEM), pl.BlockSpec(memory_space=pl.ANY)],
        out_specs=pl.BlockSpec(memory_space=pl.ANY),
        out_shape=jax.ShapeDtypeStruct((G_ROW // GB, GB, 2 * PAIRS), jnp.bfloat16),
        scratch_shapes=[
            pltpu.VMEM((NX * STK * QS, 128), jnp.float32),
            pltpu.VMEM((DEPTH, 2, PAIRS, LANES), jnp.bfloat16),
            pltpu.VMEM((GB * QS, 128), jnp.float32),
            pltpu.VMEM((2, GB, 2 * PAIRS), jnp.bfloat16),
            dma((DEPTH,)), dma((2,)),
        ],
        compiler_params=pltpu.CompilerParams(vmem_limit_bytes=VMEM_LIMIT),
        name="pick",
    )(gvec, m)


def add_rows(dst, a, b, rows, step=32):
    def one(i, carry):
        at = pl.ds(pl.multiple_of(i * step, step), step)
        dst[at, :] = (a[at, :].astype(jnp.float32) + b[at, :].astype(jnp.float32)).astype(dst.dtype)
        return carry

    lax.fori_loop(0, rows // step, one, 0)


def back_kernel(
    rows, slab, out, sw, ours, theirs, acc, zr2, yr1, zr1, yr2,
    ms, s1, d1, sz2, dz2, sy1, dy1, sz1, dz1, sy2, dy2,
):
    row, col = lax.axis_index("row"), lax.axis_index("col")
    z, yl, core = col // 4, (col // 2) % 2, col % 2
    core_peer = {"row": row, "col": z * 4 + yl * 2 + (1 - core)}
    y_peer = {"row": row, "col": z * 4 + (1 - yl) * 2 + core}
    z_peer = lambda k: {"row": row, "col": ((z + k) % 4) * 4 + yl * 2 + core}
    barrier = pltpu.get_barrier_semaphore()
    for peer in (core_peer, y_peer, z_peer(1), z_peer(2), z_peer(3)):
        pl.semaphore_signal(barrier, inc=1, device_id=peer, device_id_type=MESH)

    def place(n):
        k, s = (n // 2 + 1) % 4, n % 2
        return ((z + k) % 4) * 4 + (yl * s + (1 - yl) * (1 - s)) * 2

    load = lambda n: pltpu.make_async_copy(rows.at[place(n) + core], ours.at[n], ms.at[n])
    for n in range(8):
        load(n).start()
    pl.semaphore_wait(barrier, 5)

    scale = -1.0 / math.sqrt(NV * NC)
    def remote(src, dst, ss, ds, peer):
        return pltpu.make_async_remote_copy(src, dst, ss, ds, device_id=peer, device_id_type=MESH)

    lo, hi = pl.ds(0, LO), pl.ds(LO, HI)
    first = lambda n: remote(rows.at[place(n) + 1 - core], theirs.at[n], s1.at[n], d1.at[n], core_peer)
    for n in range(8):
        first(n).start()
    for h in range(2):
        for r in range(NS // JS):
            sw[h * 2 * PAIRS : (h + 1) * 2 * PAIRS, r * JS : r * JS + JS] = slab[h, r]
    along_z = lambda k, s: remote(
        acc.at[(k + 3) % 4 * 2 + s, hi], zr2.at[(k - 1) * 2 + s], sz2.at[(k - 1) * 2 + s], dz2.at[(k - 1) * 2 + s], z_peer(k)
    )
    along_y = lambda k: remote(acc.at[(k + 3) % 4 * 2, lo], yr1.at[k], sy1.at[k], dy1.at[k], y_peer)
    last_z = lambda k: remote(acc.at[(k + 3) % 4 * 2 + 1, lo], zr1.at[k - 1], sz1.at[k - 1], dz1.at[k - 1], z_peer(k))

    def slot(n, carry):
        k, s = (n // 2 + 1) % 4, n % 2
        load(n).wait()
        first(n).wait_recv()
        lhs = jnp.concatenate([ours[n], theirs[n]], axis=1)
        acc[n] = (jnp.dot(lhs, sw[...], preferred_element_type=jnp.float32) * scale).astype(jnp.bfloat16)

        @pl.when(n < 6)
        def _():
            along_z(k, s).start()

        @pl.when(s == 0)
        def _():
            along_y(k).start()

        return carry

    lax.fori_loop(0, 8, slot, 0)
    for k in (1, 2, 3, 0):
        along_y(k).wait_recv()
        if k:
            at = acc.at[(k + 3) % 4 * 2 + 1]
            add_rows(at, at, yr1.at[k], LO)
            last_z(k).start()
    for k in (1, 2, 3):
        along_z(k, 0).wait_recv()

    def total(i, base, terms):
        at = pl.ds(pl.multiple_of(i * 16, 16), 16)
        value = base[at, :].astype(jnp.float32)
        for ref in terms:
            value = value + ref[at, :].astype(jnp.float32)
        return at, value

    def across(i, carry):
        at, value = total(i, acc.at[6, hi], [zr2.at[0], zr2.at[2], zr2.at[4]])
        yr2[0, at, :] = value.astype(jnp.bfloat16)
        return carry

    lax.fori_loop(0, HI // 16, across, 0)
    last_y = remote(yr2.at[0], yr2.at[1], sy2.at[0], dy2.at[0], y_peer)
    last_y.start()
    for k in (1, 2, 3):
        last_z(k).wait_recv()

    def low(i, carry):
        at, value = total(i, acc.at[7, lo], [yr1.at[0], zr1.at[0], zr1.at[1], zr1.at[2]])
        out[at, :] = value
        return carry

    lax.fori_loop(0, LO // 16, low, 0)
    for k in (1, 2, 3):
        along_z(k, 1).wait_recv()
    last_y.wait_recv()

    def high(i, carry):
        at, value = total(i, acc.at[7, hi], [zr2.at[1], zr2.at[3], zr2.at[5], yr2.at[1]])
        out[pl.ds(pl.multiple_of(LO + i * 16, 16), 16), :] = value
        return carry

    lax.fori_loop(0, HI // 16, high, 0)
    for n in range(8):
        first(n).wait_send()
    for k in range(4):
        along_y(k).wait_send()
        if k:
            last_z(k).wait_send()
            along_z(k, 0).wait_send()
            along_z(k, 1).wait_send()
    last_y.wait_send()


def back(rows, slab):
    dma = pltpu.SemaphoreType.DMA
    vmem = pl.BlockSpec(memory_space=pltpu.VMEM)
    part = lambda n, rows: pltpu.VMEM((n, rows, NS), jnp.bfloat16)
    return pl.pallas_call(
        back_kernel,
        in_specs=[pl.BlockSpec(memory_space=pl.ANY), vmem],
        out_specs=vmem,
        out_shape=jax.ShapeDtypeStruct((G_DEV, NS), jnp.float32),
        scratch_shapes=[
            pltpu.VMEM((4 * PAIRS, NS), jnp.bfloat16),
            pltpu.VMEM((8, GB, 2 * PAIRS), jnp.bfloat16),
            pltpu.VMEM((8, GB, 2 * PAIRS), jnp.bfloat16),
            pltpu.VMEM((8, G_DEV, NS), jnp.bfloat16),
            part(6, HI), part(4, LO), part(3, LO), part(2, HI),
            dma((8,)), dma((8,)), dma((8,)), dma((6,)), dma((6,)), dma((4,)), dma((4,)),
            dma((3,)), dma((3,)), dma((1,)), dma((1,)),
        ],
        compiler_params=pltpu.CompilerParams(
            collective_id=3, has_side_effects=True, vmem_limit_bytes=VMEM_LIMIT
        ),
        name="back",
    )(rows, slab)


def places_kernel(mine, out, send_sem, recv_sem):
    row, col = lax.axis_index("row"), lax.axis_index("col")
    barrier = pltpu.get_barrier_semaphore()
    peers = [{"row": (row + k) % 8, "col": col} for k in range(1, 8)]
    for peer in peers:
        pl.semaphore_signal(barrier, inc=1, device_id=peer, device_id_type=MESH)
    pl.semaphore_wait(barrier, 7)
    copies = []
    for k, peer in enumerate(peers):
        copies.append(
            pltpu.make_async_remote_copy(
                mine, out.at[row], send_sem.at[k], recv_sem.at[k], device_id=peer, device_id_type=MESH
            )
        )
        copies[-1].start()
    out[row] = mine[...]
    for copy in copies:
        copy.wait_recv()
    for copy in copies:
        copy.wait_send()


def places(mine):
    return pl.pallas_call(
        places_kernel,
        in_specs=[pl.BlockSpec(memory_space=pltpu.VMEM)],
        out_specs=pl.BlockSpec(memory_space=pltpu.VMEM),
        out_shape=jax.ShapeDtypeStruct((8, G_ROW // 128, 128), jnp.int32),
        scratch_shapes=[pltpu.SemaphoreType.DMA((7,)), pltpu.SemaphoreType.DMA((7,))],
        compiler_params=pltpu.CompilerParams(collective_id=1, has_side_effects=True),
        name="places",
    )(mine)


def body(psi_val, psi_cond, energy_val, energy_cond, stick_map, gvec_map, slab_index):
    row = lax.axis_index("row")
    fold = lambda psi: (psi[:, :, :HALF], jnp.flip(psi[:, :, HALF:], axis=2))
    cond = jnp.concatenate(fold(psi_cond.transpose(1, 0, 2)), axis=2)
    val = jnp.stack([half.reshape(2, PX // 2, NV, HALF) for half in fold(psi_val.transpose(1, 0, 2))], axis=1)
    val = val.reshape(4, PX // 2, NV, HALF)

    mine = lax.dynamic_slice(stick_map, (row * STK,), (STK,))
    cols = lax.dynamic_slice(slab_index, (row * JS,), (JS,))
    maps = places(gvec_map.reshape(G_ROW // 128, 128)).reshape(-1)
    place = jnp.take(maps, cols)
    col_kx = place // STK
    col_stick = jnp.take(stick_map, cols // G_ROW * STK + place % STK)
    pad = jnp.zeros((LANES - STK,), jnp.int32)
    flat = jnp.concatenate([mine, pad, col_stick])
    ky, kz = flat // NZ, flat % NZ
    tc, ts = half_phase(ky, kz)
    turn = ((ky + kz) % 96).astype(jnp.float32) * (math.pi / 48.0)
    rot = jnp.stack([jnp.cos(turn[:LANES]), jnp.sin(turn[:LANES])])
    dy = jnp.array([0, 0, 0, 1, 0, 1, 1, 1], jnp.int32)
    dx = jnp.array([0, 1, 3, 0, 2, 1, 3, 2], jnp.int32)
    source = (row // 4 + dy) % 2 * 4 + (row % 4 + dx) % 4
    xs = (source[:, None] * PX + jnp.arange(PX, dtype=jnp.int32)[None, :]).reshape(NX)
    theta = (
        ((ky + kz)[None, LANES:] - 2 * (xs[:, None] * col_kx[None, :]) + 96 * NX) % 96
    ).astype(jnp.float32) * (math.pi / 48.0)
    ph = jnp.stack([jnp.cos(theta), jnp.sin(theta)], axis=1)

    weight = jnp.sqrt(2.0 / (energy_cond[None, :] - energy_val[:, None])) * (
        1.0 / (math.sqrt(NY * NZ) * math.sqrt(NX))
    )
    weight = weight.reshape(PAIRS)
    wide = jnp.broadcast_to(weight[:, None], (PAIRS, JS))
    freq = jnp.arange(NX, dtype=jnp.int32)
    ax = (freq[:, None] * xs[None, :] % NX).astype(jnp.float32) * (2.0 * math.pi / NX)
    cx, sx = jnp.cos(ax), jnp.sin(ax)
    table = jnp.concatenate(
        [jnp.concatenate([cx, sx], axis=1), jnp.concatenate([-sx, cx], axis=1)], axis=0
    ).astype(jnp.bfloat16)

    m, slab = front(weight, cond, val, tc, ts, rot, ph, wide, table)
    return back(pick(gvec_map, m.reshape(2, NX, PAIRS, LANES)), slab)


def solution(mesh):
    in_specs = (P(None, "row", None), P("col", "row", None), P(), P("col"), P(), P("row"), P())
    out_specs = P(("row", "col"), None)
    return jax.shard_map(body, mesh=mesh, in_specs=in_specs, out_specs=out_specs, check_vma=False)
```

```python
import math

import jax
import jax.numpy as jnp
from jax import lax
from jax.experimental import pallas as pl
from jax.experimental.pallas import tpu as pltpu
from jax.sharding import PartitionSpec as P

NX = 48
NY = 48
NZ = 48
CELLS = NY * NZ
HALF = CELLS // 2
NC = 256
NV = 16
CL = 16
PAIRS = NV * CL
STK = 192
G_ROW = 5120
NS = 1024
JS = 128
XB = 4
LANES = 256
VMEM_LIMIT = 60 * 1024 * 1024
MESH = pl.DeviceIdType.MESH


def half_phase(ky, kz):
    unit = math.pi / 48.0
    y = 2 * jnp.arange(NY // 2, dtype=jnp.int32) + 1
    z = 2 * jnp.arange(NZ, dtype=jnp.int32) + 1
    ay = ((y[:, None] * ky[None, :]) % 96).astype(jnp.float32) * unit
    az = ((z[:, None] * kz[None, :]) % 96).astype(jnp.float32) * unit
    cy, sy = jnp.cos(ay)[:, None, :], jnp.sin(ay)[:, None, :]
    cz, sz = jnp.cos(az)[None, :, :], jnp.sin(az)[None, :, :]
    cos = (cy * cz - sy * sz).reshape(HALF, -1)
    sin = -(sy * cz + cy * sz).reshape(HALF, -1)
    return cos.astype(jnp.bfloat16), sin.astype(jnp.bfloat16)


BLOCKS = 8
PX = NX // BLOCKS
PT = 3
YS = PAIRS + 8
PB = 16
MS = PB + 8


def density(vf, cbuf, b, plane, at, even, odd):
    cond = cbuf.at[b, plane]
    for v in range(NV):
        out = slice(at * PAIRS + v * CL, at * PAIRS + v * CL + CL)
        spread = lambda h: jnp.broadcast_to(vf[h, plane, v : v + 1, :], (CL, HALF)).astype(jnp.bfloat16)
        lo = spread(0) * cond[:, :HALF]
        hi = spread(1) * cond[:, HALF:]
        even[out, :] = lo + hi
        odd[out, :] = lo - hi


def transform(b, first, even, odd, tc, ts, rot, ph, y, sacc):
    a = jnp.dot(even[...], tc[...], preferred_element_type=jnp.float32)
    c = jnp.dot(odd[...], ts[...], preferred_element_type=jnp.float32)
    cosr, sinr = rot[0:1, :], rot[1:2, :]
    real, imag = sacc[0], sacc[1]
    for i in range(PT):
        x = b * PX + first + i
        rows = slice(i * PAIRS, i * PAIRS + PAIRS)
        am, cm = a[rows, :LANES], c[rows, :LANES]
        to = pl.ds(pl.multiple_of(x * YS, 8), PAIRS)
        for k, value in enumerate((cosr * am - sinr * cm, cosr * cm + sinr * am)):
            for h in range(LANES // 128):
                y[k, h, to, :] = value[:, h * 128 : h * 128 + 128]
        av, cv = a[rows, LANES:], c[rows, LANES:]
        cp, sp = ph[x, 0:1, :], ph[x, 1:2, :]
        real = real + (cp * av - sp * cv)
        imag = imag + (cp * cv + sp * av)
    sacc[0] = real
    sacc[1] = imag


def front_kernel(
    weights, cond, val, tc, ts, rot, ph, wide, table, m_out, slab_out,
    cbuf, vbuf, vf, even, odd, y, sacc, sl, mo, mb,
    lsem, cs, cr, vs, vr, gs, gr, ss, sr, fs, fr, ms,
):
    row, col = lax.axis_index("row"), lax.axis_index("col")
    yh, x = row // 4, row % 4
    z, yl, core = col // 4, (col // 2) % 2, col % 2
    zo = z + 1 - 2 * (z % 2)
    xp = {"row": yh * 4 + (x + 1) % 4, "col": col}
    xm = {"row": yh * 4 + (x + 3) % 4, "col": col}
    yc = {"row": (1 - yh) * 4 + x, "col": col}
    yv = {"row": (1 - yh) * 4 + x, "col": z * 4 + (1 - yl) * 2 + core}
    group = [
        {"row": row, "col": zo * 4 + yl * 2 + core},
        {"row": row, "col": z * 4 + yl * 2 + 1 - core},
        {"row": row, "col": zo * 4 + yl * 2 + 1 - core},
    ]
    across = [{"row": (row + k) % 8, "col": col} for k in range(1, 8)]
    part = core * 2 + z % 2

    own = [
        pltpu.make_async_copy(cond, cbuf.at[0], lsem.at[0]),
        pltpu.make_async_copy(val, vbuf.at[0], lsem.at[1]),
    ]
    for copy in own:
        copy.start()
    barrier = pltpu.get_barrier_semaphore()
    for peer in across + group + [yv]:
        pl.semaphore_signal(barrier, inc=1, device_id=peer, device_id_type=MESH)
    pl.semaphore_wait(barrier, 11)

    hops = [(0, 3, None), (0, 2, xp), (0, 1, xm), (3, 6, xp), (3, 5, xm), (2, 4, xp), (5, 7, xm)]
    hop_to = [hop[1] for hop in hops]

    def cond_hop(n):
        src, dst, peer = hops[n]
        return pltpu.make_async_remote_copy(
            cbuf.at[src] if src else cond, cbuf.at[dst], cs.at[n], cr.at[dst],
            device_id=peer or yc, device_id_type=MESH,
        )

    def val_hop(n):
        src, dst, peer = hops[n]
        return pltpu.make_async_remote_copy(
            vbuf.at[src, part] if src else val.at[part], vbuf.at[dst, part], vs.at[n], vr.at[dst],
            device_id=peer or yv, device_id_type=MESH,
        )

    def spread(b, j):
        return pltpu.make_async_remote_copy(
            vbuf.at[b, part], vbuf.at[b, part], gs.at[b * 3 + j], gr.at[b * 3 + j],
            device_id=group[j], device_id_type=MESH,
        )

    def land_val(b, *forward):
        val_hop(hop_to.index(b)).wait_recv()
        for n in forward:
            val_hop(n).start()
        for j in range(3):
            spread(b, j).start()

    def land(b, *forward):
        cond_hop(hop_to.index(b)).wait_recv()
        for n in forward:
            cond_hop(n).start()

    def ready(b):
        for j in range(3):
            spread(b, j).wait_recv()

    for n in range(3):
        val_hop(n).start()
    for n in range(3):
        cond_hop(n).start()
    sacc[...] = jnp.zeros_like(sacc)
    for copy in own:
        copy.wait()

    def block(b, carry):
        @pl.when(b == 1)
        def _():
            land_val(1)
            land_val(2, 5)
            land_val(3, 3, 4)
            land(2, 5)
            land(1)
            land(3, 3, 4)
            ready(1)

        @pl.when(b == 2)
        def _():
            land_val(4)
            land_val(5, 6)
            land_val(6)
            ready(2)

        @pl.when(b == 3)
        def _():
            land_val(7)
            ready(3)

        @pl.when(b == 4)
        def _():
            land(4)
            land(5, 6)
            ready(4)

        @pl.when(b == 5)
        def _():
            land(6)
            ready(5)

        @pl.when(b == 6)
        def _():
            ready(6)

        @pl.when(b == 7)
        def _():
            land(7)
            ready(7)

        def widen(j, carry):
            for q in range(4):
                vf[q % 2, (q // 2) * 3 + j] = vbuf[b, q, j].astype(jnp.float32)
            return carry

        lax.fori_loop(0, 3, widen, 0)

        def some(i, carry):
            for u in range(PT):
                density(vf, cbuf, b, i * PT + u, u, even, odd)
            transform(b, i * PT, even, odd, tc, ts, rot, ph, y, sacc)
            return carry

        lax.fori_loop(0, PX // PT, some, 0)
        return carry

    lax.fori_loop(0, BLOCKS, block, 0)

    for h in range(2):
        sl[h * PAIRS : h * PAIRS + PAIRS, :] = (sacc[h] * wide[...]).astype(jnp.bfloat16)
    keep = pltpu.make_async_copy(sl, slab_out.at[0, row], lsem.at[2])
    keep.start()

    def push(k):
        return pltpu.make_async_remote_copy(
            sl, slab_out.at[0, row], ss.at[k], sr.at[k], device_id=across[k], device_id_type=MESH
        )

    def hand(k):
        at = (row + 7 - k) % 8
        return pltpu.make_async_remote_copy(
            sl if k == 7 else slab_out.at[0, at], slab_out.at[1, at], fs.at[k], fr.at[k],
            device_id=group[1], device_id_type=MESH,
        )

    for k in range(7):
        push(k).start()
    hand(7).start()

    def chunk(i, carry):
        for k in range(7):

            @pl.when(i == 5 + k)
            def _():
                push(k).wait_recv()
                hand(k).start()

        slot = i % 2
        ps = pl.ds(pl.multiple_of(i * PB, PB), PB)
        out = pltpu.make_async_copy(mb.at[slot], m_out.at[:, ps, :], ms.at[slot])
        for p in range(PB):
            at = pl.ds(i * PB + p, NX, stride=YS)
            rhs = jnp.concatenate(
                [jnp.concatenate([y[k, 0, at, :], y[k, 1, at, :]], axis=1) for k in range(2)], axis=0
            ).astype(jnp.bfloat16)
            res = jnp.dot(table[...], rhs, preferred_element_type=jnp.float32) * weights[i * PB + p]
            for h in range(LANES // 128):
                mo[h, pl.ds(p, 2 * NX, stride=MS), :] = res[:, h * 128 : h * 128 + 128]

        @pl.when(i >= 2)
        def _():
            out.wait()

        for h in range(LANES // 128):
            lanes = slice(h * 128, h * 128 + 128)
            mb[slot, :, :, lanes] = mo[h].reshape(2 * NX, MS, 128)[:, :PB].astype(jnp.bfloat16)
        out.start()
        return carry

    lax.fori_loop(0, PAIRS // PB, chunk, 0)
    for slot in range(2):
        pltpu.make_async_copy(mb.at[slot], m_out.at[:, pl.ds(slot * PB, PB), :], ms.at[slot]).wait()
    keep.wait()
    for k in range(8):
        hand(k).wait_recv()
        hand(k).wait_send()
    for k in range(7):
        push(k).wait_send()
    for n in range(len(hops)):
        val_hop(n).wait_send()
        cond_hop(n).wait_send()
    for b in range(1, BLOCKS):
        for j in range(3):
            spread(b, j).wait_send()


def front(weights, cond, val, tc, ts, rot, ph, wide, table):
    dma = pltpu.SemaphoreType.DMA
    vmem = pl.BlockSpec(memory_space=pltpu.VMEM)
    hbm = pl.BlockSpec(memory_space=pl.ANY)
    bf = lambda *shape: pltpu.VMEM(shape, jnp.bfloat16)
    fl = lambda *shape: pltpu.VMEM(shape, jnp.float32)
    return pl.pallas_call(
        front_kernel,
        in_specs=[pl.BlockSpec(memory_space=pltpu.SMEM)] + [vmem] * 8,
        out_specs=[hbm, hbm],
        out_shape=[
            jax.ShapeDtypeStruct((2 * NX, PAIRS, LANES), jnp.bfloat16),
            jax.ShapeDtypeStruct((2, BLOCKS, 2 * PAIRS, JS), jnp.bfloat16),
        ],
        scratch_shapes=[
            bf(BLOCKS, PX, CL, CELLS),
            bf(BLOCKS, 4, PX // 2, NV, HALF),
            fl(2, PX, NV, HALF),
            bf(PT * PAIRS, HALF),
            bf(PT * PAIRS, HALF),
            fl(2, LANES // 128, NX * YS, 128),
            fl(2, PAIRS, JS),
            bf(2 * PAIRS, JS),
            fl(2, 2 * NX * MS, 128),
            bf(2, 2 * NX, PB, LANES),
            dma((3,)), dma((7,)), dma((8,)), dma((7,)), dma((8,)),
            dma((24,)), dma((24,)), dma((7,)), dma((7,)), dma((8,)), dma((8,)), dma((2,)),
        ],
        compiler_params=pltpu.CompilerParams(
            collective_id=2, has_side_effects=True, vmem_limit_bytes=VMEM_LIMIT
        ),
        name="front",
    )(weights, cond, val, tc, ts, rot, ph, wide, table)


GB = 320
QS = 2 * PAIRS // 128
G_DEV = 320
LO = 192
HI = G_DEV - LO
DEPTH = 16
UNROLL = 32


def pick_kernel(g_ref, m, out, mt, mi, sel, lhs, ms, os):
    def fetch(step):
        slot = step % DEPTH
        return pltpu.make_async_copy(m.at[:, step], mi.at[slot], ms.at[slot])

    for step in range(DEPTH):
        fetch(step).start()

    def turn(step, carry):
        fetch(step).wait()
        for h in range(2):
            for q in range(2):
                t = mi[step % DEPTH, h, q * 128 : q * 128 + 128, :].T.astype(jnp.float32)
                mt[pl.ds(step * (STK * QS) + h * 2 + q, STK, stride=QS), :] = t[:STK, :]

        @pl.when(step < NX - DEPTH)
        def _():
            fetch(step + DEPTH).start()

        return carry

    lax.fori_loop(0, NX, turn, 0, unroll=4)
    store = lambda n: pltpu.make_async_copy(lhs.at[n % 2], out.at[n], os.at[n % 2])

    def block(n, carry):
        def rows(i, carry):
            for u in range(UNROLL):
                g = g_ref[n * GB + i * UNROLL + u]
                to = pl.ds(pl.multiple_of((i * UNROLL + u) * QS, QS), QS)
                sel[to, :] = mt[pl.ds(pl.multiple_of(g * QS, QS), QS), :]
            return carry

        lax.fori_loop(0, GB // UNROLL, rows, 0)

        @pl.when(n >= 2)
        def _():
            store(n - 2).wait()

        for k in range(QS):
            lhs[n % 2, :, k * 128 : k * 128 + 128] = sel[pl.ds(k, GB, stride=QS), :].astype(jnp.bfloat16)
        store(n).start()
        return carry

    lax.fori_loop(0, G_ROW // GB, block, 0)
    for n in range(2):
        store(G_ROW // GB - 2 + n).wait()


def pick(gvec, m):
    dma = pltpu.SemaphoreType.DMA
    return pl.pallas_call(
        pick_kernel,
        in_specs=[pl.BlockSpec(memory_space=pltpu.SMEM), pl.BlockSpec(memory_space=pl.ANY)],
        out_specs=pl.BlockSpec(memory_space=pl.ANY),
        out_shape=jax.ShapeDtypeStruct((G_ROW // GB, GB, 2 * PAIRS), jnp.bfloat16),
        scratch_shapes=[
            pltpu.VMEM((NX * STK * QS, 128), jnp.float32),
            pltpu.VMEM((DEPTH, 2, PAIRS, LANES), jnp.bfloat16),
            pltpu.VMEM((GB * QS, 128), jnp.float32),
            pltpu.VMEM((2, GB, 2 * PAIRS), jnp.bfloat16),
            dma((DEPTH,)), dma((2,)),
        ],
        compiler_params=pltpu.CompilerParams(vmem_limit_bytes=VMEM_LIMIT),
        name="pick",
    )(gvec, m)


def add_rows(dst, a, b, rows, step=32):
    def one(i, carry):
        at = pl.ds(pl.multiple_of(i * step, step), step)
        dst[at, :] = (a[at, :].astype(jnp.float32) + b[at, :].astype(jnp.float32)).astype(dst.dtype)
        return carry

    lax.fori_loop(0, rows // step, one, 0)


def back_kernel(
    rows, slab, out, sw, ours, theirs, acc, zr2, yr1, zr1, yr2,
    ms, s1, d1, sz2, dz2, sy1, dy1, sz1, dz1, sy2, dy2,
):
    row, col = lax.axis_index("row"), lax.axis_index("col")
    z, yl, core = col // 4, (col // 2) % 2, col % 2
    core_peer = {"row": row, "col": z * 4 + yl * 2 + (1 - core)}
    y_peer = {"row": row, "col": z * 4 + (1 - yl) * 2 + core}
    z_peer = lambda k: {"row": row, "col": ((z + k) % 4) * 4 + yl * 2 + core}
    barrier = pltpu.get_barrier_semaphore()
    for peer in (core_peer, y_peer, z_peer(1), z_peer(2), z_peer(3)):
        pl.semaphore_signal(barrier, inc=1, device_id=peer, device_id_type=MESH)

    def place(n):
        k, s = (n // 2 + 1) % 4, n % 2
        return ((z + k) % 4) * 4 + (yl * s + (1 - yl) * (1 - s)) * 2

    load = lambda n: pltpu.make_async_copy(rows.at[place(n) + core], ours.at[n], ms.at[n])
    for n in range(8):
        load(n).start()
    pl.semaphore_wait(barrier, 5)

    scale = -1.0 / math.sqrt(NV * NC)
    def remote(src, dst, ss, ds, peer):
        return pltpu.make_async_remote_copy(src, dst, ss, ds, device_id=peer, device_id_type=MESH)

    lo, hi = pl.ds(0, LO), pl.ds(LO, HI)
    first = lambda n: remote(rows.at[place(n) + 1 - core], theirs.at[n], s1.at[n], d1.at[n], core_peer)
    for n in range(8):
        first(n).start()
    for h in range(2):
        for r in range(NS // JS):
            sw[h * 2 * PAIRS : (h + 1) * 2 * PAIRS, r * JS : r * JS + JS] = slab[h, r]
    along_z = lambda k, s: remote(
        acc.at[(k + 3) % 4 * 2 + s, hi], zr2.at[(k - 1) * 2 + s], sz2.at[(k - 1) * 2 + s], dz2.at[(k - 1) * 2 + s], z_peer(k)
    )
    along_y = lambda k: remote(acc.at[(k + 3) % 4 * 2, lo], yr1.at[k], sy1.at[k], dy1.at[k], y_peer)
    last_z = lambda k: remote(acc.at[(k + 3) % 4 * 2 + 1, lo], zr1.at[k - 1], sz1.at[k - 1], dz1.at[k - 1], z_peer(k))

    def slot(n, carry):
        k, s = (n // 2 + 1) % 4, n % 2
        load(n).wait()
        first(n).wait_recv()
        lhs = jnp.concatenate([ours[n], theirs[n]], axis=1)
        acc[n] = (jnp.dot(lhs, sw[...], preferred_element_type=jnp.float32) * scale).astype(jnp.bfloat16)

        @pl.when(n < 6)
        def _():
            along_z(k, s).start()

        @pl.when(s == 0)
        def _():
            along_y(k).start()

        return carry

    lax.fori_loop(0, 8, slot, 0)
    for k in (1, 2, 3, 0):
        along_y(k).wait_recv()
        if k:
            at = acc.at[(k + 3) % 4 * 2 + 1]
            add_rows(at, at, yr1.at[k], LO)
            last_z(k).start()
    for k in (1, 2, 3):
        along_z(k, 0).wait_recv()

    def total(i, base, terms):
        at = pl.ds(pl.multiple_of(i * 16, 16), 16)
        value = base[at, :].astype(jnp.float32)
        for ref in terms:
            value = value + ref[at, :].astype(jnp.float32)
        return at, value

    def across(i, carry):
        at, value = total(i, acc.at[6, hi], [zr2.at[0], zr2.at[2], zr2.at[4]])
        yr2[0, at, :] = value.astype(jnp.bfloat16)
        return carry

    lax.fori_loop(0, HI // 16, across, 0)
    last_y = remote(yr2.at[0], yr2.at[1], sy2.at[0], dy2.at[0], y_peer)
    last_y.start()
    for k in (1, 2, 3):
        last_z(k).wait_recv()

    def low(i, carry):
        at, value = total(i, acc.at[7, lo], [yr1.at[0], zr1.at[0], zr1.at[1], zr1.at[2]])
        out[at, :] = value
        return carry

    lax.fori_loop(0, LO // 16, low, 0)
    for k in (1, 2, 3):
        along_z(k, 1).wait_recv()
    last_y.wait_recv()

    def high(i, carry):
        at, value = total(i, acc.at[7, hi], [zr2.at[1], zr2.at[3], zr2.at[5], yr2.at[1]])
        out[pl.ds(pl.multiple_of(LO + i * 16, 16), 16), :] = value
        return carry

    lax.fori_loop(0, HI // 16, high, 0)
    for n in range(8):
        first(n).wait_send()
    for k in range(4):
        along_y(k).wait_send()
        if k:
            last_z(k).wait_send()
            along_z(k, 0).wait_send()
            along_z(k, 1).wait_send()
    last_y.wait_send()


def back(rows, slab):
    dma = pltpu.SemaphoreType.DMA
    vmem = pl.BlockSpec(memory_space=pltpu.VMEM)
    part = lambda n, rows: pltpu.VMEM((n, rows, NS), jnp.bfloat16)
    return pl.pallas_call(
        back_kernel,
        in_specs=[pl.BlockSpec(memory_space=pl.ANY), vmem],
        out_specs=vmem,
        out_shape=jax.ShapeDtypeStruct((G_DEV, NS), jnp.float32),
        scratch_shapes=[
            pltpu.VMEM((4 * PAIRS, NS), jnp.bfloat16),
            pltpu.VMEM((8, GB, 2 * PAIRS), jnp.bfloat16),
            pltpu.VMEM((8, GB, 2 * PAIRS), jnp.bfloat16),
            pltpu.VMEM((8, G_DEV, NS), jnp.bfloat16),
            part(6, HI), part(4, LO), part(3, LO), part(2, HI),
            dma((8,)), dma((8,)), dma((8,)), dma((6,)), dma((6,)), dma((4,)), dma((4,)),
            dma((3,)), dma((3,)), dma((1,)), dma((1,)),
        ],
        compiler_params=pltpu.CompilerParams(
            collective_id=3, has_side_effects=True, vmem_limit_bytes=VMEM_LIMIT
        ),
        name="back",
    )(rows, slab)


def places_kernel(mine, cond, val, out, cond_out, val_out, send_sem, recv_sem):
    row, col = lax.axis_index("row"), lax.axis_index("col")
    barrier = pltpu.get_barrier_semaphore()
    peers = [{"row": (row + k) % 8, "col": col} for k in range(1, 8)]
    for peer in peers:
        pl.semaphore_signal(barrier, inc=1, device_id=peer, device_id_type=MESH)
    pl.semaphore_wait(barrier, 7)
    copies = []
    for k, peer in enumerate(peers):
        copies.append(
            pltpu.make_async_remote_copy(
                mine, out.at[row], send_sem.at[k], recv_sem.at[k], device_id=peer, device_id_type=MESH
            )
        )
        copies[-1].start()
    out[row] = mine[...]
    r = lax.broadcasted_iota(jnp.int32, (128, 128), 0)
    c = lax.broadcasted_iota(jnp.int32, (128, 128), 1)
    back = (r + c == 127).astype(jnp.bfloat16)
    half = PX // 2
    cond_out[:, :, :HALF] = cond[:, :, :HALF]
    for p in range(2):
        val_out[2 * p] = val[p * half : p * half + half, :, :HALF]
    for b in range(HALF // 128):
        source = slice(CELLS - b * 128 - 128, CELLS - b * 128)
        to = slice(b * 128, b * 128 + 128)
        flip = lambda ref: jnp.dot(
            ref[:, :, source].reshape(PX * CL, 128), back, preferred_element_type=jnp.float32
        ).astype(jnp.bfloat16).reshape(PX, CL, 128)
        cond_out[:, :, HALF + b * 128 : HALF + b * 128 + 128] = flip(cond)
        turned = flip(val)
        for p in range(2):
            val_out[2 * p + 1, :, :, to] = turned[p * half : p * half + half]
    for copy in copies:
        copy.wait_recv()
    for copy in copies:
        copy.wait_send()


def places(mine, cond, val):
    return pl.pallas_call(
        places_kernel,
        in_specs=[pl.BlockSpec(memory_space=pltpu.VMEM)] * 3,
        out_specs=[pl.BlockSpec(memory_space=pltpu.VMEM)] * 3,
        out_shape=[
            jax.ShapeDtypeStruct((8, G_ROW // 128, 128), jnp.int32),
            jax.ShapeDtypeStruct((PX, CL, CELLS), jnp.bfloat16),
            jax.ShapeDtypeStruct((4, PX // 2, NV, HALF), jnp.bfloat16),
        ],
        scratch_shapes=[pltpu.SemaphoreType.DMA((7,)), pltpu.SemaphoreType.DMA((7,))],
        compiler_params=pltpu.CompilerParams(collective_id=1, has_side_effects=True),
        name="places",
    )(mine, cond, val)


def body(psi_val, psi_cond, energy_val, energy_cond, stick_map, gvec_map, slab_index):
    row = lax.axis_index("row")
    mine = lax.dynamic_slice(stick_map, (row * STK,), (STK,))
    cols = lax.dynamic_slice(slab_index, (row * JS,), (JS,))
    maps, cond, val = places(
        gvec_map.reshape(G_ROW // 128, 128), psi_cond.transpose(1, 0, 2), psi_val.transpose(1, 0, 2)
    )
    maps = maps.reshape(-1)
    place = jnp.take(maps, cols)
    col_kx = place // STK
    col_stick = jnp.take(stick_map, cols // G_ROW * STK + place % STK)
    pad = jnp.zeros((LANES - STK,), jnp.int32)
    flat = jnp.concatenate([mine, pad, col_stick])
    ky, kz = flat // NZ, flat % NZ
    tc, ts = half_phase(ky, kz)
    turn = ((ky + kz) % 96).astype(jnp.float32) * (math.pi / 48.0)
    rot = jnp.stack([jnp.cos(turn[:LANES]), jnp.sin(turn[:LANES])])
    dy = jnp.array([0, 0, 0, 1, 0, 1, 1, 1], jnp.int32)
    dx = jnp.array([0, 1, 3, 0, 2, 1, 3, 2], jnp.int32)
    source = (row // 4 + dy) % 2 * 4 + (row % 4 + dx) % 4
    xs = (source[:, None] * PX + jnp.arange(PX, dtype=jnp.int32)[None, :]).reshape(NX)
    theta = (
        ((ky + kz)[None, LANES:] - 2 * (xs[:, None] * col_kx[None, :]) + 96 * NX) % 96
    ).astype(jnp.float32) * (math.pi / 48.0)
    ph = jnp.stack([jnp.cos(theta), jnp.sin(theta)], axis=1)

    weight = jnp.sqrt(2.0 / (energy_cond[None, :] - energy_val[:, None])) * (
        1.0 / (math.sqrt(NY * NZ) * math.sqrt(NX))
    )
    weight = weight.reshape(PAIRS)
    wide = jnp.broadcast_to(weight[:, None], (PAIRS, JS))
    freq = jnp.arange(NX, dtype=jnp.int32)
    ax = (freq[:, None] * xs[None, :] % NX).astype(jnp.float32) * (2.0 * math.pi / NX)
    cx, sx = jnp.cos(ax), jnp.sin(ax)
    table = jnp.concatenate(
        [jnp.concatenate([cx, sx], axis=1), jnp.concatenate([-sx, cx], axis=1)], axis=0
    ).astype(jnp.bfloat16)

    m, slab = front(weight, cond, val, tc, ts, rot, ph, wide, table)
    return back(pick(gvec_map, m.reshape(2, NX, PAIRS, LANES)), slab)


def solution(mesh):
    in_specs = (P(None, "row", None), P("col", "row", None), P(), P("col"), P(), P("row"), P())
    out_specs = P(("row", "col"), None)
    return jax.shard_map(body, mesh=mesh, in_specs=in_specs, out_specs=out_specs, check_vma=False)
```

```python
import math

import jax
import jax.numpy as jnp
from jax import lax
from jax.experimental import pallas as pl
from jax.experimental.pallas import tpu as pltpu
from jax.sharding import PartitionSpec as P

NX = 48
NY = 48
NZ = 48
CELLS = NY * NZ
HALF = CELLS // 2
NC = 256
NV = 16
CL = 16
PAIRS = NV * CL
STK = 192
G_ROW = 5120
NS = 1024
JS = 128
XB = 4
LANES = 256
VMEM_LIMIT = 60 * 1024 * 1024
MESH = pl.DeviceIdType.MESH


def turn_angle(t):
    return (t - 96.0 * jnp.floor((t + 0.5) * (1.0 / 96.0))) * (math.pi / 48.0)


def make_tables(ks, rows_of_blocks, tc, ts, rot, ph):
    width = LANES + JS
    ky, kz = ks[0:1, :], ks[1:2, :]
    odd = lambda n: 2.0 * lax.broadcasted_iota(jnp.int32, (n, width), 0).astype(jnp.float32) + 1.0
    ay, az = turn_angle(odd(NY // 2) * ky), turn_angle(odd(NZ) * kz)
    cy, sy, cz, sz = jnp.cos(ay), jnp.sin(ay), jnp.cos(az), jnp.sin(az)
    for y in range(NY // 2):
        to = slice(y * NZ, y * NZ + NZ)
        tc[to, :] = (cy[y : y + 1, :] * cz - sy[y : y + 1, :] * sz).astype(jnp.bfloat16)
        ts[to, :] = -(sy[y : y + 1, :] * cz + cy[y : y + 1, :] * sz).astype(jnp.bfloat16)
    shift = turn_angle(ky + kz)
    rot[0:1, :] = jnp.cos(shift[:, :LANES])
    rot[1:2, :] = jnp.sin(shift[:, :LANES])
    plane = lax.broadcasted_iota(jnp.int32, (NX, JS), 0)
    xs = plane
    for b, block_row in enumerate(rows_of_blocks):
        inside = (plane >= b * PX) & (plane < b * PX + PX)
        xs = jnp.where(inside, plane + (block_row - b) * PX, xs)
    theta = turn_angle((ky + kz)[:, LANES:] - 2.0 * xs.astype(jnp.float32) * ks[2:3, LANES:])
    ph[0] = jnp.cos(theta)
    ph[1] = jnp.sin(theta)


BLOCKS = 8
PX = NX // BLOCKS
PT = 3
YS = PAIRS + 8
PB = 16
MS = PB + 8


def density(vf, cbuf, b, plane, at, even, odd):
    cond = cbuf.at[b, plane]
    for v in range(NV):
        out = slice(at * PAIRS + v * CL, at * PAIRS + v * CL + CL)
        spread = lambda h: jnp.broadcast_to(vf[h, plane, v : v + 1, :], (CL, HALF)).astype(jnp.bfloat16)
        lo = spread(0) * cond[:, :HALF]
        hi = spread(1) * cond[:, HALF:]
        even[out, :] = lo + hi
        odd[out, :] = lo - hi


def transform(b, first, even, odd, tc, ts, rot, ph, y, sacc):
    a = jnp.dot(even[...], tc[...], preferred_element_type=jnp.float32)
    c = jnp.dot(odd[...], ts[...], preferred_element_type=jnp.float32)
    cosr, sinr = rot[0:1, :], rot[1:2, :]
    real, imag = sacc[0], sacc[1]
    for i in range(PT):
        x = b * PX + first + i
        rows = slice(i * PAIRS, i * PAIRS + PAIRS)
        am, cm = a[rows, :LANES], c[rows, :LANES]
        to = pl.ds(pl.multiple_of(x * YS, 8), PAIRS)
        for k, value in enumerate((cosr * am - sinr * cm, cosr * cm + sinr * am)):
            for h in range(LANES // 128):
                y[k, h, to, :] = value[:, h * 128 : h * 128 + 128]
        av, cv = a[rows, LANES:], c[rows, LANES:]
        cp, sp = ph[0, pl.ds(x, 1), :], ph[1, pl.ds(x, 1), :]
        real = real + (cp * av - sp * cv)
        imag = imag + (cp * cv + sp * av)
    sacc[0] = real
    sacc[1] = imag


def front_kernel(
    weights, cond, val, ks, wide, table, m_out, slab_out,
    tc, ts, rot, ph, cbuf, vbuf, vf, even, odd, y, sacc, sl, mo, mb,
    lsem, cs, cr, vs, vr, gs, gr, ss, sr, fs, fr, ms,
):
    row, col = lax.axis_index("row"), lax.axis_index("col")
    yh, x = row // 4, row % 4
    z, yl, core = col // 4, (col // 2) % 2, col % 2
    zo = z + 1 - 2 * (z % 2)
    xp = {"row": yh * 4 + (x + 1) % 4, "col": col}
    xm = {"row": yh * 4 + (x + 3) % 4, "col": col}
    yc = {"row": (1 - yh) * 4 + x, "col": col}
    yv = {"row": (1 - yh) * 4 + x, "col": z * 4 + (1 - yl) * 2 + core}
    group = [
        {"row": row, "col": zo * 4 + yl * 2 + core},
        {"row": row, "col": z * 4 + yl * 2 + 1 - core},
        {"row": row, "col": zo * 4 + yl * 2 + 1 - core},
    ]
    across = [{"row": (row + k) % 8, "col": col} for k in range(1, 8)]
    part = core * 2 + z % 2

    own = [
        pltpu.make_async_copy(cond, cbuf.at[0], lsem.at[0]),
        pltpu.make_async_copy(val, vbuf.at[0], lsem.at[1]),
    ]
    for copy in own:
        copy.start()
    barrier = pltpu.get_barrier_semaphore()
    for peer in across + group + [yv]:
        pl.semaphore_signal(barrier, inc=1, device_id=peer, device_id_type=MESH)
    pl.semaphore_wait(barrier, 11)

    hops = [(0, 3, None), (0, 2, xp), (0, 1, xm), (3, 6, xp), (3, 5, xm), (2, 4, xp), (5, 7, xm)]
    hop_to = [hop[1] for hop in hops]

    def cond_hop(n):
        src, dst, peer = hops[n]
        return pltpu.make_async_remote_copy(
            cbuf.at[src] if src else cond, cbuf.at[dst], cs.at[n], cr.at[dst],
            device_id=peer or yc, device_id_type=MESH,
        )

    def val_hop(n):
        src, dst, peer = hops[n]
        return pltpu.make_async_remote_copy(
            vbuf.at[src, part] if src else val.at[part], vbuf.at[dst, part], vs.at[n], vr.at[dst],
            device_id=peer or yv, device_id_type=MESH,
        )

    def spread(b, j):
        return pltpu.make_async_remote_copy(
            vbuf.at[b, part], vbuf.at[b, part], gs.at[b * 3 + j], gr.at[b * 3 + j],
            device_id=group[j], device_id_type=MESH,
        )

    def land_val(b, *forward):
        val_hop(hop_to.index(b)).wait_recv()
        for n in forward:
            val_hop(n).start()
        for j in range(3):
            spread(b, j).start()

    def land(b, *forward):
        cond_hop(hop_to.index(b)).wait_recv()
        for n in forward:
            cond_hop(n).start()

    def ready(b):
        for j in range(3):
            spread(b, j).wait_recv()

    for n in range(3):
        val_hop(n).start()
    for n in range(3):
        cond_hop(n).start()
    sacc[...] = jnp.zeros_like(sacc)
    steps = [(0, 0), (0, 1), (0, 3), (1, 0), (0, 2), (1, 1), (1, 3), (1, 2)]
    make_tables(ks, [(yh + dy) % 2 * 4 + (x + dx) % 4 for dy, dx in steps], tc, ts, rot, ph)
    for copy in own:
        copy.wait()

    def block(b, carry):
        @pl.when(b == 1)
        def _():
            land_val(1)
            land_val(2, 5)
            land_val(3, 3, 4)
            land(2, 5)
            land(1)
            land(3, 3, 4)
            ready(1)

        @pl.when(b == 2)
        def _():
            land_val(4)
            land_val(5, 6)
            land_val(6)
            ready(2)

        @pl.when(b == 3)
        def _():
            land_val(7)
            ready(3)

        @pl.when(b == 4)
        def _():
            land(4)
            land(5, 6)
            ready(4)

        @pl.when(b == 5)
        def _():
            land(6)
            ready(5)

        @pl.when(b == 6)
        def _():
            ready(6)

        @pl.when(b == 7)
        def _():
            land(7)
            ready(7)

        def widen(j, carry):
            for q in range(4):
                vf[q % 2, (q // 2) * 3 + j] = vbuf[b, q, j].astype(jnp.float32)
            return carry

        lax.fori_loop(0, 3, widen, 0)

        def some(i, carry):
            for u in range(PT):
                density(vf, cbuf, b, i * PT + u, u, even, odd)
            transform(b, i * PT, even, odd, tc, ts, rot, ph, y, sacc)
            return carry

        lax.fori_loop(0, PX // PT, some, 0)
        return carry

    lax.fori_loop(0, BLOCKS, block, 0)

    for h in range(2):
        sl[h * PAIRS : h * PAIRS + PAIRS, :] = (sacc[h] * wide[...]).astype(jnp.bfloat16)
    keep = pltpu.make_async_copy(sl, slab_out.at[0, row], lsem.at[2])
    keep.start()

    def push(k):
        return pltpu.make_async_remote_copy(
            sl, slab_out.at[0, row], ss.at[k], sr.at[k], device_id=across[k], device_id_type=MESH
        )

    def hand(k):
        at = (row + 7 - k) % 8
        return pltpu.make_async_remote_copy(
            sl if k == 7 else slab_out.at[0, at], slab_out.at[1, at], fs.at[k], fr.at[k],
            device_id=group[1], device_id_type=MESH,
        )

    for k in range(7):
        push(k).start()
    hand(7).start()

    def chunk(i, carry):
        for k in range(7):

            @pl.when(i == 5 + k)
            def _():
                push(k).wait_recv()
                hand(k).start()

        slot = i % 2
        ps = pl.ds(pl.multiple_of(i * PB, PB), PB)
        out = pltpu.make_async_copy(mb.at[slot], m_out.at[:, ps, :], ms.at[slot])
        for p in range(PB):
            at = pl.ds(i * PB + p, NX, stride=YS)
            rhs = jnp.concatenate(
                [jnp.concatenate([y[k, 0, at, :], y[k, 1, at, :]], axis=1) for k in range(2)], axis=0
            ).astype(jnp.bfloat16)
            res = jnp.dot(table[...], rhs, preferred_element_type=jnp.float32) * weights[i * PB + p]
            for h in range(LANES // 128):
                mo[h, pl.ds(p, 2 * NX, stride=MS), :] = res[:, h * 128 : h * 128 + 128]

        @pl.when(i >= 2)
        def _():
            out.wait()

        for h in range(LANES // 128):
            lanes = slice(h * 128, h * 128 + 128)
            mb[slot, :, :, lanes] = mo[h].reshape(2 * NX, MS, 128)[:, :PB].astype(jnp.bfloat16)
        out.start()
        return carry

    lax.fori_loop(0, PAIRS // PB, chunk, 0)
    for slot in range(2):
        pltpu.make_async_copy(mb.at[slot], m_out.at[:, pl.ds(slot * PB, PB), :], ms.at[slot]).wait()
    keep.wait()
    for k in range(8):
        hand(k).wait_recv()
        hand(k).wait_send()
    for k in range(7):
        push(k).wait_send()
    for n in range(len(hops)):
        val_hop(n).wait_send()
        cond_hop(n).wait_send()
    for b in range(1, BLOCKS):
        for j in range(3):
            spread(b, j).wait_send()


def front(weights, cond, val, ks, wide, table):
    dma = pltpu.SemaphoreType.DMA
    vmem = pl.BlockSpec(memory_space=pltpu.VMEM)
    hbm = pl.BlockSpec(memory_space=pl.ANY)
    bf = lambda *shape: pltpu.VMEM(shape, jnp.bfloat16)
    fl = lambda *shape: pltpu.VMEM(shape, jnp.float32)
    return pl.pallas_call(
        front_kernel,
        in_specs=[pl.BlockSpec(memory_space=pltpu.SMEM)] + [vmem] * 5,
        out_specs=[hbm, hbm],
        out_shape=[
            jax.ShapeDtypeStruct((2 * NX, PAIRS, LANES), jnp.bfloat16),
            jax.ShapeDtypeStruct((2, BLOCKS, 2 * PAIRS, JS), jnp.bfloat16),
        ],
        scratch_shapes=[
            bf(HALF, LANES + JS),
            bf(HALF, LANES + JS),
            fl(2, LANES),
            fl(2, NX, JS),
            bf(BLOCKS, PX, CL, CELLS),
            bf(BLOCKS, 4, PX // 2, NV, HALF),
            fl(2, PX, NV, HALF),
            bf(PT * PAIRS, HALF),
            bf(PT * PAIRS, HALF),
            fl(2, LANES // 128, NX * YS, 128),
            fl(2, PAIRS, JS),
            bf(2 * PAIRS, JS),
            fl(2, 2 * NX * MS, 128),
            bf(2, 2 * NX, PB, LANES),
            dma((3,)), dma((7,)), dma((8,)), dma((7,)), dma((8,)),
            dma((24,)), dma((24,)), dma((7,)), dma((7,)), dma((8,)), dma((8,)), dma((2,)),
        ],
        compiler_params=pltpu.CompilerParams(
            collective_id=2, has_side_effects=True, vmem_limit_bytes=VMEM_LIMIT
        ),
        name="front",
    )(weights, cond, val, ks, wide, table)


GB = 320
QS = 2 * PAIRS // 128
G_DEV = 320
LO = 192
HI = G_DEV - LO
DEPTH = 16
UNROLL = 32


def pick_kernel(g_ref, m, out, mt, mi, sel, lhs, ms, os):
    def fetch(step):
        slot = step % DEPTH
        return pltpu.make_async_copy(m.at[:, step], mi.at[slot], ms.at[slot])

    for step in range(DEPTH):
        fetch(step).start()

    def turn(step, carry):
        fetch(step).wait()
        for h in range(2):
            for q in range(2):
                t = mi[step % DEPTH, h, q * 128 : q * 128 + 128, :].T.astype(jnp.float32)
                mt[pl.ds(step * (STK * QS) + h * 2 + q, STK, stride=QS), :] = t[:STK, :]

        @pl.when(step < NX - DEPTH)
        def _():
            fetch(step + DEPTH).start()

        return carry

    lax.fori_loop(0, NX, turn, 0, unroll=4)
    store = lambda n: pltpu.make_async_copy(lhs.at[n % 2], out.at[n], os.at[n % 2])

    def block(n, carry):
        def rows(i, carry):
            for u in range(UNROLL):
                g = g_ref[n * GB + i * UNROLL + u]
                to = pl.ds(pl.multiple_of((i * UNROLL + u) * QS, QS), QS)
                sel[to, :] = mt[pl.ds(pl.multiple_of(g * QS, QS), QS), :]
            return carry

        lax.fori_loop(0, GB // UNROLL, rows, 0)

        @pl.when(n >= 2)
        def _():
            store(n - 2).wait()

        for k in range(QS):
            lhs[n % 2, :, k * 128 : k * 128 + 128] = sel[pl.ds(k, GB, stride=QS), :].astype(jnp.bfloat16)
        store(n).start()
        return carry

    lax.fori_loop(0, G_ROW // GB, block, 0)
    for n in range(2):
        store(G_ROW // GB - 2 + n).wait()


def pick(gvec, m):
    dma = pltpu.SemaphoreType.DMA
    return pl.pallas_call(
        pick_kernel,
        in_specs=[pl.BlockSpec(memory_space=pltpu.SMEM), pl.BlockSpec(memory_space=pl.ANY)],
        out_specs=pl.BlockSpec(memory_space=pl.ANY),
        out_shape=jax.ShapeDtypeStruct((G_ROW // GB, GB, 2 * PAIRS), jnp.bfloat16),
        scratch_shapes=[
            pltpu.VMEM((NX * STK * QS, 128), jnp.float32),
            pltpu.VMEM((DEPTH, 2, PAIRS, LANES), jnp.bfloat16),
            pltpu.VMEM((GB * QS, 128), jnp.float32),
            pltpu.VMEM((2, GB, 2 * PAIRS), jnp.bfloat16),
            dma((DEPTH,)), dma((2,)),
        ],
        compiler_params=pltpu.CompilerParams(vmem_limit_bytes=VMEM_LIMIT),
        name="pick",
    )(gvec, m)


def add_rows(dst, a, b, rows, step=32):
    def one(i, carry):
        at = pl.ds(pl.multiple_of(i * step, step), step)
        dst[at, :] = (a[at, :].astype(jnp.float32) + b[at, :].astype(jnp.float32)).astype(dst.dtype)
        return carry

    lax.fori_loop(0, rows // step, one, 0)


def back_kernel(
    rows, slab, out, sw, ours, theirs, acc, zr2, yr1, zr1, yr2,
    ms, s1, d1, sz2, dz2, sy1, dy1, sz1, dz1, sy2, dy2,
):
    row, col = lax.axis_index("row"), lax.axis_index("col")
    z, yl, core = col // 4, (col // 2) % 2, col % 2
    core_peer = {"row": row, "col": z * 4 + yl * 2 + (1 - core)}
    y_peer = {"row": row, "col": z * 4 + (1 - yl) * 2 + core}
    z_peer = lambda k: {"row": row, "col": ((z + k) % 4) * 4 + yl * 2 + core}
    barrier = pltpu.get_barrier_semaphore()
    for peer in (core_peer, y_peer, z_peer(1), z_peer(2), z_peer(3)):
        pl.semaphore_signal(barrier, inc=1, device_id=peer, device_id_type=MESH)

    def place(n):
        k, s = (n // 2 + 1) % 4, n % 2
        return ((z + k) % 4) * 4 + (yl * s + (1 - yl) * (1 - s)) * 2

    load = lambda n: pltpu.make_async_copy(rows.at[place(n) + core], ours.at[n], ms.at[n])
    for n in range(8):
        load(n).start()
    pl.semaphore_wait(barrier, 5)

    scale = -1.0 / math.sqrt(NV * NC)
    def remote(src, dst, ss, ds, peer):
        return pltpu.make_async_remote_copy(src, dst, ss, ds, device_id=peer, device_id_type=MESH)

    lo, hi = pl.ds(0, LO), pl.ds(LO, HI)
    first = lambda n: remote(rows.at[place(n) + 1 - core], theirs.at[n], s1.at[n], d1.at[n], core_peer)
    for n in range(8):
        first(n).start()
    for h in range(2):
        for r in range(NS // JS):
            sw[h * 2 * PAIRS : (h + 1) * 2 * PAIRS, r * JS : r * JS + JS] = slab[h, r]
    along_z = lambda k, s: remote(
        acc.at[(k + 3) % 4 * 2 + s, hi], zr2.at[(k - 1) * 2 + s], sz2.at[(k - 1) * 2 + s], dz2.at[(k - 1) * 2 + s], z_peer(k)
    )
    along_y = lambda k: remote(acc.at[(k + 3) % 4 * 2, lo], yr1.at[k], sy1.at[k], dy1.at[k], y_peer)
    last_z = lambda k: remote(acc.at[(k + 3) % 4 * 2 + 1, lo], zr1.at[k - 1], sz1.at[k - 1], dz1.at[k - 1], z_peer(k))

    def slot(n, carry):
        k, s = (n // 2 + 1) % 4, n % 2
        load(n).wait()
        first(n).wait_recv()
        lhs = jnp.concatenate([ours[n], theirs[n]], axis=1)
        acc[n] = (jnp.dot(lhs, sw[...], preferred_element_type=jnp.float32) * scale).astype(jnp.bfloat16)

        @pl.when(n < 6)
        def _():
            along_z(k, s).start()

        @pl.when(s == 0)
        def _():
            along_y(k).start()

        return carry

    lax.fori_loop(0, 8, slot, 0)
    for k in (1, 2, 3, 0):
        along_y(k).wait_recv()
        if k:
            at = acc.at[(k + 3) % 4 * 2 + 1]
            add_rows(at, at, yr1.at[k], LO)
            last_z(k).start()
    for k in (1, 2, 3):
        along_z(k, 0).wait_recv()

    def total(i, base, terms):
        at = pl.ds(pl.multiple_of(i * 16, 16), 16)
        value = base[at, :].astype(jnp.float32)
        for ref in terms:
            value = value + ref[at, :].astype(jnp.float32)
        return at, value

    def across(i, carry):
        at, value = total(i, acc.at[6, hi], [zr2.at[0], zr2.at[2], zr2.at[4]])
        yr2[0, at, :] = value.astype(jnp.bfloat16)
        return carry

    lax.fori_loop(0, HI // 16, across, 0)
    last_y = remote(yr2.at[0], yr2.at[1], sy2.at[0], dy2.at[0], y_peer)
    last_y.start()
    for k in (1, 2, 3):
        last_z(k).wait_recv()

    def low(i, carry):
        at, value = total(i, acc.at[7, lo], [yr1.at[0], zr1.at[0], zr1.at[1], zr1.at[2]])
        out[at, :] = value
        return carry

    lax.fori_loop(0, LO // 16, low, 0)
    for k in (1, 2, 3):
        along_z(k, 1).wait_recv()
    last_y.wait_recv()

    def high(i, carry):
        at, value = total(i, acc.at[7, hi], [zr2.at[1], zr2.at[3], zr2.at[5], yr2.at[1]])
        out[pl.ds(pl.multiple_of(LO + i * 16, 16), 16), :] = value
        return carry

    lax.fori_loop(0, HI // 16, high, 0)
    for n in range(8):
        first(n).wait_send()
    for k in range(4):
        along_y(k).wait_send()
        if k:
            last_z(k).wait_send()
            along_z(k, 0).wait_send()
            along_z(k, 1).wait_send()
    last_y.wait_send()


def back(rows, slab):
    dma = pltpu.SemaphoreType.DMA
    vmem = pl.BlockSpec(memory_space=pltpu.VMEM)
    part = lambda n, rows: pltpu.VMEM((n, rows, NS), jnp.bfloat16)
    return pl.pallas_call(
        back_kernel,
        in_specs=[pl.BlockSpec(memory_space=pl.ANY), vmem],
        out_specs=vmem,
        out_shape=jax.ShapeDtypeStruct((G_DEV, NS), jnp.float32),
        scratch_shapes=[
            pltpu.VMEM((4 * PAIRS, NS), jnp.bfloat16),
            pltpu.VMEM((8, GB, 2 * PAIRS), jnp.bfloat16),
            pltpu.VMEM((8, GB, 2 * PAIRS), jnp.bfloat16),
            pltpu.VMEM((8, G_DEV, NS), jnp.bfloat16),
            part(6, HI), part(4, LO), part(3, LO), part(2, HI),
            dma((8,)), dma((8,)), dma((8,)), dma((6,)), dma((6,)), dma((4,)), dma((4,)),
            dma((3,)), dma((3,)), dma((1,)), dma((1,)),
        ],
        compiler_params=pltpu.CompilerParams(
            collective_id=3, has_side_effects=True, vmem_limit_bytes=VMEM_LIMIT
        ),
        name="back",
    )(rows, slab)


def places_kernel(mine, cond, val, out, cond_out, val_out, send_sem, recv_sem):
    row, col = lax.axis_index("row"), lax.axis_index("col")
    barrier = pltpu.get_barrier_semaphore()
    peers = [{"row": (row + k) % 8, "col": col} for k in range(1, 8)]
    for peer in peers:
        pl.semaphore_signal(barrier, inc=1, device_id=peer, device_id_type=MESH)
    pl.semaphore_wait(barrier, 7)
    copies = []
    for k, peer in enumerate(peers):
        copies.append(
            pltpu.make_async_remote_copy(
                mine, out.at[row], send_sem.at[k], recv_sem.at[k], device_id=peer, device_id_type=MESH
            )
        )
        copies[-1].start()
    out[row] = mine[...]
    r = lax.broadcasted_iota(jnp.int32, (128, 128), 0)
    c = lax.broadcasted_iota(jnp.int32, (128, 128), 1)
    back = (r + c == 127).astype(jnp.bfloat16)
    half = PX // 2
    cond_out[:, :, :HALF] = cond[:, :, :HALF]
    for p in range(2):
        val_out[2 * p] = val[p * half : p * half + half, :, :HALF]
    for b in range(HALF // 128):
        source = slice(CELLS - b * 128 - 128, CELLS - b * 128)
        to = slice(b * 128, b * 128 + 128)
        flip = lambda ref: jnp.dot(
            ref[:, :, source].reshape(PX * CL, 128), back, preferred_element_type=jnp.float32
        ).astype(jnp.bfloat16).reshape(PX, CL, 128)
        cond_out[:, :, HALF + b * 128 : HALF + b * 128 + 128] = flip(cond)
        turned = flip(val)
        for p in range(2):
            val_out[2 * p + 1, :, :, to] = turned[p * half : p * half + half]
    for copy in copies:
        copy.wait_recv()
    for copy in copies:
        copy.wait_send()


def places(mine, cond, val):
    return pl.pallas_call(
        places_kernel,
        in_specs=[pl.BlockSpec(memory_space=pltpu.VMEM)] * 3,
        out_specs=[pl.BlockSpec(memory_space=pltpu.VMEM)] * 3,
        out_shape=[
            jax.ShapeDtypeStruct((8, G_ROW // 128, 128), jnp.int32),
            jax.ShapeDtypeStruct((PX, CL, CELLS), jnp.bfloat16),
            jax.ShapeDtypeStruct((4, PX // 2, NV, HALF), jnp.bfloat16),
        ],
        scratch_shapes=[pltpu.SemaphoreType.DMA((7,)), pltpu.SemaphoreType.DMA((7,))],
        compiler_params=pltpu.CompilerParams(collective_id=1, has_side_effects=True),
        name="places",
    )(mine, cond, val)


def body(psi_val, psi_cond, energy_val, energy_cond, stick_map, gvec_map, slab_index):
    row = lax.axis_index("row")
    mine = lax.dynamic_slice(stick_map, (row * STK,), (STK,))
    cols = lax.dynamic_slice(slab_index, (row * JS,), (JS,))
    maps, cond, val = places(
        gvec_map.reshape(G_ROW // 128, 128), psi_cond.transpose(1, 0, 2), psi_val.transpose(1, 0, 2)
    )
    maps = maps.reshape(-1)
    place = jnp.take(maps, cols)
    col_kx = place // STK
    col_stick = jnp.take(stick_map, cols // G_ROW * STK + place % STK)
    pad = jnp.zeros((LANES - STK,), jnp.int32)
    flat = jnp.concatenate([mine, pad, col_stick])
    ky, kz = flat // NZ, flat % NZ
    full_kx = jnp.concatenate([jnp.zeros((LANES,), jnp.int32), col_kx])
    ks = jnp.stack([ky, kz, full_kx]).astype(jnp.float32)
    dy = jnp.array([0, 0, 0, 1, 0, 1, 1, 1], jnp.int32)
    dx = jnp.array([0, 1, 3, 0, 2, 1, 3, 2], jnp.int32)
    source = (row // 4 + dy) % 2 * 4 + (row % 4 + dx) % 4
    xs = (source[:, None] * PX + jnp.arange(PX, dtype=jnp.int32)[None, :]).reshape(NX)
    weight = jnp.sqrt(2.0 / (energy_cond[None, :] - energy_val[:, None])) * (
        1.0 / (math.sqrt(NY * NZ) * math.sqrt(NX))
    )
    weight = weight.reshape(PAIRS)
    wide = jnp.broadcast_to(weight[:, None], (PAIRS, JS))
    freq = jnp.arange(NX, dtype=jnp.int32)
    ax = (freq[:, None] * xs[None, :] % NX).astype(jnp.float32) * (2.0 * math.pi / NX)
    cx, sx = jnp.cos(ax), jnp.sin(ax)
    table = jnp.concatenate(
        [jnp.concatenate([cx, sx], axis=1), jnp.concatenate([-sx, cx], axis=1)], axis=0
    ).astype(jnp.bfloat16)

    m, slab = front(weight, cond, val, ks, wide, table)
    return back(pick(gvec_map, m.reshape(2, NX, PAIRS, LANES)), slab)


def solution(mesh):
    in_specs = (P(None, "row", None), P("col", "row", None), P(), P("col"), P(), P("row"), P())
    out_specs = P(("row", "col"), None)
    return jax.shard_map(body, mesh=mesh, in_specs=in_specs, out_specs=out_specs, check_vma=False)
```

```python
import math

import jax
import jax.numpy as jnp
from jax import lax
from jax.experimental import pallas as pl
from jax.experimental.pallas import tpu as pltpu
from jax.sharding import PartitionSpec as P

NX = 48
NY = 48
NZ = 48
CELLS = NY * NZ
HALF = CELLS // 2
NC = 256
NV = 16
CL = 16
PAIRS = NV * CL
STK = 192
G_ROW = 5120
NS = 1024
JS = 128
XB = 4
LANES = 256
VMEM_LIMIT = 60 * 1024 * 1024
MESH = pl.DeviceIdType.MESH


def turn_angle(t):
    return (t - 96.0 * jnp.floor((t + 0.5) * (1.0 / 96.0))) * (math.pi / 48.0)


def make_tables(ks, rows_of_blocks, tc, ts, rot, ph):
    width = LANES + JS
    ky, kz = ks[0:1, :], ks[1:2, :]
    odd = lambda n: 2.0 * lax.broadcasted_iota(jnp.int32, (n, width), 0).astype(jnp.float32) + 1.0
    ay, az = turn_angle(odd(NY // 2) * ky), turn_angle(odd(NZ) * kz)
    cy, sy, cz, sz = jnp.cos(ay), jnp.sin(ay), jnp.cos(az), jnp.sin(az)
    for y in range(NY // 2):
        to = slice(y * NZ, y * NZ + NZ)
        tc[to, :] = (cy[y : y + 1, :] * cz - sy[y : y + 1, :] * sz).astype(jnp.bfloat16)
        ts[to, :] = -(sy[y : y + 1, :] * cz + cy[y : y + 1, :] * sz).astype(jnp.bfloat16)
    shift = turn_angle(ky + kz)
    rot[0:1, :] = jnp.cos(shift[:, :LANES])
    rot[1:2, :] = jnp.sin(shift[:, :LANES])
    plane = lax.broadcasted_iota(jnp.int32, (NX, JS), 0)
    xs = plane
    for b, block_row in enumerate(rows_of_blocks):
        inside = (plane >= b * PX) & (plane < b * PX + PX)
        xs = jnp.where(inside, plane + (block_row - b) * PX, xs)
    theta = turn_angle((ky + kz)[:, LANES:] - 2.0 * xs.astype(jnp.float32) * ks[2:3, LANES:])
    ph[0] = jnp.cos(theta)
    ph[1] = jnp.sin(theta)


BLOCKS = 8
PX = NX // BLOCKS
PT = 3
YS = PAIRS + 8
PB = 16
MS = PB + 8


def density(vf, cbuf, b, plane, at, even, odd):
    cond = cbuf.at[b, plane]
    for v in range(NV):
        out = slice(at * PAIRS + v * CL, at * PAIRS + v * CL + CL)
        spread = lambda h: jnp.broadcast_to(vf[h, plane, v : v + 1, :], (CL, HALF)).astype(jnp.bfloat16)
        lo = spread(0) * cond[:, :HALF]
        hi = spread(1) * cond[:, HALF:]
        even[out, :] = lo + hi
        odd[out, :] = lo - hi


def transform(b, first, even, odd, tc, ts, rot, ph, y, sacc):
    a = jnp.dot(even[...], tc[...], preferred_element_type=jnp.float32)
    c = jnp.dot(odd[...], ts[...], preferred_element_type=jnp.float32)
    cosr, sinr = rot[0:1, :], rot[1:2, :]
    real, imag = sacc[0], sacc[1]
    for i in range(PT):
        x = b * PX + first + i
        rows = slice(i * PAIRS, i * PAIRS + PAIRS)
        am, cm = a[rows, :LANES], c[rows, :LANES]
        to = pl.ds(pl.multiple_of(x * YS, 8), PAIRS)
        for k, value in enumerate((cosr * am - sinr * cm, cosr * cm + sinr * am)):
            for h in range(LANES // 128):
                y[k, h, to, :] = value[:, h * 128 : h * 128 + 128]
        av, cv = a[rows, LANES:], c[rows, LANES:]
        cp, sp = ph[0, pl.ds(x, 1), :], ph[1, pl.ds(x, 1), :]
        real = real + (cp * av - sp * cv)
        imag = imag + (cp * cv + sp * av)
    sacc[0] = real
    sacc[1] = imag


def front_kernel(
    weights, cond, val, near_cond, near_val, ks, wide, table, m_out, slab_out,
    tc, ts, rot, ph, cbuf, vbuf, vf, even, odd, y, sacc, sl, mo, mb,
    lsem, cs, cr, vs, vr, gs, gr, ss, sr, fs, fr, ms,
):
    row, col = lax.axis_index("row"), lax.axis_index("col")
    yh, x = row // 4, row % 4
    z, yl, core = col // 4, (col // 2) % 2, col % 2
    zo = z + 1 - 2 * (z % 2)
    xp = {"row": yh * 4 + (x + 1) % 4, "col": col}
    xm = {"row": yh * 4 + (x + 3) % 4, "col": col}
    group = [
        {"row": row, "col": zo * 4 + yl * 2 + core},
        {"row": row, "col": z * 4 + yl * 2 + 1 - core},
        {"row": row, "col": zo * 4 + yl * 2 + 1 - core},
    ]
    across = [{"row": (row + k) % 8, "col": col} for k in range(1, 8)]
    part = core * 2 + z % 2

    own = [
        pltpu.make_async_copy(cond, cbuf.at[0], lsem.at[0]),
        pltpu.make_async_copy(val, vbuf.at[0], lsem.at[1]),
        pltpu.make_async_copy(near_cond, cbuf.at[pl.ds(1, 3)], lsem.at[2]),
    ]
    for k in range(3):
        own.append(pltpu.make_async_copy(near_val.at[k], vbuf.at[k + 1, part], lsem.at[3 + k]))
    for copy in own:
        copy.start()
    barrier = pltpu.get_barrier_semaphore()
    for peer in across + group:
        pl.semaphore_signal(barrier, inc=1, device_id=peer, device_id_type=MESH)
    pl.semaphore_wait(barrier, 10)

    hops = [(3, 6, xp), (3, 5, xm), (2, 4, xp), (5, 7, xm)]
    hop_to = [hop[1] for hop in hops]

    def cond_hop(n):
        src, dst, peer = hops[n]
        return pltpu.make_async_remote_copy(
            cbuf.at[src], cbuf.at[dst], cs.at[n], cr.at[dst], device_id=peer, device_id_type=MESH
        )

    def val_hop(n):
        src, dst, peer = hops[n]
        return pltpu.make_async_remote_copy(
            vbuf.at[src, part], vbuf.at[dst, part], vs.at[n], vr.at[dst], device_id=peer, device_id_type=MESH
        )

    def spread(b, j):
        return pltpu.make_async_remote_copy(
            vbuf.at[b, part], vbuf.at[b, part], gs.at[b * 3 + j], gr.at[b * 3 + j],
            device_id=group[j], device_id_type=MESH,
        )

    def land_val(b, *forward):
        val_hop(hop_to.index(b)).wait_recv()
        for n in forward:
            val_hop(n).start()
        for j in range(3):
            spread(b, j).start()

    def land(b, *forward):
        cond_hop(hop_to.index(b)).wait_recv()
        for n in forward:
            cond_hop(n).start()

    def ready(b):
        for j in range(3):
            spread(b, j).wait_recv()

    for copy in own:
        copy.wait()
    for n in range(3):
        val_hop(n).start()
    for n in (1, 2, 0):
        cond_hop(n).start()
    for b in range(1, 4):
        for j in range(3):
            spread(b, j).start()
    sacc[...] = jnp.zeros_like(sacc)
    steps = [(0, 0), (0, 1), (0, 3), (1, 0), (0, 2), (1, 1), (1, 3), (1, 2)]
    make_tables(ks, [(yh + dy) % 2 * 4 + (x + dx) % 4 for dy, dx in steps], tc, ts, rot, ph)

    def block(b, carry):
        @pl.when(b == 1)
        def _():
            ready(1)
            land_val(5, 3)
            land_val(4)
            land_val(6)

        @pl.when(b == 2)
        def _():
            ready(2)
            land_val(7)
            land(5, 3)

        @pl.when(b == 3)
        def _():
            ready(3)

        @pl.when(b == 4)
        def _():
            land(4)
            ready(4)

        @pl.when(b == 5)
        def _():
            ready(5)

        @pl.when(b == 6)
        def _():
            land(6)
            ready(6)

        @pl.when(b == 7)
        def _():
            land(7)
            ready(7)

        def widen(j, carry):
            for q in range(4):
                vf[q % 2, (q // 2) * 3 + j] = vbuf[b, q, j].astype(jnp.float32)
            return carry

        lax.fori_loop(0, 3, widen, 0)

        def some(i, carry):
            for u in range(PT):
                density(vf, cbuf, b, i * PT + u, u, even, odd)
            transform(b, i * PT, even, odd, tc, ts, rot, ph, y, sacc)
            return carry

        lax.fori_loop(0, PX // PT, some, 0)
        return carry

    lax.fori_loop(0, BLOCKS, block, 0)

    for h in range(2):
        sl[h * PAIRS : h * PAIRS + PAIRS, :] = (sacc[h] * wide[...]).astype(jnp.bfloat16)
    keep = pltpu.make_async_copy(sl, slab_out.at[0, row], lsem.at[6])
    keep.start()

    def push(k):
        return pltpu.make_async_remote_copy(
            sl, slab_out.at[0, row], ss.at[k], sr.at[k], device_id=across[k], device_id_type=MESH
        )

    def hand(k):
        at = (row + 7 - k) % 8
        return pltpu.make_async_remote_copy(
            sl if k == 7 else slab_out.at[0, at], slab_out.at[1, at], fs.at[k], fr.at[k],
            device_id=group[1], device_id_type=MESH,
        )

    for k in range(7):
        push(k).start()
    hand(7).start()

    def chunk(i, carry):
        for k in range(7):

            @pl.when(i == 5 + k)
            def _():
                push(k).wait_recv()
                hand(k).start()

        slot = i % 2
        ps = pl.ds(pl.multiple_of(i * PB, PB), PB)
        out = pltpu.make_async_copy(mb.at[slot], m_out.at[:, ps, :], ms.at[slot])
        for p in range(PB):
            at = pl.ds(i * PB + p, NX, stride=YS)
            rhs = jnp.concatenate(
                [jnp.concatenate([y[k, 0, at, :], y[k, 1, at, :]], axis=1) for k in range(2)], axis=0
            ).astype(jnp.bfloat16)
            res = jnp.dot(table[...], rhs, preferred_element_type=jnp.float32) * weights[i * PB + p]
            for h in range(LANES // 128):
                mo[h, pl.ds(p, 2 * NX, stride=MS), :] = res[:, h * 128 : h * 128 + 128]

        @pl.when(i >= 2)
        def _():
            out.wait()

        for h in range(LANES // 128):
            lanes = slice(h * 128, h * 128 + 128)
            mb[slot, :, :, lanes] = mo[h].reshape(2 * NX, MS, 128)[:, :PB].astype(jnp.bfloat16)
        out.start()
        return carry

    lax.fori_loop(0, PAIRS // PB, chunk, 0)
    for slot in range(2):
        pltpu.make_async_copy(mb.at[slot], m_out.at[:, pl.ds(slot * PB, PB), :], ms.at[slot]).wait()
    keep.wait()
    for k in range(8):
        hand(k).wait_recv()
        hand(k).wait_send()
    for k in range(7):
        push(k).wait_send()
    for n in range(len(hops)):
        val_hop(n).wait_send()
        cond_hop(n).wait_send()
    for b in range(1, BLOCKS):
        for j in range(3):
            spread(b, j).wait_send()


def front(weights, cond, val, near_cond, near_val, ks, wide, table):
    dma = pltpu.SemaphoreType.DMA
    vmem = pl.BlockSpec(memory_space=pltpu.VMEM)
    hbm = pl.BlockSpec(memory_space=pl.ANY)
    bf = lambda *shape: pltpu.VMEM(shape, jnp.bfloat16)
    fl = lambda *shape: pltpu.VMEM(shape, jnp.float32)
    return pl.pallas_call(
        front_kernel,
        in_specs=[pl.BlockSpec(memory_space=pltpu.SMEM)] + [hbm] * 4 + [vmem] * 3,
        out_specs=[hbm, hbm],
        out_shape=[
            jax.ShapeDtypeStruct((2 * NX, PAIRS, LANES), jnp.bfloat16),
            jax.ShapeDtypeStruct((2, BLOCKS, 2 * PAIRS, JS), jnp.bfloat16),
        ],
        scratch_shapes=[
            bf(HALF, LANES + JS),
            bf(HALF, LANES + JS),
            fl(2, LANES),
            fl(2, NX, JS),
            bf(BLOCKS, PX, CL, CELLS),
            bf(BLOCKS, 4, PX // 2, NV, HALF),
            fl(2, PX, NV, HALF),
            bf(PT * PAIRS, HALF),
            bf(PT * PAIRS, HALF),
            fl(2, LANES // 128, NX * YS, 128),
            fl(2, PAIRS, JS),
            bf(2 * PAIRS, JS),
            fl(2, 2 * NX * MS, 128),
            bf(2, 2 * NX, PB, LANES),
            dma((7,)), dma((4,)), dma((8,)), dma((4,)), dma((8,)),
            dma((24,)), dma((24,)), dma((7,)), dma((7,)), dma((8,)), dma((8,)), dma((2,)),
        ],
        compiler_params=pltpu.CompilerParams(
            collective_id=2, has_side_effects=True, vmem_limit_bytes=VMEM_LIMIT
        ),
        name="front",
    )(weights, cond, val, near_cond, near_val, ks, wide, table)


GB = 320
QS = 2 * PAIRS // 128
G_DEV = 320
LO = 192
HI = G_DEV - LO
DEPTH = 16
UNROLL = 32


def pick_kernel(g_ref, m, out, mt, mi, sel, lhs, ms, os):
    def fetch(step):
        slot = step % DEPTH
        return pltpu.make_async_copy(m.at[:, step], mi.at[slot], ms.at[slot])

    for step in range(DEPTH):
        fetch(step).start()

    def turn(step, carry):
        fetch(step).wait()
        for h in range(2):
            for q in range(2):
                t = mi[step % DEPTH, h, q * 128 : q * 128 + 128, :].T.astype(jnp.float32)
                mt[pl.ds(step * (STK * QS) + h * 2 + q, STK, stride=QS), :] = t[:STK, :]

        @pl.when(step < NX - DEPTH)
        def _():
            fetch(step + DEPTH).start()

        return carry

    lax.fori_loop(0, NX, turn, 0, unroll=4)
    store = lambda n: pltpu.make_async_copy(lhs.at[n % 2], out.at[n], os.at[n % 2])

    def block(n, carry):
        def rows(i, carry):
            for u in range(UNROLL):
                g = g_ref[n * GB + i * UNROLL + u]
                to = pl.ds(pl.multiple_of((i * UNROLL + u) * QS, QS), QS)
                sel[to, :] = mt[pl.ds(pl.multiple_of(g * QS, QS), QS), :]
            return carry

        lax.fori_loop(0, GB // UNROLL, rows, 0)

        @pl.when(n >= 2)
        def _():
            store(n - 2).wait()

        for k in range(QS):
            lhs[n % 2, :, k * 128 : k * 128 + 128] = sel[pl.ds(k, GB, stride=QS), :].astype(jnp.bfloat16)
        store(n).start()
        return carry

    lax.fori_loop(0, G_ROW // GB, block, 0)
    for n in range(2):
        store(G_ROW // GB - 2 + n).wait()


def pick(gvec, m):
    dma = pltpu.SemaphoreType.DMA
    return pl.pallas_call(
        pick_kernel,
        in_specs=[pl.BlockSpec(memory_space=pltpu.SMEM), pl.BlockSpec(memory_space=pl.ANY)],
        out_specs=pl.BlockSpec(memory_space=pl.ANY),
        out_shape=jax.ShapeDtypeStruct((G_ROW // GB, GB, 2 * PAIRS), jnp.bfloat16),
        scratch_shapes=[
            pltpu.VMEM((NX * STK * QS, 128), jnp.float32),
            pltpu.VMEM((DEPTH, 2, PAIRS, LANES), jnp.bfloat16),
            pltpu.VMEM((GB * QS, 128), jnp.float32),
            pltpu.VMEM((2, GB, 2 * PAIRS), jnp.bfloat16),
            dma((DEPTH,)), dma((2,)),
        ],
        compiler_params=pltpu.CompilerParams(vmem_limit_bytes=VMEM_LIMIT),
        name="pick",
    )(gvec, m)


def add_rows(dst, a, b, rows, step=32):
    def one(i, carry):
        at = pl.ds(pl.multiple_of(i * step, step), step)
        dst[at, :] = (a[at, :].astype(jnp.float32) + b[at, :].astype(jnp.float32)).astype(dst.dtype)
        return carry

    lax.fori_loop(0, rows // step, one, 0)


def back_kernel(
    rows, slab, out, sw, ours, theirs, acc, zr2, yr1, zr1, yr2,
    ms, s1, d1, sz2, dz2, sy1, dy1, sz1, dz1, sy2, dy2,
):
    row, col = lax.axis_index("row"), lax.axis_index("col")
    z, yl, core = col // 4, (col // 2) % 2, col % 2
    core_peer = {"row": row, "col": z * 4 + yl * 2 + (1 - core)}
    y_peer = {"row": row, "col": z * 4 + (1 - yl) * 2 + core}
    z_peer = lambda k: {"row": row, "col": ((z + k) % 4) * 4 + yl * 2 + core}
    barrier = pltpu.get_barrier_semaphore()
    for peer in (core_peer, y_peer, z_peer(1), z_peer(2), z_peer(3)):
        pl.semaphore_signal(barrier, inc=1, device_id=peer, device_id_type=MESH)

    def place(n):
        k, s = (n // 2 + 1) % 4, n % 2
        return ((z + k) % 4) * 4 + (yl * s + (1 - yl) * (1 - s)) * 2

    load = lambda n: pltpu.make_async_copy(rows.at[place(n) + core], ours.at[n], ms.at[n])
    for n in range(8):
        load(n).start()
    pl.semaphore_wait(barrier, 5)

    scale = -1.0 / math.sqrt(NV * NC)
    def remote(src, dst, ss, ds, peer):
        return pltpu.make_async_remote_copy(src, dst, ss, ds, device_id=peer, device_id_type=MESH)

    lo, hi = pl.ds(0, LO), pl.ds(LO, HI)
    first = lambda n: remote(rows.at[place(n) + 1 - core], theirs.at[n], s1.at[n], d1.at[n], core_peer)
    for n in range(8):
        first(n).start()
    for h in range(2):
        for r in range(NS // JS):
            sw[h * 2 * PAIRS : (h + 1) * 2 * PAIRS, r * JS : r * JS + JS] = slab[h, r]
    along_z = lambda k, s: remote(
        acc.at[(k + 3) % 4 * 2 + s, hi], zr2.at[(k - 1) * 2 + s], sz2.at[(k - 1) * 2 + s], dz2.at[(k - 1) * 2 + s], z_peer(k)
    )
    along_y = lambda k: remote(acc.at[(k + 3) % 4 * 2, lo], yr1.at[k], sy1.at[k], dy1.at[k], y_peer)
    last_z = lambda k: remote(acc.at[(k + 3) % 4 * 2 + 1, lo], zr1.at[k - 1], sz1.at[k - 1], dz1.at[k - 1], z_peer(k))

    def slot(n, carry):
        k, s = (n // 2 + 1) % 4, n % 2
        load(n).wait()
        first(n).wait_recv()
        lhs = jnp.concatenate([ours[n], theirs[n]], axis=1)
        acc[n] = (jnp.dot(lhs, sw[...], preferred_element_type=jnp.float32) * scale).astype(jnp.bfloat16)

        @pl.when(n < 6)
        def _():
            along_z(k, s).start()

        @pl.when(s == 0)
        def _():
            along_y(k).start()

        return carry

    lax.fori_loop(0, 8, slot, 0)
    for k in (1, 2, 3, 0):
        along_y(k).wait_recv()
        if k:
            at = acc.at[(k + 3) % 4 * 2 + 1]
            add_rows(at, at, yr1.at[k], LO)
            last_z(k).start()
    for k in (1, 2, 3):
        along_z(k, 0).wait_recv()

    def total(i, base, terms):
        at = pl.ds(pl.multiple_of(i * 16, 16), 16)
        value = base[at, :].astype(jnp.float32)
        for ref in terms:
            value = value + ref[at, :].astype(jnp.float32)
        return at, value

    def across(i, carry):
        at, value = total(i, acc.at[6, hi], [zr2.at[0], zr2.at[2], zr2.at[4]])
        yr2[0, at, :] = value.astype(jnp.bfloat16)
        return carry

    lax.fori_loop(0, HI // 16, across, 0)
    last_y = remote(yr2.at[0], yr2.at[1], sy2.at[0], dy2.at[0], y_peer)
    last_y.start()
    for k in (1, 2, 3):
        last_z(k).wait_recv()

    def low(i, carry):
        at, value = total(i, acc.at[7, lo], [yr1.at[0], zr1.at[0], zr1.at[1], zr1.at[2]])
        out[at, :] = value
        return carry

    lax.fori_loop(0, LO // 16, low, 0)
    for k in (1, 2, 3):
        along_z(k, 1).wait_recv()
    last_y.wait_recv()

    def high(i, carry):
        at, value = total(i, acc.at[7, hi], [zr2.at[1], zr2.at[3], zr2.at[5], yr2.at[1]])
        out[pl.ds(pl.multiple_of(LO + i * 16, 16), 16), :] = value
        return carry

    lax.fori_loop(0, HI // 16, high, 0)
    for n in range(8):
        first(n).wait_send()
    for k in range(4):
        along_y(k).wait_send()
        if k:
            last_z(k).wait_send()
            along_z(k, 0).wait_send()
            along_z(k, 1).wait_send()
    last_y.wait_send()


def back(rows, slab):
    dma = pltpu.SemaphoreType.DMA
    vmem = pl.BlockSpec(memory_space=pltpu.VMEM)
    part = lambda n, rows: pltpu.VMEM((n, rows, NS), jnp.bfloat16)
    return pl.pallas_call(
        back_kernel,
        in_specs=[pl.BlockSpec(memory_space=pl.ANY), vmem],
        out_specs=vmem,
        out_shape=jax.ShapeDtypeStruct((G_DEV, NS), jnp.float32),
        scratch_shapes=[
            pltpu.VMEM((4 * PAIRS, NS), jnp.bfloat16),
            pltpu.VMEM((8, GB, 2 * PAIRS), jnp.bfloat16),
            pltpu.VMEM((8, GB, 2 * PAIRS), jnp.bfloat16),
            pltpu.VMEM((8, G_DEV, NS), jnp.bfloat16),
            part(6, HI), part(4, LO), part(3, LO), part(2, HI),
            dma((8,)), dma((8,)), dma((8,)), dma((6,)), dma((6,)), dma((4,)), dma((4,)),
            dma((3,)), dma((3,)), dma((1,)), dma((1,)),
        ],
        compiler_params=pltpu.CompilerParams(
            collective_id=3, has_side_effects=True, vmem_limit_bytes=VMEM_LIMIT
        ),
        name="back",
    )(rows, slab)


def places_kernel(
    mine, cond, val, out, cond_out, val_out, near_cond, near_val, send_sem, recv_sem, cs, cr, vs, vr
):
    row, col = lax.axis_index("row"), lax.axis_index("col")
    yh, x = row // 4, row % 4
    z, yl, core = col // 4, (col // 2) % 2, col % 2
    part = core * 2 + z % 2
    barrier = pltpu.get_barrier_semaphore()
    peers = [{"row": (row + k) % 8, "col": col} for k in range(1, 8)]
    xp = {"row": yh * 4 + (x + 1) % 4, "col": col}
    xm = {"row": yh * 4 + (x + 3) % 4, "col": col}
    yc = {"row": (1 - yh) * 4 + x, "col": col}
    yv = {"row": (1 - yh) * 4 + x, "col": z * 4 + (1 - yl) * 2 + core}
    for peer in peers + [yv]:
        pl.semaphore_signal(barrier, inc=1, device_id=peer, device_id_type=MESH)
    r = lax.broadcasted_iota(jnp.int32, (128, 128), 0)
    c = lax.broadcasted_iota(jnp.int32, (128, 128), 1)
    back = (r + c == 127).astype(jnp.bfloat16)
    half = PX // 2
    cond_out[:, :, :HALF] = cond[:, :, :HALF]
    for p in range(2):
        val_out[2 * p] = val[p * half : p * half + half, :, :HALF]
    for b in range(HALF // 128):
        source = slice(CELLS - b * 128 - 128, CELLS - b * 128)
        to = slice(b * 128, b * 128 + 128)
        flip = lambda ref: jnp.dot(
            ref[:, :, source].reshape(PX * CL, 128), back, preferred_element_type=jnp.float32
        ).astype(jnp.bfloat16).reshape(PX, CL, 128)
        cond_out[:, :, HALF + b * 128 : HALF + b * 128 + 128] = flip(cond)
        turned = flip(val)
        for p in range(2):
            val_out[2 * p + 1, :, :, to] = turned[p * half : p * half + half]
    pl.semaphore_wait(barrier, 8)
    copies = []
    for k, peer in enumerate(peers):
        copies.append(
            pltpu.make_async_remote_copy(
                mine, out.at[row], send_sem.at[k], recv_sem.at[k], device_id=peer, device_id_type=MESH
            )
        )
    for k, peer in enumerate((xm, xp, yv)):
        copies.append(
            pltpu.make_async_remote_copy(
                val_out.at[part], near_val.at[k], vs.at[k], vr.at[k], device_id=peer, device_id_type=MESH
            )
        )
    for k, peer in enumerate((xm, xp, yc)):
        copies.append(
            pltpu.make_async_remote_copy(
                cond_out, near_cond.at[k], cs.at[k], cr.at[k], device_id=peer, device_id_type=MESH
            )
        )
    for copy in copies:
        copy.start()
    out[row] = mine[...]
    for copy in copies:
        copy.wait_recv()
    for copy in copies:
        copy.wait_send()


def places(mine, cond, val):
    return pl.pallas_call(
        places_kernel,
        in_specs=[pl.BlockSpec(memory_space=pltpu.VMEM)] * 3,
        out_specs=[pl.BlockSpec(memory_space=pltpu.VMEM)] * 5,
        out_shape=[
            jax.ShapeDtypeStruct((8, G_ROW // 128, 128), jnp.int32),
            jax.ShapeDtypeStruct((PX, CL, CELLS), jnp.bfloat16),
            jax.ShapeDtypeStruct((4, PX // 2, NV, HALF), jnp.bfloat16),
            jax.ShapeDtypeStruct((3, PX, CL, CELLS), jnp.bfloat16),
            jax.ShapeDtypeStruct((3, PX // 2, NV, HALF), jnp.bfloat16),
        ],
        scratch_shapes=[pltpu.SemaphoreType.DMA((n,)) for n in (7, 7, 3, 3, 3, 3)],
        compiler_params=pltpu.CompilerParams(collective_id=1, has_side_effects=True),
        name="places",
    )(mine, cond, val)


def body(psi_val, psi_cond, energy_val, energy_cond, stick_map, gvec_map, slab_index):
    row = lax.axis_index("row")
    mine = lax.dynamic_slice(stick_map, (row * STK,), (STK,))
    cols = lax.dynamic_slice(slab_index, (row * JS,), (JS,))
    maps, *near = places(
        gvec_map.reshape(G_ROW // 128, 128), psi_cond.transpose(1, 0, 2), psi_val.transpose(1, 0, 2)
    )
    maps = maps.reshape(-1)
    place = jnp.take(maps, cols)
    col_kx = place // STK
    col_stick = jnp.take(stick_map, cols // G_ROW * STK + place % STK)
    pad = jnp.zeros((LANES - STK,), jnp.int32)
    flat = jnp.concatenate([mine, pad, col_stick])
    ky, kz = flat // NZ, flat % NZ
    full_kx = jnp.concatenate([jnp.zeros((LANES,), jnp.int32), col_kx])
    ks = jnp.stack([ky, kz, full_kx]).astype(jnp.float32)
    dy = jnp.array([0, 0, 0, 1, 0, 1, 1, 1], jnp.int32)
    dx = jnp.array([0, 1, 3, 0, 2, 1, 3, 2], jnp.int32)
    source = (row // 4 + dy) % 2 * 4 + (row % 4 + dx) % 4
    xs = (source[:, None] * PX + jnp.arange(PX, dtype=jnp.int32)[None, :]).reshape(NX)
    weight = jnp.sqrt(2.0 / (energy_cond[None, :] - energy_val[:, None])) * (
        1.0 / (math.sqrt(NY * NZ) * math.sqrt(NX))
    )
    weight = weight.reshape(PAIRS)
    wide = jnp.broadcast_to(weight[:, None], (PAIRS, JS))
    freq = jnp.arange(NX, dtype=jnp.int32)
    ax = (freq[:, None] * xs[None, :] % NX).astype(jnp.float32) * (2.0 * math.pi / NX)
    cx, sx = jnp.cos(ax), jnp.sin(ax)
    table = jnp.concatenate(
        [jnp.concatenate([cx, sx], axis=1), jnp.concatenate([-sx, cx], axis=1)], axis=0
    ).astype(jnp.bfloat16)

    m, slab = front(weight, *near, ks, wide, table)
    return back(pick(gvec_map, m.reshape(2, NX, PAIRS, LANES)), slab)


def solution(mesh):
    in_specs = (P(None, "row", None), P("col", "row", None), P(), P("col"), P(), P("row"), P())
    out_specs = P(("row", "col"), None)
    return jax.shard_map(body, mesh=mesh, in_specs=in_specs, out_specs=out_specs, check_vma=False)
```

```python
import math

import jax
import jax.numpy as jnp
from jax import lax
from jax.experimental import pallas as pl
from jax.experimental.pallas import tpu as pltpu
from jax.sharding import PartitionSpec as P

NX = 48
NY = 48
NZ = 48
CELLS = NY * NZ
HALF = CELLS // 2
NC = 256
NV = 16
CL = 16
PAIRS = NV * CL
STK = 192
G_ROW = 5120
NS = 1024
JS = 128
XB = 4
LANES = 256
VMEM_LIMIT = 60 * 1024 * 1024
MESH = pl.DeviceIdType.MESH


def turn_angle(t):
    return (t - 96.0 * jnp.floor((t + 0.5) * (1.0 / 96.0))) * (math.pi / 48.0)


def make_tables(ks, rows_of_blocks, tc, ts, rot, ph, table):
    width = LANES + JS
    ky, kz = ks[0:1, :], ks[1:2, :]
    odd = lambda n: 2.0 * lax.broadcasted_iota(jnp.int32, (n, width), 0).astype(jnp.float32) + 1.0
    ay, az = turn_angle(odd(NY // 2) * ky), turn_angle(odd(NZ) * kz)
    cy, sy, cz, sz = jnp.cos(ay), jnp.sin(ay), jnp.cos(az), jnp.sin(az)
    for y in range(NY // 2):
        to = slice(y * NZ, y * NZ + NZ)
        tc[to, :] = (cy[y : y + 1, :] * cz - sy[y : y + 1, :] * sz).astype(jnp.bfloat16)
        ts[to, :] = -(sy[y : y + 1, :] * cz + cy[y : y + 1, :] * sz).astype(jnp.bfloat16)
    shift = turn_angle(ky + kz)
    rot[0:1, :] = jnp.cos(shift[:, :LANES])
    rot[1:2, :] = jnp.sin(shift[:, :LANES])

    def true_plane(plane):
        xs = plane
        for b, block_row in enumerate(rows_of_blocks):
            inside = (plane >= b * PX) & (plane < b * PX + PX)
            xs = jnp.where(inside, plane + (block_row - b) * PX, xs)
        return xs.astype(jnp.float32)

    xs = true_plane(lax.broadcasted_iota(jnp.int32, (NX, JS), 0))
    theta = turn_angle((ky + kz)[:, LANES:] - 2.0 * xs * ks[2:3, LANES:])
    ph[0] = jnp.cos(theta)
    ph[1] = jnp.sin(theta)
    r = lax.broadcasted_iota(jnp.int32, (2 * NX, 2 * NX), 0)
    c = lax.broadcasted_iota(jnp.int32, (2 * NX, 2 * NX), 1)
    low, left = r < NX, c < NX
    freq = jnp.where(low, r, r - NX).astype(jnp.float32)
    angle = turn_angle(2.0 * freq * true_plane(jnp.where(left, c, c - NX)))
    sine = jnp.sin(angle)
    table[...] = jnp.where(low == left, jnp.cos(angle), jnp.where(low, sine, -sine)).astype(jnp.bfloat16)


BLOCKS = 8
PX = NX // BLOCKS
PT = 3
YS = PAIRS + 8
PB = 16
MS = PB + 8


def density(vf, cbuf, b, plane, at, even, odd):
    cond = cbuf.at[b, plane]
    for v in range(NV):
        out = slice(at * PAIRS + v * CL, at * PAIRS + v * CL + CL)
        spread = lambda h: jnp.broadcast_to(vf[h, plane, v : v + 1, :], (CL, HALF)).astype(jnp.bfloat16)
        lo = spread(0) * cond[:, :HALF]
        hi = spread(1) * cond[:, HALF:]
        even[out, :] = lo + hi
        odd[out, :] = lo - hi


def transform(b, first, even, odd, tc, ts, rot, ph, y, sacc):
    a = jnp.dot(even[...], tc[...], preferred_element_type=jnp.float32)
    c = jnp.dot(odd[...], ts[...], preferred_element_type=jnp.float32)
    cosr, sinr = rot[0:1, :], rot[1:2, :]
    real, imag = sacc[0], sacc[1]
    for i in range(PT):
        x = b * PX + first + i
        rows = slice(i * PAIRS, i * PAIRS + PAIRS)
        am, cm = a[rows, :LANES], c[rows, :LANES]
        to = pl.ds(pl.multiple_of(x * YS, 8), PAIRS)
        for k, value in enumerate((cosr * am - sinr * cm, cosr * cm + sinr * am)):
            for h in range(LANES // 128):
                y[k, h, to, :] = value[:, h * 128 : h * 128 + 128]
        av, cv = a[rows, LANES:], c[rows, LANES:]
        cp, sp = ph[0, pl.ds(x, 1), :], ph[1, pl.ds(x, 1), :]
        real = real + (cp * av - sp * cv)
        imag = imag + (cp * cv + sp * av)
    sacc[0] = real
    sacc[1] = imag


def front_kernel(
    weights, cond, val, ks, m_out, slab_out,
    tc, ts, rot, ph, table, cbuf, vbuf, vf, even, odd, y, sacc, sl, mo, mb,
    lsem, cs, cr, vs, vr, gs, gr, ss, sr, fs, fr, ms,
):
    row, col = lax.axis_index("row"), lax.axis_index("col")
    yh, x = row // 4, row % 4
    z, yl, core = col // 4, (col // 2) % 2, col % 2
    zo = z + 1 - 2 * (z % 2)
    xp = {"row": yh * 4 + (x + 1) % 4, "col": col}
    xm = {"row": yh * 4 + (x + 3) % 4, "col": col}
    yc = {"row": (1 - yh) * 4 + x, "col": col}
    yv = {"row": (1 - yh) * 4 + x, "col": z * 4 + (1 - yl) * 2 + core}
    group = [
        {"row": row, "col": zo * 4 + yl * 2 + core},
        {"row": row, "col": z * 4 + yl * 2 + 1 - core},
        {"row": row, "col": zo * 4 + yl * 2 + 1 - core},
    ]
    across = [{"row": (row + k) % 8, "col": col} for k in range(1, 8)]
    part = core * 2 + z % 2

    own = [
        pltpu.make_async_copy(cond, cbuf.at[0], lsem.at[0]),
        pltpu.make_async_copy(val, vbuf.at[0], lsem.at[1]),
    ]
    for copy in own:
        copy.start()
    barrier = pltpu.get_barrier_semaphore()
    for peer in across + group + [yv]:
        pl.semaphore_signal(barrier, inc=1, device_id=peer, device_id_type=MESH)
    pl.semaphore_wait(barrier, 11)

    hops = [(0, 3, None), (0, 2, xp), (0, 1, xm), (3, 6, xp), (3, 5, xm), (2, 4, xp), (5, 7, xm)]
    hop_to = [hop[1] for hop in hops]

    def cond_hop(n):
        src, dst, peer = hops[n]
        return pltpu.make_async_remote_copy(
            cbuf.at[src] if src else cond, cbuf.at[dst], cs.at[n], cr.at[dst],
            device_id=peer or yc, device_id_type=MESH,
        )

    def val_hop(n):
        src, dst, peer = hops[n]
        return pltpu.make_async_remote_copy(
            vbuf.at[src, part] if src else val.at[part], vbuf.at[dst, part], vs.at[n], vr.at[dst],
            device_id=peer or yv, device_id_type=MESH,
        )

    def spread(b, j):
        return pltpu.make_async_remote_copy(
            vbuf.at[b, part], vbuf.at[b, part], gs.at[b * 3 + j], gr.at[b * 3 + j],
            device_id=group[j], device_id_type=MESH,
        )

    def land_val(b, *forward):
        val_hop(hop_to.index(b)).wait_recv()
        for n in forward:
            val_hop(n).start()
        for j in range(3):
            spread(b, j).start()

    def land(b, *forward):
        cond_hop(hop_to.index(b)).wait_recv()
        for n in forward:
            cond_hop(n).start()

    def ready(b):
        for j in range(3):
            spread(b, j).wait_recv()

    for n in range(3):
        val_hop(n).start()
    for n in range(3):
        cond_hop(n).start()
    sacc[...] = jnp.zeros_like(sacc)
    steps = [(0, 0), (0, 1), (0, 3), (1, 0), (0, 2), (1, 1), (1, 3), (1, 2)]
    make_tables(ks, [(yh + dy) % 2 * 4 + (x + dx) % 4 for dy, dx in steps], tc, ts, rot, ph, table)
    for copy in own:
        copy.wait()

    def block(b, carry):
        @pl.when(b == 1)
        def _():
            land_val(1)
            land_val(2, 5)
            land_val(3, 3, 4)
            land(2, 5)
            land(1)
            land(3, 3, 4)
            ready(1)

        @pl.when(b == 2)
        def _():
            land_val(4)
            land_val(5, 6)
            land_val(6)
            ready(2)

        @pl.when(b == 3)
        def _():
            land_val(7)
            ready(3)

        @pl.when(b == 4)
        def _():
            land(4)
            land(5, 6)
            ready(4)

        @pl.when(b == 5)
        def _():
            land(6)
            ready(5)

        @pl.when(b == 6)
        def _():
            ready(6)

        @pl.when(b == 7)
        def _():
            land(7)
            ready(7)

        def widen(j, carry):
            for q in range(4):
                vf[q % 2, (q // 2) * 3 + j] = vbuf[b, q, j].astype(jnp.float32)
            return carry

        lax.fori_loop(0, 3, widen, 0)

        def some(i, carry):
            for u in range(PT):
                density(vf, cbuf, b, i * PT + u, u, even, odd)
            transform(b, i * PT, even, odd, tc, ts, rot, ph, y, sacc)
            return carry

        lax.fori_loop(0, PX // PT, some, 0)
        return carry

    lax.fori_loop(0, BLOCKS, block, 0)

    for h in range(2):
        sl[h * PAIRS : h * PAIRS + PAIRS, :] = sacc[h].astype(jnp.bfloat16)
    keep = pltpu.make_async_copy(sl, slab_out.at[0, row], lsem.at[2])
    keep.start()

    def push(k):
        return pltpu.make_async_remote_copy(
            sl, slab_out.at[0, row], ss.at[k], sr.at[k], device_id=across[k], device_id_type=MESH
        )

    def hand(k):
        at = (row + 7 - k) % 8
        return pltpu.make_async_remote_copy(
            sl if k == 7 else slab_out.at[0, at], slab_out.at[1, at], fs.at[k], fr.at[k],
            device_id=group[1], device_id_type=MESH,
        )

    for k in range(7):
        push(k).start()
    hand(7).start()

    def chunk(i, carry):
        for k in range(7):

            @pl.when(i == 5 + k)
            def _():
                push(k).wait_recv()
                hand(k).start()

        slot = i % 2
        ps = pl.ds(pl.multiple_of(i * PB, PB), PB)
        out = pltpu.make_async_copy(mb.at[slot], m_out.at[:, ps, :], ms.at[slot])
        for p in range(PB):
            at = pl.ds(i * PB + p, NX, stride=YS)
            rhs = jnp.concatenate(
                [jnp.concatenate([y[k, 0, at, :], y[k, 1, at, :]], axis=1) for k in range(2)], axis=0
            ).astype(jnp.bfloat16)
            res = jnp.dot(table[...], rhs, preferred_element_type=jnp.float32) * weights[i * PB + p]
            for h in range(LANES // 128):
                mo[h, pl.ds(p, 2 * NX, stride=MS), :] = res[:, h * 128 : h * 128 + 128]

        @pl.when(i >= 2)
        def _():
            out.wait()

        for h in range(LANES // 128):
            lanes = slice(h * 128, h * 128 + 128)
            mb[slot, :, :, lanes] = mo[h].reshape(2 * NX, MS, 128)[:, :PB].astype(jnp.bfloat16)
        out.start()
        return carry

    lax.fori_loop(0, PAIRS // PB, chunk, 0)
    for slot in range(2):
        pltpu.make_async_copy(mb.at[slot], m_out.at[:, pl.ds(slot * PB, PB), :], ms.at[slot]).wait()
    keep.wait()
    for k in range(8):
        hand(k).wait_recv()
        hand(k).wait_send()
    for k in range(7):
        push(k).wait_send()
    for n in range(len(hops)):
        val_hop(n).wait_send()
        cond_hop(n).wait_send()
    for b in range(1, BLOCKS):
        for j in range(3):
            spread(b, j).wait_send()


def front(weights, cond, val, ks):
    dma = pltpu.SemaphoreType.DMA
    vmem = pl.BlockSpec(memory_space=pltpu.VMEM)
    hbm = pl.BlockSpec(memory_space=pl.ANY)
    bf = lambda *shape: pltpu.VMEM(shape, jnp.bfloat16)
    fl = lambda *shape: pltpu.VMEM(shape, jnp.float32)
    return pl.pallas_call(
        front_kernel,
        in_specs=[pl.BlockSpec(memory_space=pltpu.SMEM)] + [vmem] * 3,
        out_specs=[hbm, hbm],
        out_shape=[
            jax.ShapeDtypeStruct((2 * NX, PAIRS, LANES), jnp.bfloat16),
            jax.ShapeDtypeStruct((2, BLOCKS, 2 * PAIRS, JS), jnp.bfloat16),
        ],
        scratch_shapes=[
            bf(HALF, LANES + JS),
            bf(HALF, LANES + JS),
            fl(2, LANES),
            fl(2, NX, JS),
            bf(2 * NX, 2 * NX),
            bf(BLOCKS, PX, CL, CELLS),
            bf(BLOCKS, 4, PX // 2, NV, HALF),
            fl(2, PX, NV, HALF),
            bf(PT * PAIRS, HALF),
            bf(PT * PAIRS, HALF),
            fl(2, LANES // 128, NX * YS, 128),
            fl(2, PAIRS, JS),
            bf(2 * PAIRS, JS),
            fl(2, 2 * NX * MS, 128),
            bf(2, 2 * NX, PB, LANES),
            dma((3,)), dma((7,)), dma((8,)), dma((7,)), dma((8,)),
            dma((24,)), dma((24,)), dma((7,)), dma((7,)), dma((8,)), dma((8,)), dma((2,)),
        ],
        compiler_params=pltpu.CompilerParams(
            collective_id=2, has_side_effects=True, vmem_limit_bytes=VMEM_LIMIT
        ),
        name="front",
    )(weights, cond, val, ks)


GB = 320
QS = 2 * PAIRS // 128
G_DEV = 320
LO = 192
HI = G_DEV - LO
DEPTH = 16
UNROLL = 32


def pick_kernel(g_ref, m, out, mt, mi, sel, lhs, ms, os):
    def fetch(step):
        slot = step % DEPTH
        return pltpu.make_async_copy(m.at[:, step], mi.at[slot], ms.at[slot])

    for step in range(DEPTH):
        fetch(step).start()

    def turn(step, carry):
        fetch(step).wait()
        for h in range(2):
            for q in range(2):
                t = mi[step % DEPTH, h, q * 128 : q * 128 + 128, :].T.astype(jnp.float32)
                mt[pl.ds(step * (STK * QS) + h * 2 + q, STK, stride=QS), :] = t[:STK, :]

        @pl.when(step < NX - DEPTH)
        def _():
            fetch(step + DEPTH).start()

        return carry

    lax.fori_loop(0, NX, turn, 0, unroll=4)
    store = lambda n: pltpu.make_async_copy(lhs.at[n % 2], out.at[n], os.at[n % 2])

    def block(n, carry):
        def rows(i, carry):
            for u in range(UNROLL):
                g = g_ref[n * GB + i * UNROLL + u]
                to = pl.ds(pl.multiple_of((i * UNROLL + u) * QS, QS), QS)
                sel[to, :] = mt[pl.ds(pl.multiple_of(g * QS, QS), QS), :]
            return carry

        lax.fori_loop(0, GB // UNROLL, rows, 0)

        @pl.when(n >= 2)
        def _():
            store(n - 2).wait()

        for k in range(QS):
            lhs[n % 2, :, k * 128 : k * 128 + 128] = sel[pl.ds(k, GB, stride=QS), :].astype(jnp.bfloat16)
        store(n).start()
        return carry

    lax.fori_loop(0, G_ROW // GB, block, 0)
    for n in range(2):
        store(G_ROW // GB - 2 + n).wait()


def pick(gvec, m):
    dma = pltpu.SemaphoreType.DMA
    return pl.pallas_call(
        pick_kernel,
        in_specs=[pl.BlockSpec(memory_space=pltpu.SMEM), pl.BlockSpec(memory_space=pl.ANY)],
        out_specs=pl.BlockSpec(memory_space=pl.ANY),
        out_shape=jax.ShapeDtypeStruct((G_ROW // GB, GB, 2 * PAIRS), jnp.bfloat16),
        scratch_shapes=[
            pltpu.VMEM((NX * STK * QS, 128), jnp.float32),
            pltpu.VMEM((DEPTH, 2, PAIRS, LANES), jnp.bfloat16),
            pltpu.VMEM((GB * QS, 128), jnp.float32),
            pltpu.VMEM((2, GB, 2 * PAIRS), jnp.bfloat16),
            dma((DEPTH,)), dma((2,)),
        ],
        compiler_params=pltpu.CompilerParams(vmem_limit_bytes=VMEM_LIMIT),
        name="pick",
    )(gvec, m)


def add_rows(dst, a, b, rows, step=32):
    def one(i, carry):
        at = pl.ds(pl.multiple_of(i * step, step), step)
        dst[at, :] = (a[at, :].astype(jnp.float32) + b[at, :].astype(jnp.float32)).astype(dst.dtype)
        return carry

    lax.fori_loop(0, rows // step, one, 0)


def back_kernel(
    rows, slab, out, sw, ours, theirs, acc, zr2, yr1, zr1, yr2,
    ms, s1, d1, sz2, dz2, sy1, dy1, sz1, dz1, sy2, dy2,
):
    row, col = lax.axis_index("row"), lax.axis_index("col")
    z, yl, core = col // 4, (col // 2) % 2, col % 2
    core_peer = {"row": row, "col": z * 4 + yl * 2 + (1 - core)}
    y_peer = {"row": row, "col": z * 4 + (1 - yl) * 2 + core}
    z_peer = lambda k: {"row": row, "col": ((z + k) % 4) * 4 + yl * 2 + core}
    barrier = pltpu.get_barrier_semaphore()
    for peer in (core_peer, y_peer, z_peer(1), z_peer(2), z_peer(3)):
        pl.semaphore_signal(barrier, inc=1, device_id=peer, device_id_type=MESH)

    def place(n):
        k, s = (n // 2 + 1) % 4, n % 2
        return ((z + k) % 4) * 4 + (yl * s + (1 - yl) * (1 - s)) * 2

    load = lambda n: pltpu.make_async_copy(rows.at[place(n) + core], ours.at[n], ms.at[n])
    for n in range(8):
        load(n).start()
    pl.semaphore_wait(barrier, 5)

    scale = -1.0 / math.sqrt(NV * NC)
    def remote(src, dst, ss, ds, peer):
        return pltpu.make_async_remote_copy(src, dst, ss, ds, device_id=peer, device_id_type=MESH)

    lo, hi = pl.ds(0, LO), pl.ds(LO, HI)
    first = lambda n: remote(rows.at[place(n) + 1 - core], theirs.at[n], s1.at[n], d1.at[n], core_peer)
    for n in range(2):
        first(n).start()
    for h in range(2):
        for r in range(NS // JS):
            sw[h * 2 * PAIRS : (h + 1) * 2 * PAIRS, r * JS : r * JS + JS] = slab[h, r]
    along_z = lambda k, s: remote(
        acc.at[(k + 3) % 4 * 2 + s, hi], zr2.at[(k - 1) * 2 + s], sz2.at[(k - 1) * 2 + s], dz2.at[(k - 1) * 2 + s], z_peer(k)
    )
    along_y = lambda k: remote(acc.at[(k + 3) % 4 * 2, lo], yr1.at[k], sy1.at[k], dy1.at[k], y_peer)
    last_z = lambda k: remote(acc.at[(k + 3) % 4 * 2 + 1, lo], zr1.at[k - 1], sz1.at[k - 1], dz1.at[k - 1], z_peer(k))

    def slot(n, carry):
        k, s = (n // 2 + 1) % 4, n % 2
        load(n).wait()
        first(n).wait_recv()

        @pl.when(n < 6)
        def _():
            first(n + 2).start()

        lhs = jnp.concatenate([ours[n], theirs[n]], axis=1)
        acc[n] = (jnp.dot(lhs, sw[...], preferred_element_type=jnp.float32) * scale).astype(jnp.bfloat16)

        @pl.when(n < 6)
        def _():
            along_z(k, s).start()

        @pl.when(s == 0)
        def _():
            along_y(k).start()

        return carry

    lax.fori_loop(0, 8, slot, 0)
    for k in (1, 2, 3, 0):
        along_y(k).wait_recv()
        if k:
            at = acc.at[(k + 3) % 4 * 2 + 1]
            add_rows(at, at, yr1.at[k], LO)
            last_z(k).start()
    for k in (1, 2, 3):
        along_z(k, 0).wait_recv()

    def total(i, base, terms):
        at = pl.ds(pl.multiple_of(i * 16, 16), 16)
        value = base[at, :].astype(jnp.float32)
        for ref in terms:
            value = value + ref[at, :].astype(jnp.float32)
        return at, value

    def across(i, carry):
        at, value = total(i, acc.at[6, hi], [zr2.at[0], zr2.at[2], zr2.at[4]])
        yr2[0, at, :] = value.astype(jnp.bfloat16)
        return carry

    lax.fori_loop(0, HI // 16, across, 0)
    last_y = remote(yr2.at[0], yr2.at[1], sy2.at[0], dy2.at[0], y_peer)
    last_y.start()
    for k in (1, 2, 3):
        last_z(k).wait_recv()

    def low(i, carry):
        at, value = total(i, acc.at[7, lo], [yr1.at[0], zr1.at[0], zr1.at[1], zr1.at[2]])
        out[at, :] = value
        return carry

    lax.fori_loop(0, LO // 16, low, 0)
    for k in (1, 2, 3):
        along_z(k, 1).wait_recv()
    last_y.wait_recv()

    def high(i, carry):
        at, value = total(i, acc.at[7, hi], [zr2.at[1], zr2.at[3], zr2.at[5], yr2.at[1]])
        out[pl.ds(pl.multiple_of(LO + i * 16, 16), 16), :] = value
        return carry

    lax.fori_loop(0, HI // 16, high, 0)
    for n in range(8):
        first(n).wait_send()
    for k in range(4):
        along_y(k).wait_send()
        if k:
            last_z(k).wait_send()
            along_z(k, 0).wait_send()
            along_z(k, 1).wait_send()
    last_y.wait_send()


def back(rows, slab):
    dma = pltpu.SemaphoreType.DMA
    vmem = pl.BlockSpec(memory_space=pltpu.VMEM)
    part = lambda n, rows: pltpu.VMEM((n, rows, NS), jnp.bfloat16)
    return pl.pallas_call(
        back_kernel,
        in_specs=[pl.BlockSpec(memory_space=pl.ANY), vmem],
        out_specs=vmem,
        out_shape=jax.ShapeDtypeStruct((G_DEV, NS), jnp.float32),
        scratch_shapes=[
            pltpu.VMEM((4 * PAIRS, NS), jnp.bfloat16),
            pltpu.VMEM((8, GB, 2 * PAIRS), jnp.bfloat16),
            pltpu.VMEM((8, GB, 2 * PAIRS), jnp.bfloat16),
            pltpu.VMEM((8, G_DEV, NS), jnp.bfloat16),
            part(6, HI), part(4, LO), part(3, LO), part(2, HI),
            dma((8,)), dma((8,)), dma((8,)), dma((6,)), dma((6,)), dma((4,)), dma((4,)),
            dma((3,)), dma((3,)), dma((1,)), dma((1,)),
        ],
        compiler_params=pltpu.CompilerParams(
            collective_id=3, has_side_effects=True, vmem_limit_bytes=VMEM_LIMIT
        ),
        name="back",
    )(rows, slab)


def places_kernel(mine, cond, val, out, cond_out, val_out, send_sem, recv_sem):
    row, col = lax.axis_index("row"), lax.axis_index("col")
    barrier = pltpu.get_barrier_semaphore()
    peers = [{"row": (row + k) % 8, "col": col} for k in range(1, 8)]
    for peer in peers:
        pl.semaphore_signal(barrier, inc=1, device_id=peer, device_id_type=MESH)
    pl.semaphore_wait(barrier, 7)
    copies = []
    for k, peer in enumerate(peers):
        copies.append(
            pltpu.make_async_remote_copy(
                mine, out.at[row], send_sem.at[k], recv_sem.at[k], device_id=peer, device_id_type=MESH
            )
        )
        copies[-1].start()
    out[row] = mine[...]
    r = lax.broadcasted_iota(jnp.int32, (128, 128), 0)
    c = lax.broadcasted_iota(jnp.int32, (128, 128), 1)
    back = (r + c == 127).astype(jnp.bfloat16)
    half = PX // 2
    cond_out[:, :, :HALF] = cond[:, :, :HALF]
    for p in range(2):
        val_out[2 * p] = val[p * half : p * half + half, :, :HALF]
    for b in range(HALF // 128):
        source = slice(CELLS - b * 128 - 128, CELLS - b * 128)
        to = slice(b * 128, b * 128 + 128)
        flip = lambda ref: jnp.dot(
            ref[:, :, source].reshape(PX * CL, 128), back, preferred_element_type=jnp.float32
        ).astype(jnp.bfloat16).reshape(PX, CL, 128)
        cond_out[:, :, HALF + b * 128 : HALF + b * 128 + 128] = flip(cond)
        turned = flip(val)
        for p in range(2):
            val_out[2 * p + 1, :, :, to] = turned[p * half : p * half + half]
    for copy in copies:
        copy.wait_recv()
    for copy in copies:
        copy.wait_send()


def places(mine, cond, val):
    return pl.pallas_call(
        places_kernel,
        in_specs=[pl.BlockSpec(memory_space=pltpu.VMEM)] * 3,
        out_specs=[pl.BlockSpec(memory_space=pltpu.VMEM)] * 3,
        out_shape=[
            jax.ShapeDtypeStruct((8, G_ROW // 128, 128), jnp.int32),
            jax.ShapeDtypeStruct((PX, CL, CELLS), jnp.bfloat16),
            jax.ShapeDtypeStruct((4, PX // 2, NV, HALF), jnp.bfloat16),
        ],
        scratch_shapes=[pltpu.SemaphoreType.DMA((7,)), pltpu.SemaphoreType.DMA((7,))],
        compiler_params=pltpu.CompilerParams(collective_id=1, has_side_effects=True),
        name="places",
    )(mine, cond, val)


def body(psi_val, psi_cond, energy_val, energy_cond, stick_map, gvec_map, slab_index):
    row = lax.axis_index("row")
    mine = lax.dynamic_slice(stick_map, (row * STK,), (STK,))
    cols = lax.dynamic_slice(slab_index, (row * JS,), (JS,))
    maps, cond, val = places(
        gvec_map.reshape(G_ROW // 128, 128), psi_cond.transpose(1, 0, 2), psi_val.transpose(1, 0, 2)
    )
    maps = maps.reshape(-1)
    place = jnp.take(maps, cols)
    col_kx = place // STK
    col_stick = jnp.take(stick_map, cols // G_ROW * STK + place % STK)
    pad = jnp.zeros((LANES - STK,), jnp.int32)
    flat = jnp.concatenate([mine, pad, col_stick])
    ky, kz = flat // NZ, flat % NZ
    full_kx = jnp.concatenate([jnp.zeros((LANES,), jnp.int32), col_kx])
    ks = jnp.stack([ky, kz, full_kx]).astype(jnp.float32)
    weight = (2.0 / (NY * NZ * NX)) / (energy_cond[None, :] - energy_val[:, None])
    m, slab = front(weight.reshape(PAIRS), cond, val, ks)
    return back(pick(gvec_map, m.reshape(2, NX, PAIRS, LANES)), slab)


def solution(mesh):
    in_specs = (P(None, "row", None), P("col", "row", None), P(), P("col"), P(), P("row"), P())
    out_specs = P(("row", "col"), None)
    return jax.shard_map(body, mesh=mesh, in_specs=in_specs, out_specs=out_specs, check_vma=False)
```

```python
import math

import jax
import jax.numpy as jnp
from jax import lax
from jax.experimental import pallas as pl
from jax.experimental.pallas import tpu as pltpu
from jax.sharding import PartitionSpec as P

NX = 48
NY = 48
NZ = 48
CELLS = NY * NZ
HALF = CELLS // 2
NC = 256
NV = 16
CL = 16
PAIRS = NV * CL
STK = 192
G_ROW = 5120
NS = 1024
JS = 128
XB = 4
LANES = 256
VMEM_LIMIT = 60 * 1024 * 1024
MESH = pl.DeviceIdType.MESH


def turn_angle(t):
    return (t - 96.0 * jnp.floor((t + 0.5) * (1.0 / 96.0))) * (math.pi / 48.0)


def make_tables(ks, rows_of_blocks, tc, ts, rot, ph, table):
    width = LANES + JS
    ky, kz = ks[0:1, :], ks[1:2, :]
    odd = lambda n: 2.0 * lax.broadcasted_iota(jnp.int32, (n, width), 0).astype(jnp.float32) + 1.0
    ay, az = turn_angle(odd(NY // 2) * ky), turn_angle(odd(NZ) * kz)
    cy, sy, cz, sz = jnp.cos(ay), jnp.sin(ay), jnp.cos(az), jnp.sin(az)
    for y in range(NY // 2):
        to = slice(y * NZ, y * NZ + NZ)
        tc[to, :] = (cy[y : y + 1, :] * cz - sy[y : y + 1, :] * sz).astype(jnp.bfloat16)
        ts[to, :] = -(sy[y : y + 1, :] * cz + cy[y : y + 1, :] * sz).astype(jnp.bfloat16)
    shift = turn_angle(ky + kz)
    rot[0:1, :] = jnp.cos(shift[:, :LANES])
    rot[1:2, :] = jnp.sin(shift[:, :LANES])

    def true_plane(plane):
        xs = plane
        for b, block_row in enumerate(rows_of_blocks):
            inside = (plane >= b * PX) & (plane < b * PX + PX)
            xs = jnp.where(inside, plane + (block_row - b) * PX, xs)
        return xs.astype(jnp.float32)

    xs = true_plane(lax.broadcasted_iota(jnp.int32, (NX, JS), 0))
    theta = turn_angle((ky + kz)[:, LANES:] - 2.0 * xs * ks[2:3, LANES:])
    ph[0] = jnp.cos(theta)
    ph[1] = jnp.sin(theta)
    r = lax.broadcasted_iota(jnp.int32, (2 * NX, 2 * NX), 0)
    c = lax.broadcasted_iota(jnp.int32, (2 * NX, 2 * NX), 1)
    low, left = r < NX, c < NX
    freq = jnp.where(low, r, r - NX).astype(jnp.float32)
    angle = turn_angle(2.0 * freq * true_plane(jnp.where(left, c, c - NX)))
    sine = jnp.sin(angle)
    table[...] = jnp.where(low == left, jnp.cos(angle), jnp.where(low, sine, -sine)).astype(jnp.bfloat16)


BLOCKS = 8
PX = NX // BLOCKS
PT = 3
YS = PAIRS + 8
PB = 16
MS = PB + 8


def density(vf, cbuf, b, plane, at, even, odd):
    cond = cbuf.at[b, plane]
    for v in range(NV):
        out = slice(at * PAIRS + v * CL, at * PAIRS + v * CL + CL)
        spread = lambda h: jnp.broadcast_to(vf[h, plane, v : v + 1, :], (CL, HALF)).astype(jnp.bfloat16)
        lo = spread(0) * cond[:, :HALF]
        hi = spread(1) * cond[:, HALF:]
        even[out, :] = lo + hi
        odd[out, :] = lo - hi


def transform(b, first, even, odd, tc, ts, rot, ph, y, sacc):
    a = jnp.dot(even[...], tc[...], preferred_element_type=jnp.float32)
    c = jnp.dot(odd[...], ts[...], preferred_element_type=jnp.float32)
    cosr, sinr = rot[0:1, :], rot[1:2, :]
    real, imag = sacc[0], sacc[1]
    for i in range(PT):
        x = b * PX + first + i
        rows = slice(i * PAIRS, i * PAIRS + PAIRS)
        am, cm = a[rows, :LANES], c[rows, :LANES]
        to = pl.ds(pl.multiple_of(x * YS, 8), PAIRS)
        for k, value in enumerate((cosr * am - sinr * cm, cosr * cm + sinr * am)):
            for h in range(LANES // 128):
                y[k, h, to, :] = value[:, h * 128 : h * 128 + 128]
        av, cv = a[rows, LANES:], c[rows, LANES:]
        cp, sp = ph[0, pl.ds(x, 1), :], ph[1, pl.ds(x, 1), :]
        real = real + (cp * av - sp * cv)
        imag = imag + (cp * cv + sp * av)
    sacc[0] = real
    sacc[1] = imag


def front_kernel(
    weights, cond, val, ks, m_out, slab_out,
    tc, ts, rot, ph, table, cbuf, vbuf, vf, even, odd, y, sacc, sl, mo, mb,
    lsem, cs, cr, vs, vr, gs, gr, ss, sr, fs, fr, ms,
):
    row, col = lax.axis_index("row"), lax.axis_index("col")
    yh, x = row // 4, row % 4
    z, yl, core = col // 4, (col // 2) % 2, col % 2
    zo = z + 1 - 2 * (z % 2)
    xp = {"row": yh * 4 + (x + 1) % 4, "col": col}
    xm = {"row": yh * 4 + (x + 3) % 4, "col": col}
    yc = {"row": (1 - yh) * 4 + x, "col": col}
    yv = {"row": (1 - yh) * 4 + x, "col": z * 4 + (1 - yl) * 2 + core}
    group = [
        {"row": row, "col": zo * 4 + yl * 2 + core},
        {"row": row, "col": z * 4 + yl * 2 + 1 - core},
        {"row": row, "col": zo * 4 + yl * 2 + 1 - core},
    ]
    across = [{"row": (row + k) % 8, "col": col} for k in range(1, 8)]
    part = core * 2 + z % 2

    own = [
        pltpu.make_async_copy(cond, cbuf.at[0], lsem.at[0]),
        pltpu.make_async_copy(val, vbuf.at[0], lsem.at[1]),
    ]
    for copy in own:
        copy.start()
    barrier = pltpu.get_barrier_semaphore()
    for peer in across + group + [yv]:
        pl.semaphore_signal(barrier, inc=1, device_id=peer, device_id_type=MESH)
    pl.semaphore_wait(barrier, 11)

    hops = [(0, 3, None), (0, 2, xp), (0, 1, xm), (3, 6, xp), (3, 5, xm), (2, 4, xp), (5, 7, xm)]
    hop_to = [hop[1] for hop in hops]

    def cond_hop(n):
        src, dst, peer = hops[n]
        return pltpu.make_async_remote_copy(
            cbuf.at[src] if src else cond, cbuf.at[dst], cs.at[n], cr.at[dst],
            device_id=peer or yc, device_id_type=MESH,
        )

    def val_hop(n):
        src, dst, peer = hops[n]
        return pltpu.make_async_remote_copy(
            vbuf.at[src, part] if src else val.at[part], vbuf.at[dst, part], vs.at[n], vr.at[dst],
            device_id=peer or yv, device_id_type=MESH,
        )

    def spread(b, j):
        return pltpu.make_async_remote_copy(
            vbuf.at[b, part], vbuf.at[b, part], gs.at[b * 3 + j], gr.at[b * 3 + j],
            device_id=group[j], device_id_type=MESH,
        )

    def land_val(b, *forward):
        val_hop(hop_to.index(b)).wait_recv()
        for n in forward:
            val_hop(n).start()
        for j in range(3):
            spread(b, j).start()

    def land(b, *forward):
        cond_hop(hop_to.index(b)).wait_recv()
        for n in forward:
            cond_hop(n).start()

    def ready(b):
        for j in range(3):
            spread(b, j).wait_recv()

    for n in range(3):
        val_hop(n).start()
    for n in range(3):
        cond_hop(n).start()
    sacc[...] = jnp.zeros_like(sacc)
    steps = [(0, 0), (0, 1), (0, 3), (1, 0), (0, 2), (1, 1), (1, 3), (1, 2)]
    make_tables(ks, [(yh + dy) % 2 * 4 + (x + dx) % 4 for dy, dx in steps], tc, ts, rot, ph, table)
    for copy in own:
        copy.wait()

    def block(b, carry):
        @pl.when(b == 1)
        def _():
            land_val(1)
            land_val(2, 5)
            land_val(3, 3, 4)
            land(2, 5)
            land(1)
            land(3, 3, 4)
            ready(1)

        @pl.when(b == 2)
        def _():
            land_val(4)
            land_val(5, 6)
            land_val(6)
            ready(2)

        @pl.when(b == 3)
        def _():
            land_val(7)
            ready(3)

        @pl.when(b == 4)
        def _():
            land(4)
            land(5, 6)
            ready(4)

        @pl.when(b == 5)
        def _():
            land(6)
            ready(5)

        @pl.when(b == 6)
        def _():
            ready(6)

        @pl.when(b == 7)
        def _():
            land(7)
            ready(7)

        def widen(j, carry):
            for q in range(4):
                vf[q % 2, (q // 2) * 3 + j] = vbuf[b, q, j].astype(jnp.float32)
            return carry

        lax.fori_loop(0, 3, widen, 0)

        def some(i, carry):
            for u in range(PT):
                density(vf, cbuf, b, i * PT + u, u, even, odd)
            transform(b, i * PT, even, odd, tc, ts, rot, ph, y, sacc)
            return carry

        lax.fori_loop(0, PX // PT, some, 0)
        return carry

    lax.fori_loop(0, BLOCKS, block, 0)

    for h in range(2):
        sl[h * PAIRS : h * PAIRS + PAIRS, :] = sacc[h].astype(jnp.bfloat16)
    keep = pltpu.make_async_copy(sl, slab_out.at[0, row], lsem.at[2])
    keep.start()

    def push(k):
        return pltpu.make_async_remote_copy(
            sl, slab_out.at[0, row], ss.at[k], sr.at[k], device_id=across[k], device_id_type=MESH
        )

    def hand(k):
        at = (row + 7 - k) % 8
        return pltpu.make_async_remote_copy(
            sl if k == 7 else slab_out.at[0, at], slab_out.at[1, at], fs.at[k], fr.at[k],
            device_id=group[1], device_id_type=MESH,
        )

    for k in range(7):
        push(k).start()
    hand(7).start()

    def chunk(i, carry):
        for k in range(7):

            @pl.when(i == 5 + k)
            def _():
                push(k).wait_recv()
                hand(k).start()

        slot = i % 2
        ps = pl.ds(pl.multiple_of(i * PB, PB), PB)
        out = pltpu.make_async_copy(mb.at[slot], m_out.at[:, ps, :], ms.at[slot])
        for p in range(PB):
            at = pl.ds(i * PB + p, NX, stride=YS)
            rhs = jnp.concatenate(
                [jnp.concatenate([y[k, 0, at, :], y[k, 1, at, :]], axis=1) for k in range(2)], axis=0
            ).astype(jnp.bfloat16)
            res = jnp.dot(table[...], rhs, preferred_element_type=jnp.float32) * weights[i * PB + p]
            for h in range(LANES // 128):
                mo[h, pl.ds(p, 2 * NX, stride=MS), :] = res[:, h * 128 : h * 128 + 128]

        @pl.when(i >= 2)
        def _():
            out.wait()

        for h in range(LANES // 128):
            lanes = slice(h * 128, h * 128 + 128)
            mb[slot, :, :, lanes] = mo[h].reshape(2 * NX, MS, 128)[:, :PB].astype(jnp.bfloat16)
        out.start()
        return carry

    lax.fori_loop(0, PAIRS // PB, chunk, 0)
    for slot in range(2):
        pltpu.make_async_copy(mb.at[slot], m_out.at[:, pl.ds(slot * PB, PB), :], ms.at[slot]).wait()
    keep.wait()
    for k in range(8):
        hand(k).wait_recv()
        hand(k).wait_send()
    for k in range(7):
        push(k).wait_send()
    for n in range(len(hops)):
        val_hop(n).wait_send()
        cond_hop(n).wait_send()
    for b in range(1, BLOCKS):
        for j in range(3):
            spread(b, j).wait_send()


def front(weights, cond, val, ks):
    dma = pltpu.SemaphoreType.DMA
    vmem = pl.BlockSpec(memory_space=pltpu.VMEM)
    hbm = pl.BlockSpec(memory_space=pl.ANY)
    bf = lambda *shape: pltpu.VMEM(shape, jnp.bfloat16)
    fl = lambda *shape: pltpu.VMEM(shape, jnp.float32)
    return pl.pallas_call(
        front_kernel,
        in_specs=[pl.BlockSpec(memory_space=pltpu.SMEM)] + [vmem] * 3,
        out_specs=[hbm, hbm],
        out_shape=[
            jax.ShapeDtypeStruct((2 * NX, PAIRS, LANES), jnp.bfloat16),
            jax.ShapeDtypeStruct((2, BLOCKS, 2 * PAIRS, JS), jnp.bfloat16),
        ],
        scratch_shapes=[
            bf(HALF, LANES + JS),
            bf(HALF, LANES + JS),
            fl(2, LANES),
            fl(2, NX, JS),
            bf(2 * NX, 2 * NX),
            bf(BLOCKS, PX, CL, CELLS),
            bf(BLOCKS, 4, PX // 2, NV, HALF),
            fl(2, PX, NV, HALF),
            bf(PT * PAIRS, HALF),
            bf(PT * PAIRS, HALF),
            fl(2, LANES // 128, NX * YS, 128),
            fl(2, PAIRS, JS),
            bf(2 * PAIRS, JS),
            fl(2, 2 * NX * MS, 128),
            bf(2, 2 * NX, PB, LANES),
            dma((3,)), dma((7,)), dma((8,)), dma((7,)), dma((8,)),
            dma((24,)), dma((24,)), dma((7,)), dma((7,)), dma((8,)), dma((8,)), dma((2,)),
        ],
        compiler_params=pltpu.CompilerParams(
            collective_id=2, has_side_effects=True, vmem_limit_bytes=VMEM_LIMIT
        ),
        name="front",
    )(weights, cond, val, ks)


GB = 320
QS = 2 * PAIRS // 128
G_DEV = 320
LO = 192
HI = G_DEV - LO
DEPTH = 24
UNROLL = 64


def pick_kernel(g_ref, m, out, mt, mi, sel, lhs, ms, os):
    def fetch(step):
        slot = step % DEPTH
        return pltpu.make_async_copy(m.at[:, step], mi.at[slot], ms.at[slot])

    for step in range(DEPTH):
        fetch(step).start()

    def turn(step, carry):
        fetch(step).wait()
        for h in range(2):
            for q in range(2):
                t = mi[step % DEPTH, h, q * 128 : q * 128 + 128, :].T.astype(jnp.float32)
                mt[pl.ds(step * (STK * QS) + h * 2 + q, STK, stride=QS), :] = t[:STK, :]

        @pl.when(step < NX - DEPTH)
        def _():
            fetch(step + DEPTH).start()

        return carry

    lax.fori_loop(0, NX, turn, 0, unroll=8)
    store = lambda n: pltpu.make_async_copy(lhs.at[n % 2], out.at[n], os.at[n % 2])

    def block(n, carry):
        def rows(i, carry):
            for u in range(UNROLL):
                g = g_ref[n * GB + i * UNROLL + u]
                to = pl.ds(pl.multiple_of((i * UNROLL + u) * QS, QS), QS)
                sel[to, :] = mt[pl.ds(pl.multiple_of(g * QS, QS), QS), :]
            return carry

        lax.fori_loop(0, GB // UNROLL, rows, 0)

        @pl.when(n >= 2)
        def _():
            store(n - 2).wait()

        for k in range(QS):
            lhs[n % 2, :, k * 128 : k * 128 + 128] = sel[pl.ds(k, GB, stride=QS), :].astype(jnp.bfloat16)
        store(n).start()
        return carry

    lax.fori_loop(0, G_ROW // GB, block, 0)
    for n in range(2):
        store(G_ROW // GB - 2 + n).wait()


def pick(gvec, m):
    dma = pltpu.SemaphoreType.DMA
    return pl.pallas_call(
        pick_kernel,
        in_specs=[pl.BlockSpec(memory_space=pltpu.SMEM), pl.BlockSpec(memory_space=pl.ANY)],
        out_specs=pl.BlockSpec(memory_space=pl.ANY),
        out_shape=jax.ShapeDtypeStruct((G_ROW // GB, GB, 2 * PAIRS), jnp.bfloat16),
        scratch_shapes=[
            pltpu.VMEM((NX * STK * QS, 128), jnp.float32),
            pltpu.VMEM((DEPTH, 2, PAIRS, LANES), jnp.bfloat16),
            pltpu.VMEM((GB * QS, 128), jnp.float32),
            pltpu.VMEM((2, GB, 2 * PAIRS), jnp.bfloat16),
            dma((DEPTH,)), dma((2,)),
        ],
        compiler_params=pltpu.CompilerParams(vmem_limit_bytes=VMEM_LIMIT),
        name="pick",
    )(gvec, m)


def add_rows(dst, a, b, rows, step=32):
    def one(i, carry):
        at = pl.ds(pl.multiple_of(i * step, step), step)
        dst[at, :] = (a[at, :].astype(jnp.float32) + b[at, :].astype(jnp.float32)).astype(dst.dtype)
        return carry

    lax.fori_loop(0, rows // step, one, 0)


def back_kernel(
    rows, slab, out, sw, ours, theirs, acc, zr2, yr1, zr1, yr2,
    ms, s1, d1, sz2, dz2, sy1, dy1, sz1, dz1, sy2, dy2,
):
    row, col = lax.axis_index("row"), lax.axis_index("col")
    z, yl, core = col // 4, (col // 2) % 2, col % 2
    core_peer = {"row": row, "col": z * 4 + yl * 2 + (1 - core)}
    y_peer = {"row": row, "col": z * 4 + (1 - yl) * 2 + core}
    z_peer = lambda k: {"row": row, "col": ((z + k) % 4) * 4 + yl * 2 + core}
    barrier = pltpu.get_barrier_semaphore()
    for peer in (core_peer, y_peer, z_peer(1), z_peer(2), z_peer(3)):
        pl.semaphore_signal(barrier, inc=1, device_id=peer, device_id_type=MESH)

    def place(n):
        k, s = (n // 2 + 1) % 4, n % 2
        return ((z + k) % 4) * 4 + (yl * s + (1 - yl) * (1 - s)) * 2

    load = lambda n: pltpu.make_async_copy(rows.at[place(n) + core], ours.at[n], ms.at[n])
    for n in range(8):
        load(n).start()
    pl.semaphore_wait(barrier, 5)

    scale = -1.0 / math.sqrt(NV * NC)
    def remote(src, dst, ss, ds, peer):
        return pltpu.make_async_remote_copy(src, dst, ss, ds, device_id=peer, device_id_type=MESH)

    lo, hi = pl.ds(0, LO), pl.ds(LO, HI)
    first = lambda n: remote(rows.at[place(n) + 1 - core], theirs.at[n], s1.at[n], d1.at[n], core_peer)
    for n in range(2):
        first(n).start()
    for h in range(2):
        for r in range(NS // JS):
            sw[h * 2 * PAIRS : (h + 1) * 2 * PAIRS, r * JS : r * JS + JS] = slab[h, r]
    along_z = lambda k, s: remote(
        acc.at[(k + 3) % 4 * 2 + s, hi], zr2.at[(k - 1) * 2 + s], sz2.at[(k - 1) * 2 + s], dz2.at[(k - 1) * 2 + s], z_peer(k)
    )
    along_y = lambda k: remote(acc.at[(k + 3) % 4 * 2, lo], yr1.at[k], sy1.at[k], dy1.at[k], y_peer)
    last_z = lambda k: remote(acc.at[(k + 3) % 4 * 2 + 1, lo], zr1.at[k - 1], sz1.at[k - 1], dz1.at[k - 1], z_peer(k))

    def slot(n, carry):
        k, s = (n // 2 + 1) % 4, n % 2
        load(n).wait()
        first(n).wait_recv()

        @pl.when(n < 6)
        def _():
            first(n + 2).start()

        lhs = jnp.concatenate([ours[n], theirs[n]], axis=1)
        acc[n] = (jnp.dot(lhs, sw[...], preferred_element_type=jnp.float32) * scale).astype(jnp.bfloat16)

        @pl.when(n < 6)
        def _():
            along_z(k, s).start()

        @pl.when(s == 0)
        def _():
            along_y(k).start()

        return carry

    lax.fori_loop(0, 8, slot, 0)
    for k in (1, 2, 3, 0):
        along_y(k).wait_recv()
        if k:
            at = acc.at[(k + 3) % 4 * 2 + 1]
            add_rows(at, at, yr1.at[k], LO)
            last_z(k).start()
    for k in (1, 2, 3):
        along_z(k, 0).wait_recv()

    def total(i, base, terms):
        at = pl.ds(pl.multiple_of(i * 16, 16), 16)
        value = base[at, :].astype(jnp.float32)
        for ref in terms:
            value = value + ref[at, :].astype(jnp.float32)
        return at, value

    def across(i, carry):
        at, value = total(i, acc.at[6, hi], [zr2.at[0], zr2.at[2], zr2.at[4]])
        yr2[0, at, :] = value.astype(jnp.bfloat16)
        return carry

    lax.fori_loop(0, HI // 16, across, 0)
    last_y = remote(yr2.at[0], yr2.at[1], sy2.at[0], dy2.at[0], y_peer)
    last_y.start()
    for k in (1, 2, 3):
        last_z(k).wait_recv()

    def low(i, carry):
        at, value = total(i, acc.at[7, lo], [yr1.at[0], zr1.at[0], zr1.at[1], zr1.at[2]])
        out[at, :] = value
        return carry

    lax.fori_loop(0, LO // 16, low, 0)
    for k in (1, 2, 3):
        along_z(k, 1).wait_recv()
    last_y.wait_recv()

    def high(i, carry):
        at, value = total(i, acc.at[7, hi], [zr2.at[1], zr2.at[3], zr2.at[5], yr2.at[1]])
        out[pl.ds(pl.multiple_of(LO + i * 16, 16), 16), :] = value
        return carry

    lax.fori_loop(0, HI // 16, high, 0)
    for n in range(8):
        first(n).wait_send()
    for k in range(4):
        along_y(k).wait_send()
        if k:
            last_z(k).wait_send()
            along_z(k, 0).wait_send()
            along_z(k, 1).wait_send()
    last_y.wait_send()


def back(rows, slab):
    dma = pltpu.SemaphoreType.DMA
    vmem = pl.BlockSpec(memory_space=pltpu.VMEM)
    part = lambda n, rows: pltpu.VMEM((n, rows, NS), jnp.bfloat16)
    return pl.pallas_call(
        back_kernel,
        in_specs=[pl.BlockSpec(memory_space=pl.ANY), vmem],
        out_specs=vmem,
        out_shape=jax.ShapeDtypeStruct((G_DEV, NS), jnp.float32),
        scratch_shapes=[
            pltpu.VMEM((4 * PAIRS, NS), jnp.bfloat16),
            pltpu.VMEM((8, GB, 2 * PAIRS), jnp.bfloat16),
            pltpu.VMEM((8, GB, 2 * PAIRS), jnp.bfloat16),
            pltpu.VMEM((8, G_DEV, NS), jnp.bfloat16),
            part(6, HI), part(4, LO), part(3, LO), part(2, HI),
            dma((8,)), dma((8,)), dma((8,)), dma((6,)), dma((6,)), dma((4,)), dma((4,)),
            dma((3,)), dma((3,)), dma((1,)), dma((1,)),
        ],
        compiler_params=pltpu.CompilerParams(
            collective_id=3, has_side_effects=True, vmem_limit_bytes=VMEM_LIMIT
        ),
        name="back",
    )(rows, slab)


def places_kernel(mine, cond, val, out, cond_out, val_out, send_sem, recv_sem):
    row, col = lax.axis_index("row"), lax.axis_index("col")
    barrier = pltpu.get_barrier_semaphore()
    peers = [{"row": (row + k) % 8, "col": col} for k in range(1, 8)]
    for peer in peers:
        pl.semaphore_signal(barrier, inc=1, device_id=peer, device_id_type=MESH)
    pl.semaphore_wait(barrier, 7)
    copies = []
    for k, peer in enumerate(peers):
        copies.append(
            pltpu.make_async_remote_copy(
                mine, out.at[row], send_sem.at[k], recv_sem.at[k], device_id=peer, device_id_type=MESH
            )
        )
        copies[-1].start()
    out[row] = mine[...]
    r = lax.broadcasted_iota(jnp.int32, (128, 128), 0)
    c = lax.broadcasted_iota(jnp.int32, (128, 128), 1)
    back = (r + c == 127).astype(jnp.bfloat16)
    half = PX // 2
    cond_out[:, :, :HALF] = cond[:, :, :HALF]
    for p in range(2):
        val_out[2 * p] = val[p * half : p * half + half, :, :HALF]
    for b in range(HALF // 128):
        source = slice(CELLS - b * 128 - 128, CELLS - b * 128)
        to = slice(b * 128, b * 128 + 128)
        flip = lambda ref: jnp.dot(
            ref[:, :, source].reshape(PX * CL, 128), back, preferred_element_type=jnp.float32
        ).astype(jnp.bfloat16).reshape(PX, CL, 128)
        cond_out[:, :, HALF + b * 128 : HALF + b * 128 + 128] = flip(cond)
        turned = flip(val)
        for p in range(2):
            val_out[2 * p + 1, :, :, to] = turned[p * half : p * half + half]
    for copy in copies:
        copy.wait_recv()
    for copy in copies:
        copy.wait_send()


def places(mine, cond, val):
    return pl.pallas_call(
        places_kernel,
        in_specs=[pl.BlockSpec(memory_space=pltpu.VMEM)] * 3,
        out_specs=[pl.BlockSpec(memory_space=pltpu.VMEM)] * 3,
        out_shape=[
            jax.ShapeDtypeStruct((8, G_ROW // 128, 128), jnp.int32),
            jax.ShapeDtypeStruct((PX, CL, CELLS), jnp.bfloat16),
            jax.ShapeDtypeStruct((4, PX // 2, NV, HALF), jnp.bfloat16),
        ],
        scratch_shapes=[pltpu.SemaphoreType.DMA((7,)), pltpu.SemaphoreType.DMA((7,))],
        compiler_params=pltpu.CompilerParams(collective_id=1, has_side_effects=True),
        name="places",
    )(mine, cond, val)


def body(psi_val, psi_cond, energy_val, energy_cond, stick_map, gvec_map, slab_index):
    row = lax.axis_index("row")
    mine = lax.dynamic_slice(stick_map, (row * STK,), (STK,))
    cols = lax.dynamic_slice(slab_index, (row * JS,), (JS,))
    maps, cond, val = places(
        gvec_map.reshape(G_ROW // 128, 128), psi_cond.transpose(1, 0, 2), psi_val.transpose(1, 0, 2)
    )
    maps = maps.reshape(-1)
    place = jnp.take(maps, cols)
    col_kx = place // STK
    col_stick = jnp.take(stick_map, cols // G_ROW * STK + place % STK)
    pad = jnp.zeros((LANES - STK,), jnp.int32)
    flat = jnp.concatenate([mine, pad, col_stick])
    ky, kz = flat // NZ, flat % NZ
    full_kx = jnp.concatenate([jnp.zeros((LANES,), jnp.int32), col_kx])
    ks = jnp.stack([ky, kz, full_kx]).astype(jnp.float32)
    weight = (2.0 / (NY * NZ * NX)) / (energy_cond[None, :] - energy_val[:, None])
    m, slab = front(weight.reshape(PAIRS), cond, val, ks)
    return back(pick(gvec_map, m.reshape(2, NX, PAIRS, LANES)), slab)


def solution(mesh):
    in_specs = (P(None, "row", None), P("col", "row", None), P(), P("col"), P(), P("row"), P())
    out_specs = P(("row", "col"), None)
    return jax.shard_map(body, mesh=mesh, in_specs=in_specs, out_specs=out_specs, check_vma=False)
```

```python
import math

import jax
import jax.numpy as jnp
from jax import lax
from jax.experimental import pallas as pl
from jax.experimental.pallas import tpu as pltpu
from jax.sharding import PartitionSpec as P

NX = 48
NY = 48
NZ = 48
CELLS = NY * NZ
HALF = CELLS // 2
NC = 256
NV = 16
CL = 16
PAIRS = NV * CL
STK = 192
G_ROW = 5120
NS = 1024
JS = 128
XB = 4
LANES = 256
VMEM_LIMIT = 60 * 1024 * 1024
MESH = pl.DeviceIdType.MESH


def turn_angle(t):
    return (t - 96.0 * jnp.floor((t + 0.5) * (1.0 / 96.0))) * (math.pi / 48.0)


def make_tables(ks, rows_of_blocks, tc, ts, rot, ph, table):
    width = LANES + JS
    ky, kz = ks[0:1, :], ks[1:2, :]
    odd = lambda n: 2.0 * lax.broadcasted_iota(jnp.int32, (n, width), 0).astype(jnp.float32) + 1.0
    ay, az = turn_angle(odd(NY // 2) * ky), turn_angle(odd(NZ) * kz)
    cy, sy, cz, sz = jnp.cos(ay), jnp.sin(ay), jnp.cos(az), jnp.sin(az)
    for y in range(NY // 2):
        to = slice(y * NZ, y * NZ + NZ)
        tc[to, :] = (cy[y : y + 1, :] * cz - sy[y : y + 1, :] * sz).astype(jnp.bfloat16)
        ts[to, :] = -(sy[y : y + 1, :] * cz + cy[y : y + 1, :] * sz).astype(jnp.bfloat16)
    shift = turn_angle(ky + kz)
    rot[0:1, :] = jnp.cos(shift[:, :LANES])
    rot[1:2, :] = jnp.sin(shift[:, :LANES])

    def true_plane(plane):
        xs = plane
        for b, block_row in enumerate(rows_of_blocks):
            inside = (plane >= b * PX) & (plane < b * PX + PX)
            xs = jnp.where(inside, plane + (block_row - b) * PX, xs)
        return xs.astype(jnp.float32)

    xs = true_plane(lax.broadcasted_iota(jnp.int32, (NX, JS), 0))
    theta = turn_angle((ky + kz)[:, LANES:] - 2.0 * xs * ks[2:3, LANES:])
    ph[0] = jnp.cos(theta)
    ph[1] = jnp.sin(theta)
    r = lax.broadcasted_iota(jnp.int32, (2 * NX, 2 * NX), 0)
    c = lax.broadcasted_iota(jnp.int32, (2 * NX, 2 * NX), 1)
    low, left = r < NX, c < NX
    freq = jnp.where(low, r, r - NX).astype(jnp.float32)
    angle = turn_angle(2.0 * freq * true_plane(jnp.where(left, c, c - NX)))
    sine = jnp.sin(angle)
    table[...] = jnp.where(low == left, jnp.cos(angle), jnp.where(low, sine, -sine)).astype(jnp.bfloat16)


BLOCKS = 8
PX = NX // BLOCKS
PT = 3
YS = PAIRS + 8
PB = 16
MS = PB + 8


def density(vf, cbuf, b, plane, at, even, odd):
    cond = cbuf.at[b, plane]
    for v in range(NV):
        out = slice(at * PAIRS + v * CL, at * PAIRS + v * CL + CL)
        spread = lambda h: jnp.broadcast_to(vf[h, plane, v : v + 1, :], (CL, HALF)).astype(jnp.bfloat16)
        lo = spread(0) * cond[:, :HALF]
        hi = spread(1) * cond[:, HALF:]
        even[out, :] = lo + hi
        odd[out, :] = lo - hi


def transform(b, first, even, odd, tc, ts, rot, ph, y, sacc):
    a = jnp.dot(even[...], tc[...], preferred_element_type=jnp.float32)
    c = jnp.dot(odd[...], ts[...], preferred_element_type=jnp.float32)
    cosr, sinr = rot[0:1, :], rot[1:2, :]
    real, imag = sacc[0], sacc[1]
    for i in range(PT):
        x = b * PX + first + i
        rows = slice(i * PAIRS, i * PAIRS + PAIRS)
        am, cm = a[rows, :LANES], c[rows, :LANES]
        to = pl.ds(pl.multiple_of(x * YS, 8), PAIRS)
        for k, value in enumerate((cosr * am - sinr * cm, cosr * cm + sinr * am)):
            for h in range(LANES // 128):
                y[k, h, to, :] = value[:, h * 128 : h * 128 + 128]
        av, cv = a[rows, LANES:], c[rows, LANES:]
        cp, sp = ph[0, pl.ds(x, 1), :], ph[1, pl.ds(x, 1), :]
        real = real + (cp * av - sp * cv)
        imag = imag + (cp * cv + sp * av)
    sacc[0] = real
    sacc[1] = imag


def front_kernel(
    weights, cond, val, ks, m_out, slab_out,
    tc, ts, rot, ph, table, cbuf, vbuf, vf, even, odd, y, sacc, sl, mo, mb,
    lsem, cs, cr, vs, vr, gs, gr, ss, sr, fs, fr, ms,
):
    row, col = lax.axis_index("row"), lax.axis_index("col")
    yh, x = row // 4, row % 4
    z, yl, core = col // 4, (col // 2) % 2, col % 2
    zo = z + 1 - 2 * (z % 2)
    xp = {"row": yh * 4 + (x + 1) % 4, "col": col}
    xm = {"row": yh * 4 + (x + 3) % 4, "col": col}
    yc = {"row": (1 - yh) * 4 + x, "col": col}
    yv = {"row": (1 - yh) * 4 + x, "col": z * 4 + (1 - yl) * 2 + core}
    group = [
        {"row": row, "col": zo * 4 + yl * 2 + core},
        {"row": row, "col": z * 4 + yl * 2 + 1 - core},
        {"row": row, "col": zo * 4 + yl * 2 + 1 - core},
    ]
    across = [{"row": (row + k) % 8, "col": col} for k in range(1, 8)]
    part = core * 2 + z % 2

    own = [
        pltpu.make_async_copy(cond, cbuf.at[0], lsem.at[0]),
        pltpu.make_async_copy(val, vbuf.at[0], lsem.at[1]),
    ]
    for copy in own:
        copy.start()
    barrier = pltpu.get_barrier_semaphore()
    for peer in across + group + [yv]:
        pl.semaphore_signal(barrier, inc=1, device_id=peer, device_id_type=MESH)
    pl.semaphore_wait(barrier, 11)

    hops = [(0, 3, None), (0, 2, xp), (0, 1, xm), (3, 6, xp), (3, 5, xm), (2, 4, xp), (5, 7, xm)]
    hop_to = [hop[1] for hop in hops]

    def cond_hop(n):
        src, dst, peer = hops[n]
        return pltpu.make_async_remote_copy(
            cbuf.at[src] if src else cond, cbuf.at[dst], cs.at[n], cr.at[dst],
            device_id=peer or yc, device_id_type=MESH,
        )

    def val_hop(n):
        src, dst, peer = hops[n]
        return pltpu.make_async_remote_copy(
            vbuf.at[src, part] if src else val.at[part], vbuf.at[dst, part], vs.at[n], vr.at[dst],
            device_id=peer or yv, device_id_type=MESH,
        )

    def spread(b, j):
        return pltpu.make_async_remote_copy(
            vbuf.at[b, part], vbuf.at[b, part], gs.at[b * 3 + j], gr.at[b * 3 + j],
            device_id=group[j], device_id_type=MESH,
        )

    def land_val(b, *forward):
        val_hop(hop_to.index(b)).wait_recv()
        for n in forward:
            val_hop(n).start()
        for j in range(3):
            spread(b, j).start()

    def land(b, *forward):
        cond_hop(hop_to.index(b)).wait_recv()
        for n in forward:
            cond_hop(n).start()

    def ready(b):
        for j in range(3):
            spread(b, j).wait_recv()

    for n in range(3):
        val_hop(n).start()
    for n in range(3):
        cond_hop(n).start()
    sacc[...] = jnp.zeros_like(sacc)
    steps = [(0, 0), (0, 1), (0, 3), (1, 0), (0, 2), (1, 1), (1, 3), (1, 2)]
    make_tables(ks, [(yh + dy) % 2 * 4 + (x + dx) % 4 for dy, dx in steps], tc, ts, rot, ph, table)
    for copy in own:
        copy.wait()

    def block(b, carry):
        @pl.when(b == 1)
        def _():
            land_val(1)
            land_val(2, 5)
            land_val(3, 3, 4)
            land(2, 5)
            land(1)
            land(3, 3, 4)
            ready(1)

        @pl.when(b == 2)
        def _():
            land_val(4)
            land_val(5, 6)
            land_val(6)
            ready(2)

        @pl.when(b == 3)
        def _():
            land_val(7)
            ready(3)

        @pl.when(b == 4)
        def _():
            land(4)
            land(5, 6)
            ready(4)

        @pl.when(b == 5)
        def _():
            land(6)
            ready(5)

        @pl.when(b == 6)
        def _():
            ready(6)

        @pl.when(b == 7)
        def _():
            land(7)
            ready(7)

        def widen(j, carry):
            for q in range(4):
                vf[q % 2, (q // 2) * 3 + j] = vbuf[b, q, j].astype(jnp.float32)
            return carry

        lax.fori_loop(0, 3, widen, 0)

        def some(i, carry):
            for u in range(PT):
                density(vf, cbuf, b, i * PT + u, u, even, odd)
            transform(b, i * PT, even, odd, tc, ts, rot, ph, y, sacc)
            return carry

        lax.fori_loop(0, PX // PT, some, 0)
        return carry

    lax.fori_loop(0, BLOCKS, block, 0)

    for h in range(2):
        sl[h * PAIRS : h * PAIRS + PAIRS, :] = sacc[h].astype(jnp.bfloat16)
    keep = pltpu.make_async_copy(sl, slab_out.at[0, row], lsem.at[2])
    keep.start()

    def push(k):
        return pltpu.make_async_remote_copy(
            sl, slab_out.at[0, row], ss.at[k], sr.at[k], device_id=across[k], device_id_type=MESH
        )

    def hand(k):
        at = (row + 7 - k) % 8
        return pltpu.make_async_remote_copy(
            sl if k == 7 else slab_out.at[0, at], slab_out.at[1, at], fs.at[k], fr.at[k],
            device_id=group[1], device_id_type=MESH,
        )

    for k in range(7):
        push(k).start()
    hand(7).start()

    def chunk(i, carry):
        for k in range(7):

            @pl.when(i == 5 + k)
            def _():
                push(k).wait_recv()
                hand(k).start()

        slot = i % 2
        ps = pl.ds(pl.multiple_of(i * PB, PB), PB)
        out = pltpu.make_async_copy(mb.at[slot], m_out.at[:, ps, :], ms.at[slot])
        for p in range(PB):
            at = pl.ds(i * PB + p, NX, stride=YS)
            rhs = jnp.concatenate(
                [jnp.concatenate([y[k, 0, at, :], y[k, 1, at, :]], axis=1) for k in range(2)], axis=0
            ).astype(jnp.bfloat16)
            res = jnp.dot(table[...], rhs, preferred_element_type=jnp.float32) * weights[i * PB + p]
            for h in range(LANES // 128):
                mo[h, pl.ds(p, 2 * NX, stride=MS), :] = res[:, h * 128 : h * 128 + 128]

        @pl.when(i >= 2)
        def _():
            out.wait()

        for h in range(LANES // 128):
            lanes = slice(h * 128, h * 128 + 128)
            mb[slot, :, :, lanes] = mo[h, : 2 * NX * MS, :].reshape(2 * NX, MS, 128)[:, :PB].astype(jnp.bfloat16)
        out.start()
        return carry

    lax.fori_loop(0, PAIRS // PB, chunk, 0)
    for slot in range(2):
        pltpu.make_async_copy(mb.at[slot], m_out.at[:, pl.ds(slot * PB, PB), :], ms.at[slot]).wait()
    keep.wait()
    for k in range(8):
        hand(k).wait_recv()
        hand(k).wait_send()
    for k in range(7):
        push(k).wait_send()
    for n in range(len(hops)):
        val_hop(n).wait_send()
        cond_hop(n).wait_send()
    for b in range(1, BLOCKS):
        for j in range(3):
            spread(b, j).wait_send()


def front(weights, cond, val, ks):
    dma = pltpu.SemaphoreType.DMA
    vmem = pl.BlockSpec(memory_space=pltpu.VMEM)
    hbm = pl.BlockSpec(memory_space=pl.ANY)
    bf = lambda *shape: pltpu.VMEM(shape, jnp.bfloat16)
    fl = lambda *shape: pltpu.VMEM(shape, jnp.float32)
    return pl.pallas_call(
        front_kernel,
        in_specs=[pl.BlockSpec(memory_space=pltpu.SMEM)] + [vmem] * 3,
        out_specs=[hbm, hbm],
        out_shape=[
            jax.ShapeDtypeStruct((2 * NX, PAIRS, LANES), jnp.bfloat16),
            jax.ShapeDtypeStruct((2, BLOCKS, 2 * PAIRS, JS), jnp.bfloat16),
        ],
        scratch_shapes=[
            bf(HALF, LANES + JS),
            bf(HALF, LANES + JS),
            fl(2, LANES),
            fl(2, NX, JS),
            bf(2 * NX, 2 * NX),
            bf(BLOCKS, PX, CL, CELLS),
            bf(BLOCKS, 4, PX // 2, NV, HALF),
            fl(2, PX, NV, HALF),
            bf(PT * PAIRS, HALF),
            bf(PT * PAIRS, HALF),
            fl(2, LANES // 128, NX * YS + YS, 128),
            fl(2, PAIRS, JS),
            bf(2 * PAIRS, JS),
            fl(2, 2 * NX * MS + MS, 128),
            bf(2, 2 * NX, PB, LANES),
            dma((3,)), dma((7,)), dma((8,)), dma((7,)), dma((8,)),
            dma((24,)), dma((24,)), dma((7,)), dma((7,)), dma((8,)), dma((8,)), dma((2,)),
        ],
        compiler_params=pltpu.CompilerParams(
            collective_id=2, has_side_effects=True, vmem_limit_bytes=VMEM_LIMIT
        ),
        name="front",
    )(weights, cond, val, ks)


GB = 320
QS = 2 * PAIRS // 128
G_DEV = 320
LO = 192
HI = G_DEV - LO
DEPTH = 24
UNROLL = 64


def pick_kernel(g_ref, m, out, mt, mi, sel, lhs, ms, os):
    def fetch(step):
        slot = step % DEPTH
        return pltpu.make_async_copy(m.at[:, step], mi.at[slot], ms.at[slot])

    for step in range(DEPTH):
        fetch(step).start()

    def turn(step, carry):
        fetch(step).wait()
        for h in range(2):
            for q in range(2):
                t = mi[step % DEPTH, h, q * 128 : q * 128 + 128, :].T.astype(jnp.float32)
                mt[pl.ds(step * (STK * QS) + h * 2 + q, STK, stride=QS), :] = t[:STK, :]

        @pl.when(step < NX - DEPTH)
        def _():
            fetch(step + DEPTH).start()

        return carry

    lax.fori_loop(0, NX, turn, 0, unroll=8)
    store = lambda n: pltpu.make_async_copy(lhs.at[n % 2], out.at[n], os.at[n % 2])

    def block(n, carry):
        def rows(i, carry):
            for u in range(UNROLL):
                g = g_ref[n * GB + i * UNROLL + u]
                to = pl.ds(pl.multiple_of((i * UNROLL + u) * QS, QS), QS)
                sel[to, :] = mt[pl.ds(pl.multiple_of(g * QS, QS), QS), :]
            return carry

        lax.fori_loop(0, GB // UNROLL, rows, 0)

        @pl.when(n >= 2)
        def _():
            store(n - 2).wait()

        for k in range(QS):
            lhs[n % 2, :, k * 128 : k * 128 + 128] = sel[pl.ds(k, GB, stride=QS), :].astype(jnp.bfloat16)
        store(n).start()
        return carry

    lax.fori_loop(0, G_ROW // GB, block, 0)
    for n in range(2):
        store(G_ROW // GB - 2 + n).wait()


def pick(gvec, m):
    dma = pltpu.SemaphoreType.DMA
    return pl.pallas_call(
        pick_kernel,
        in_specs=[pl.BlockSpec(memory_space=pltpu.SMEM), pl.BlockSpec(memory_space=pl.ANY)],
        out_specs=pl.BlockSpec(memory_space=pl.ANY),
        out_shape=jax.ShapeDtypeStruct((G_ROW // GB, GB, 2 * PAIRS), jnp.bfloat16),
        scratch_shapes=[
            pltpu.VMEM((NX * STK * QS + 8, 128), jnp.float32),
            pltpu.VMEM((DEPTH, 2, PAIRS, LANES), jnp.bfloat16),
            pltpu.VMEM((GB * QS + 8, 128), jnp.float32),
            pltpu.VMEM((2, GB, 2 * PAIRS), jnp.bfloat16),
            dma((DEPTH,)), dma((2,)),
        ],
        compiler_params=pltpu.CompilerParams(vmem_limit_bytes=VMEM_LIMIT),
        name="pick",
    )(gvec, m)


def add_rows(dst, a, b, rows, step=32):
    def one(i, carry):
        at = pl.ds(pl.multiple_of(i * step, step), step)
        dst[at, :] = (a[at, :].astype(jnp.float32) + b[at, :].astype(jnp.float32)).astype(dst.dtype)
        return carry

    lax.fori_loop(0, rows // step, one, 0)


def back_kernel(
    rows, slab, out, sw, ours, theirs, acc, zr2, yr1, zr1, yr2,
    ms, s1, d1, sz2, dz2, sy1, dy1, sz1, dz1, sy2, dy2,
):
    row, col = lax.axis_index("row"), lax.axis_index("col")
    z, yl, core = col // 4, (col // 2) % 2, col % 2
    core_peer = {"row": row, "col": z * 4 + yl * 2 + (1 - core)}
    y_peer = {"row": row, "col": z * 4 + (1 - yl) * 2 + core}
    z_peer = lambda k: {"row": row, "col": ((z + k) % 4) * 4 + yl * 2 + core}
    barrier = pltpu.get_barrier_semaphore()
    for peer in (core_peer, y_peer, z_peer(1), z_peer(2), z_peer(3)):
        pl.semaphore_signal(barrier, inc=1, device_id=peer, device_id_type=MESH)

    def place(n):
        k, s = (n // 2 + 1) % 4, n % 2
        return ((z + k) % 4) * 4 + (yl * s + (1 - yl) * (1 - s)) * 2

    load = lambda n: pltpu.make_async_copy(rows.at[place(n) + core], ours.at[n], ms.at[n])
    for n in range(8):
        load(n).start()
    pl.semaphore_wait(barrier, 5)

    scale = -1.0 / math.sqrt(NV * NC)
    def remote(src, dst, ss, ds, peer):
        return pltpu.make_async_remote_copy(src, dst, ss, ds, device_id=peer, device_id_type=MESH)

    lo, hi = pl.ds(0, LO), pl.ds(LO, HI)
    first = lambda n: remote(rows.at[place(n) + 1 - core], theirs.at[n], s1.at[n], d1.at[n], core_peer)
    for n in range(2):
        first(n).start()
    for h in range(2):
        for r in range(NS // JS):
            sw[h * 2 * PAIRS : (h + 1) * 2 * PAIRS, r * JS : r * JS + JS] = slab[h, r]
    along_z = lambda k, s: remote(
        acc.at[(k + 3) % 4 * 2 + s, hi], zr2.at[(k - 1) * 2 + s], sz2.at[(k - 1) * 2 + s], dz2.at[(k - 1) * 2 + s], z_peer(k)
    )
    along_y = lambda k: remote(acc.at[(k + 3) % 4 * 2, lo], yr1.at[k], sy1.at[k], dy1.at[k], y_peer)
    last_z = lambda k: remote(acc.at[(k + 3) % 4 * 2 + 1, lo], zr1.at[k - 1], sz1.at[k - 1], dz1.at[k - 1], z_peer(k))

    def slot(n, carry):
        k, s = (n // 2 + 1) % 4, n % 2
        load(n).wait()
        first(n).wait_recv()

        @pl.when(n < 6)
        def _():
            first(n + 2).start()

        lhs = jnp.concatenate([ours[n], theirs[n]], axis=1)
        acc[n] = (jnp.dot(lhs, sw[...], preferred_element_type=jnp.float32) * scale).astype(jnp.bfloat16)

        @pl.when(n < 6)
        def _():
            along_z(k, s).start()

        @pl.when(s == 0)
        def _():
            along_y(k).start()

        return carry

    lax.fori_loop(0, 8, slot, 0)
    for k in (1, 2, 3, 0):
        along_y(k).wait_recv()
        if k:
            at = acc.at[(k + 3) % 4 * 2 + 1]
            add_rows(at, at, yr1.at[k], LO)
            last_z(k).start()
    for k in (1, 2, 3):
        along_z(k, 0).wait_recv()

    def total(i, base, terms):
        at = pl.ds(pl.multiple_of(i * 16, 16), 16)
        value = base[at, :].astype(jnp.float32)
        for ref in terms:
            value = value + ref[at, :].astype(jnp.float32)
        return at, value

    def across(i, carry):
        at, value = total(i, acc.at[6, hi], [zr2.at[0], zr2.at[2], zr2.at[4]])
        yr2[0, at, :] = value.astype(jnp.bfloat16)
        return carry

    lax.fori_loop(0, HI // 16, across, 0)
    last_y = remote(yr2.at[0], yr2.at[1], sy2.at[0], dy2.at[0], y_peer)
    last_y.start()
    for k in (1, 2, 3):
        last_z(k).wait_recv()

    def low(i, carry):
        at, value = total(i, acc.at[7, lo], [yr1.at[0], zr1.at[0], zr1.at[1], zr1.at[2]])
        out[at, :] = value
        return carry

    lax.fori_loop(0, LO // 16, low, 0)
    for k in (1, 2, 3):
        along_z(k, 1).wait_recv()
    last_y.wait_recv()

    def high(i, carry):
        at, value = total(i, acc.at[7, hi], [zr2.at[1], zr2.at[3], zr2.at[5], yr2.at[1]])
        out[pl.ds(pl.multiple_of(LO + i * 16, 16), 16), :] = value
        return carry

    lax.fori_loop(0, HI // 16, high, 0)
    for n in range(8):
        first(n).wait_send()
    for k in range(4):
        along_y(k).wait_send()
        if k:
            last_z(k).wait_send()
            along_z(k, 0).wait_send()
            along_z(k, 1).wait_send()
    last_y.wait_send()


def back(rows, slab):
    dma = pltpu.SemaphoreType.DMA
    vmem = pl.BlockSpec(memory_space=pltpu.VMEM)
    part = lambda n, rows: pltpu.VMEM((n, rows, NS), jnp.bfloat16)
    return pl.pallas_call(
        back_kernel,
        in_specs=[pl.BlockSpec(memory_space=pl.ANY), vmem],
        out_specs=vmem,
        out_shape=jax.ShapeDtypeStruct((G_DEV, NS), jnp.float32),
        scratch_shapes=[
            pltpu.VMEM((4 * PAIRS, NS), jnp.bfloat16),
            pltpu.VMEM((8, GB, 2 * PAIRS), jnp.bfloat16),
            pltpu.VMEM((8, GB, 2 * PAIRS), jnp.bfloat16),
            pltpu.VMEM((8, G_DEV, NS), jnp.bfloat16),
            part(6, HI), part(4, LO), part(3, LO), part(2, HI),
            dma((8,)), dma((8,)), dma((8,)), dma((6,)), dma((6,)), dma((4,)), dma((4,)),
            dma((3,)), dma((3,)), dma((1,)), dma((1,)),
        ],
        compiler_params=pltpu.CompilerParams(
            collective_id=3, has_side_effects=True, vmem_limit_bytes=VMEM_LIMIT
        ),
        name="back",
    )(rows, slab)


def places_kernel(mine, cond, val, out, cond_out, val_out, send_sem, recv_sem):
    row, col = lax.axis_index("row"), lax.axis_index("col")
    barrier = pltpu.get_barrier_semaphore()
    peers = [{"row": (row + k) % 8, "col": col} for k in range(1, 8)]
    for peer in peers:
        pl.semaphore_signal(barrier, inc=1, device_id=peer, device_id_type=MESH)
    pl.semaphore_wait(barrier, 7)
    copies = []
    for k, peer in enumerate(peers):
        copies.append(
            pltpu.make_async_remote_copy(
                mine, out.at[row], send_sem.at[k], recv_sem.at[k], device_id=peer, device_id_type=MESH
            )
        )
        copies[-1].start()
    out[row] = mine[...]
    r = lax.broadcasted_iota(jnp.int32, (128, 128), 0)
    c = lax.broadcasted_iota(jnp.int32, (128, 128), 1)
    back = (r + c == 127).astype(jnp.bfloat16)
    half = PX // 2
    cond_out[:, :, :HALF] = cond[:, :, :HALF]
    for p in range(2):
        val_out[2 * p] = val[p * half : p * half + half, :, :HALF]
    for b in range(HALF // 128):
        source = slice(CELLS - b * 128 - 128, CELLS - b * 128)
        to = slice(b * 128, b * 128 + 128)
        flip = lambda ref: jnp.dot(
            ref[:, :, source].reshape(PX * CL, 128), back, preferred_element_type=jnp.float32
        ).astype(jnp.bfloat16).reshape(PX, CL, 128)
        cond_out[:, :, HALF + b * 128 : HALF + b * 128 + 128] = flip(cond)
        turned = flip(val)
        for p in range(2):
            val_out[2 * p + 1, :, :, to] = turned[p * half : p * half + half]
    for copy in copies:
        copy.wait_recv()
    for copy in copies:
        copy.wait_send()


def places(mine, cond, val):
    return pl.pallas_call(
        places_kernel,
        in_specs=[pl.BlockSpec(memory_space=pltpu.VMEM)] * 3,
        out_specs=[pl.BlockSpec(memory_space=pltpu.VMEM)] * 3,
        out_shape=[
            jax.ShapeDtypeStruct((8, G_ROW // 128, 128), jnp.int32),
            jax.ShapeDtypeStruct((PX, CL, CELLS), jnp.bfloat16),
            jax.ShapeDtypeStruct((4, PX // 2, NV, HALF), jnp.bfloat16),
        ],
        scratch_shapes=[pltpu.SemaphoreType.DMA((7,)), pltpu.SemaphoreType.DMA((7,))],
        compiler_params=pltpu.CompilerParams(collective_id=1, has_side_effects=True),
        name="places",
    )(mine, cond, val)


def body(psi_val, psi_cond, energy_val, energy_cond, stick_map, gvec_map, slab_index):
    row = lax.axis_index("row")
    mine = lax.dynamic_slice(stick_map, (row * STK,), (STK,))
    cols = lax.dynamic_slice(slab_index, (row * JS,), (JS,))
    maps, cond, val = places(
        gvec_map.reshape(G_ROW // 128, 128), psi_cond.transpose(1, 0, 2), psi_val.transpose(1, 0, 2)
    )
    maps = maps.reshape(-1)
    place = jnp.take(maps, cols)
    col_kx = place // STK
    col_stick = jnp.take(stick_map, cols // G_ROW * STK + place % STK)
    pad = jnp.zeros((LANES - STK,), jnp.int32)
    flat = jnp.concatenate([mine, pad, col_stick])
    ky, kz = flat // NZ, flat % NZ
    full_kx = jnp.concatenate([jnp.zeros((LANES,), jnp.int32), col_kx])
    ks = jnp.stack([ky, kz, full_kx]).astype(jnp.float32)
    weight = (2.0 / (NY * NZ * NX)) / (energy_cond[None, :] - energy_val[:, None])
    m, slab = front(weight.reshape(PAIRS), cond, val, ks)
    return back(pick(gvec_map, m.reshape(2, NX, PAIRS, LANES)), slab)


def solution(mesh):
    in_specs = (P(None, "row", None), P("col", "row", None), P(), P("col"), P(), P("row"), P())
    out_specs = P(("row", "col"), None)
    return jax.shard_map(body, mesh=mesh, in_specs=in_specs, out_specs=out_specs, check_vma=False)
```
